32 devices in a mesh: dp: 4 (over y, x), fsdp: 8 (over z, core).
Axes of the slice: x: 2, y: 2, z: 4, core: 2. Of those that a mesh axis runs over, the one named last changes fastest.
Arguments:
- samples: bfloat16 [32, 64, 64, 128], P(('dp', 'fsdp')), may hold values from -6 to 6
- cotangent: bfloat16 [32, 32, 32, 256], P(('dp', 'fsdp')), may hold values from -6 to 6
- class_ids: int32 [32], P(('dp', 'fsdp')), may hold values from 0 to 15
- conv_state: float32 [4, 4, 147456], P(None, None, ('dp', 'fsdp')), as said below
- mlp_state: float32 [4, 401408], P(None, ('dp', 'fsdp')), as said below
- small_state: float32 [4, 1792], P(None, ('dp', 'fsdp')), as said below
Outputs:
- block_out: bfloat16 [32, 32, 32, 256], P(('dp', 'fsdp'))
- input_grad: bfloat16 [32, 64, 64, 128], P(('dp', 'fsdp'))
- conv_new: float32 [4, 4, 147456], P(None, None, ('dp', 'fsdp'))
- mlp_new: float32 [4, 401408], P(None, ('dp', 'fsdp'))
- small_new: float32 [4, 1792], P(None, ('dp', 'fsdp'))
- conv_copy: bfloat16 [4, 147456], P(None, ('dp', 'fsdp'))
- mlp_copy: bfloat16 [401408], P(('dp', 'fsdp'))
- small_copy: bfloat16 [1792], P(('dp', 'fsdp'))
The draws below stay inside these ranges and needn't reach their ends.
Inputs may be any that keep to these rules, and one draw needn't show every extreme that they name: `conv_state`: slot 2 (second moments) of each state is positive. `mlp_state`: slot 2 (second moments) of each state is positive. `small_state`: slot 2 (second moments) of each state is positive.
All inputs are finite; a program needn't handle non-finite values.
Results may differ from the reference program's by a relative error of at most 0.0066.
Values may be sent and summed in bfloat16 or wider, within the bound.
No kernel may reach another device: no remote copies, remote signals or barrier semaphores. Data moves between devices by JAX's collectives and lax.ppermute only.
A program may use at most 192 MiB of HBM per device.

```python
import math
import jax
import jax.numpy as jnp
import numpy as np
from jax import lax

C = 128
EMB = 512
GROUPS = 8
H = 64
W = 64
NCLASS = 16
STEP = 10
SAMPLES = 32
KERNEL = 147456
MLP_LEN = 401408
SMALL_LEN = 1792


def build_stack(noise_draw, factor_draw, spread, grad_scale):
    weight = noise_draw[0] * spread
    first_moment = noise_draw[1] * (0.1 / 0.9) * grad_scale
    second = 2.0 * (0.001 / 0.999) * grad_scale * grad_scale * jnp.exp(factor_draw * math.log(2.0))
    average = weight + 0.2 * spread * noise_draw[3]
    return jnp.stack([weight, first_moment, second, average]).astype(jnp.float32)


def draw_conv_state(key, part):
    key = jax.random.fold_in(key, 3)
    key_list = jax.random.split(key, 2)
    stack_shape = (4, 4, KERNEL)
    noise_draw = jax.random.truncated_normal(key_list[0], -4.0, 4.0, stack_shape, jnp.float32)
    factor_draw = jax.random.uniform(key_list[1], stack_shape[1:], jnp.float32, -1.0, 1.0)
    grad_scale = 0.5 * math.sqrt(SAMPLES * H * W)
    return build_stack(noise_draw, factor_draw, (9 * C) ** (-0.5), grad_scale)


def draw_mlp_state(key, part):
    key = jax.random.fold_in(key, 5)
    key_list = jax.random.split(key, 2)
    stack_shape = (4, MLP_LEN)
    noise_draw = jax.random.truncated_normal(key_list[0], -4.0, 4.0, stack_shape, jnp.float32)
    factor_draw = jax.random.uniform(key_list[1], (MLP_LEN,), jnp.float32, -1.0, 1.0)
    flat_index = jnp.arange(MLP_LEN, dtype=jnp.int32)
    spread = jnp.where(flat_index < NCLASS * EMB, 1.0, EMB ** (-0.5)).astype(jnp.float32)
    grad_scale = 0.3 * math.sqrt(SAMPLES * H * W)
    return build_stack(noise_draw, factor_draw, spread, grad_scale)


def draw_small_state(key, part):
    key = jax.random.fold_in(key, 7)
    key_list = jax.random.split(key, 2)
    stack_shape = (4, SMALL_LEN)
    noise_draw = jax.random.truncated_normal(key_list[0], -4.0, 4.0, stack_shape, jnp.float32)
    factor_draw = jax.random.uniform(key_list[1], (SMALL_LEN,), jnp.float32, -1.0, 1.0)
    grad_scale = 0.5 * math.sqrt(SAMPLES * H * W)
    return build_stack(noise_draw, factor_draw, 0.2, grad_scale)


def place_ends(values, own_key, smallest, largest):
    dims = values.shape
    place = [jax.random.randint(jax.random.fold_in(own_key, axis), (), 0, dims[axis]) for axis in range(len(dims))]
    values = values.at[tuple(place)].set(smallest)
    longest = dims.index(max(dims))
    place[longest] = (place[longest] + 1) % dims[longest]
    return values.at[tuple(place)].set(largest)


def block_levels(key, shape, cuts, low, top_value):
    factor_of, own = 1.0, jax.random.fold_in(key, 6)
    for position, parts in cuts:
        steps = jnp.exp(jax.random.uniform(jax.random.fold_in(own, position), (parts,), jnp.float32, low / len(cuts), top_value / len(cuts)))
        factor_of = factor_of * jnp.repeat(steps, shape[position] // parts).reshape([-1 if axis == position else 1 for axis in range(len(shape))])
    return factor_of


def cumulative_ranks(number_of, lean):
    weights = [(1 << 20) // math.isqrt(rank ** lean) + 1 for rank in range(1, number_of + 1)]
    scale = 1 + sum(weights) // (1 << 30)
    return np.cumsum(np.array([max(1, weight // scale) for weight in weights]))


def ranked(stream_key, shape, number_of, lean):
    grid = cumulative_ranks(number_of, lean)
    ticket = jax.random.randint(jax.random.fold_in(stream_key, 1), shape, 0, int(grid[number_of - 1]))
    standing = jnp.searchsorted(jnp.asarray(grid, jnp.int32), ticket, side="right")
    return jax.random.permutation(jax.random.fold_in(stream_key, 2), number_of)[standing].astype(jnp.int32)


def bell_draw(own_key, shape, scale, most, shards=(), kind=jnp.bfloat16):
    loudness = block_levels(own_key, shape, shards, -0.22, 0.18) if shards else 1.0
    drawn = jax.random.normal(own_key, shape, jnp.float32) * scale * loudness
    return jnp.minimum(jnp.maximum(drawn, -most), most).astype(kind)


def setup_inputs(seed: int = 0) -> dict:
    keys = jax.random.split(jax.random.key(seed), 7)
    return {
        "samples": bell_draw(keys[0], (SAMPLES, H, W, C), 1.0, 6.0, ((0, 32),)),
        "cotangent": bell_draw(keys[1], (SAMPLES, H // 2, W // 2, 2 * C), 1.0, 6.0, ((0, 32),)),
        "class_ids": place_ends(ranked(keys[2], (SAMPLES,), NCLASS, 2), jax.random.fold_in(keys[2], 3), 0, NCLASS - 1).astype(jnp.int32),
        "conv_state": draw_conv_state(jax.random.fold_in(keys[6], 71), 0),
        "mlp_state": draw_mlp_state(jax.random.fold_in(keys[6], 71), 0),
        "small_state": draw_small_state(jax.random.fold_in(keys[6], 71), 0),
    }


beta_one = 0.9
beta_two = 0.999
adam_eps = 1e-08
ema_decay = 0.99
norm_eps = 1e-05
rate_conv = 0.08
rate_table = 0.6
rate_dense = 0.1
rate_small = 0.15
decay_weights = 0.01

@jax.custom_vjp
def low(v):
    return lax.optimization_barrier(v.astype(jnp.bfloat16)).astype(jnp.float32)

@jax.custom_vjp
def low_back(v):
    return v

def low_keep(v):
    return (low(v), None)

def low_pass(kept, grad):
    return (grad,)

def back_keep(v):
    return (v, None)

def back_low(kept, grad):
    return (low(grad),)
low.defvjp(low_keep, low_pass)
low_back.defvjp(back_keep, back_low)

def group_norm(values, offset_gain, offset_bias):
    grouped = values.reshape(values.shape[:3] + (GROUPS, C // GROUPS))
    centre = lax.optimization_barrier(jnp.mean(grouped, axis=(1, 2, 4), keepdims=True))
    spread = lax.optimization_barrier(jnp.mean(jnp.square(grouped - centre), axis=(1, 2, 4), keepdims=True))
    scaled = ((grouped - centre) * lax.rsqrt(spread + norm_eps)).reshape(values.shape)
    return scaled * (1.0 + offset_gain) + offset_bias

def front_part(values, offset_gain, offset_bias):
    return jax.nn.gelu(group_norm(values, offset_gain, offset_bias), approximate=False)

def conv_ref(values, kernel, stride):
    return lax.conv_general_dilated(values, kernel, (stride, stride), ((1, 1), (1, 1)), dimension_numbers=('NHWC', 'HWIO', 'NHWC'), precision=lax.Precision.HIGHEST)

def split_kernels(conv_all):
    kernel_one = conv_all[0].reshape(3, 3, C, C)
    kernel_two = conv_all[1].reshape(3, 3, C, C)
    kernel_down = jnp.concatenate([conv_all[2].reshape(3, 3, C, C), conv_all[3].reshape(3, 3, C, C)], axis=3)
    return (kernel_one, kernel_two, kernel_down)

def split_dense(dense_all):
    table_len = NCLASS * EMB
    class_embed = dense_all[:table_len].reshape(NCLASS, EMB)
    dense_one = dense_all[table_len:table_len + EMB * EMB].reshape(EMB, EMB)
    dense_two = dense_all[table_len + EMB * EMB:].reshape(EMB, 2 * C)
    return (class_embed, dense_one, dense_two)

def split_small(small_all):
    widths = [C, C, C, C, C, C, 2 * C, EMB, 2 * C]
    pieces = []
    offset = 0
    for extent in widths:
        pieces.append(small_all[offset:offset + extent])
        offset = offset + extent
    return pieces

def class_table(class_embed, dense_one, bias_hidden, dense_two, bias_out):
    hidden = jax.nn.gelu(jnp.dot(class_embed, dense_one, preferred_element_type=jnp.float32, precision=lax.Precision.HIGHEST) + bias_hidden, approximate=False)
    return jnp.dot(hidden, dense_two, preferred_element_type=jnp.float32, precision=lax.Precision.HIGHEST) + bias_out

def block_forward(field_in, block_ids, conv_all, dense_all, small_all):
    kernel_one, kernel_two, kernel_down = split_kernels(conv_all)
    class_embed, dense_one, dense_two = split_dense(dense_all)
    gain_one, shift_one, conv_bias_one, gain_two, shift_two, conv_bias_two, bias_down, bias_hidden, bias_out = split_small(small_all)
    class_values = class_table(class_embed, dense_one, bias_hidden, dense_two, bias_out)
    chosen = class_values[block_ids]
    film_scale = chosen[:, None, None, :C]
    film_shift = chosen[:, None, None, C:]
    act_one = low(front_part(field_in, gain_one, shift_one))
    conv_one_out = low_back(conv_ref(act_one, kernel_one, 1)) + conv_bias_one
    modulated = conv_one_out * (1.0 + film_scale) + film_shift
    act_two = low(front_part(modulated, gain_two, shift_two))
    conv_two_out = low_back(conv_ref(act_two, kernel_two, 1)) + conv_bias_two
    residual = low(field_in + conv_two_out)
    return conv_ref(residual, kernel_down, 2) + bias_down

def adam_update(state_stack, gradient, step_rate, weight_decay):
    weight = state_stack[0]
    first_moment = beta_one * state_stack[1] + (1.0 - beta_one) * gradient
    second = beta_two * state_stack[2] + (1.0 - beta_two) * gradient * gradient
    first_hat = first_moment / (1.0 - beta_one ** STEP)
    second_hat = second / (1.0 - beta_two ** STEP)
    weight_new = weight - step_rate * (first_hat / (jnp.sqrt(second_hat) + adam_eps) + weight_decay * weight)
    average = ema_decay * state_stack[3] + (1.0 - ema_decay) * weight_new
    return (jnp.stack([weight_new, first_moment, second, average]), weight_new.astype(jnp.bfloat16))

def reference(samples, cotangent, class_ids, conv_state, mlp_state, small_state):
    conv_all = lax.optimization_barrier(conv_state[0].astype(jnp.bfloat16)).astype(jnp.float32)
    dense_all = lax.optimization_barrier(mlp_state[0].astype(jnp.bfloat16)).astype(jnp.float32)
    small_all = lax.optimization_barrier(small_state[0].astype(jnp.bfloat16)).astype(jnp.float32)
    block_size = math.gcd(SAMPLES, 16)
    block_count = SAMPLES // block_size
    source_blocks = samples.reshape(block_count, block_size, H, W, C)
    cot_blocks = cotangent.reshape(block_count, block_size, H // 2, W // 2, 2 * C)
    id_blocks = class_ids.reshape(block_count, block_size)

    def one_block(grad_carry, block_items):
        block_in, block_cot, block_ids = block_items

        def forward(field_in, conv_w, dense_w, small_w):
            return block_forward(field_in, block_ids, conv_w, dense_w, small_w)
        block_value, pull_back = jax.vjp(forward, block_in.astype(jnp.float32), conv_all, dense_all, small_all)
        grad_field, grad_conv, grad_dense, grad_small = pull_back(block_cot.astype(jnp.float32))
        grad_carry = (grad_carry[0] + grad_conv, grad_carry[1] + grad_dense, grad_carry[2] + grad_small)
        return (grad_carry, (block_value.astype(jnp.bfloat16), grad_field.astype(jnp.bfloat16)))
    start_carry = (jnp.zeros((4, KERNEL), jnp.float32), jnp.zeros((MLP_LEN,), jnp.float32), jnp.zeros((SMALL_LEN,), jnp.float32))
    grad_sums, out_blocks = lax.scan(one_block, start_carry, (source_blocks, cot_blocks, id_blocks))
    block_out = out_blocks[0].reshape(SAMPLES, H // 2, W // 2, 2 * C)
    input_grad = out_blocks[1].reshape(SAMPLES, H, W, C)
    flat_index = jnp.arange(MLP_LEN, dtype=jnp.int32)
    dense_rate = jnp.where(flat_index < NCLASS * EMB, rate_table, rate_dense)
    conv_new, conv_copy = adam_update(conv_state, grad_sums[0], rate_conv, decay_weights)
    mlp_new, mlp_copy = adam_update(mlp_state, grad_sums[1], dense_rate, decay_weights)
    small_new, small_copy = adam_update(small_state, grad_sums[2], rate_small, 0.0)
    return (block_out, input_grad, conv_new, mlp_new, small_new, conv_copy, mlp_copy, small_copy)
```

```python
import jax
import jax.numpy as jnp
from jax import lax
from jax.experimental import pallas as pl
from jax.experimental.pallas import tpu as pltpu
from jax.sharding import PartitionSpec as P

C = 128
EMB = 512
GROUPS = 8
H = 64
W = 64
NCLASS = 16
STEP = 10
TAPS = 9
CELLS = H * W
PER_GROUP = CELLS * (C // GROUPS)
TABLE_ROWS = NCLASS * EMB // C
M1_ROWS = EMB * EMB // C
M2_ROWS = EMB * 2
MLP_ROWS = TABLE_ROWS + M1_ROWS + M2_ROWS
KERNEL_ROWS = TAPS * C
AXES = ("dp", "fsdp")

beta_one = 0.9
beta_two = 0.999
adam_eps = 1e-08
ema_decay = 0.99
norm_eps = 1e-05
rate_conv = 0.08
rate_table = 0.6
rate_dense = 0.1
rate_small = 0.15
decay_weights = 0.01

f32 = jnp.float32
bf16 = jnp.bfloat16
NN = (((1,), (0,)), ((), ()))
NT = (((1,), (1,)), ((), ()))
TN = (((0,), (0,)), ((), ()))
VMEM_LIMIT = 58 << 20
R = 8
Q = 8


def mm(a, b, dims=NN):
    return lax.dot_general(a, b, dims, preferred_element_type=f32)


def three(v):
    high = v.astype(bf16)
    rest = v - high.astype(f32)
    mid = rest.astype(bf16)
    return high, mid, (rest - mid.astype(f32)).astype(bf16)


def group_sum(rows):
    lane = lax.broadcasted_iota(jnp.int32, rows.shape, 1)
    for step in (1, 2, 4, 8):
        up = pltpu.roll(rows, C - step, 1)
        down = pltpu.roll(rows, step, 1)
        rows = rows + jnp.where((lane & step) == 0, up, down)
    return rows


def fold(values):
    return jnp.sum(values.reshape(-1, 8, values.shape[-1]), axis=0)


def total_of(partial):
    return jnp.broadcast_to(jnp.sum(partial, axis=0, keepdims=True), partial.shape)


def one(rows):
    return rows[0:1].reshape(1, 1, C)


def normal_cdf(v):
    return 0.5 * (1.0 + lax.erf(v * 0.7071067811865476))


def gelu_slope(v, prob):
    return prob + v * (jnp.exp(-0.5 * v * v) * 0.3989422804014327)


def put_windows(win_ref, row, values):
    rows = values.shape[0]
    place = lax.broadcasted_iota(jnp.int32, values.shape, 1)
    left = jnp.where(place == 0, 0.0, pltpu.roll(values, 1, 1))
    right = jnp.where(place == W - 1, 0.0, pltpu.roll(values, W - 1, 1))
    win_ref[pl.ds(row + 1, rows), :, 0:C] = left.astype(bf16)
    win_ref[pl.ds(row + 1, rows), :, C : 2 * C] = values.astype(bf16)
    win_ref[pl.ds(row + 1, rows), :, 2 * C : 3 * C] = right.astype(bf16)


def clear_edges(win_ref):
    edge = jnp.zeros((1,) + tuple(win_ref.shape[1:]), win_ref.dtype)
    win_ref[0:1] = edge
    win_ref[H + 1 : H + 2] = edge


def pair_forward(pair_ref, kernel_ref):
    zero = jnp.zeros((3 * C, C), bf16)
    pair_ref[0 : TAPS * C, 0:C] = kernel_ref[...]
    pair_ref[TAPS * C :, 0:C] = zero
    pair_ref[0 : 3 * C, C:] = zero
    pair_ref[3 * C :, C:] = kernel_ref[...]


def flip(block):
    return jnp.transpose(block.astype(f32)).astype(bf16)


def pair_backward(pair_ref, kernel_ref):
    zero = jnp.zeros((3 * C, C), bf16)
    pair_ref[TAPS * C :, 0:C] = zero
    pair_ref[0 : 3 * C, C:] = zero
    for tap in range(TAPS):
        block = flip(kernel_ref[(TAPS - 1 - tap) * C : (TAPS - tap) * C, :])
        pair_ref[tap * C : (tap + 1) * C, 0:C] = block
        pair_ref[(tap + 3) * C : (tap + 4) * C, C:] = block


def pair_conv(win_ref, pair_ref, first):
    view = win_ref.reshape(H // 2 + 1, 2, W, 3 * C)
    taken = [view[pl.ds(first + t // 2, Q), t % 2] for t in range(4)]
    stacked = jnp.concatenate(taken, axis=-1).reshape(Q * W, 12 * C)
    return mm(stacked, pair_ref[...]).reshape(Q, W, 2 * C)


def pairs_of(ref, first):
    view = ref.reshape(H // 2, 2, W, C)
    return [view.at[pl.ds(first, Q), parity] for parity in range(2)]


def kernel_grad(act_ref, win_ref, out_ref):
    left = act_ref[1 : H + 1, :, C : 2 * C].reshape(CELLS, C)
    right = jnp.concatenate([win_ref[t : t + H] for t in range(3)], axis=-1)
    got = mm(left, right.reshape(CELLS, TAPS * C), TN)
    for t in range(TAPS):
        out_ref[t * C : (t + 1) * C, :] = got[:, (TAPS - 1 - t) * C : (TAPS - t) * C]


def block_body(
    cls_ref, x_ref, cot_ref, k1_ref, k2_ref, kd0_ref, kd1_ref, small_ref, table_ref, m1_ref, m2_ref,
    out_ref, dx_ref, gk1_ref, gk2_ref, gkd0_ref, gkd1_ref, gsmall_ref, gclass_ref,
    a1w, a2w, tw, rw, cw, c1, g1p, g2p, drf, pair,
):
    def small_row(index):
        return jnp.broadcast_to(small_ref[index : index + 1, :].astype(f32), (8, C))

    def small_run(first, count):
        return jnp.concatenate([small_ref[first + i : first + i + 1, :].astype(f32) for i in range(count)], axis=1)

    gain1, bias1, cb1, gain2, bias2, cb2 = [small_row(i) for i in range(6)]
    zero8 = jnp.zeros((8, C), f32)

    hidden = mm(table_ref[...], m1_ref[...]) + small_run(8, 4)
    act = hidden * normal_cdf(hidden)
    ss = sum(mm(part, m2_ref[...]) for part in three(act)) + small_run(12, 2)
    mine = lax.broadcasted_iota(jnp.int32, (NCLASS, 2 * C), 0) == cls_ref[0]
    chosen = jnp.sum(jnp.where(mine, ss, 0.0), axis=0, keepdims=True)
    scale = jnp.broadcast_to(1.0 + chosen[:, :C], (8, C))
    shift = jnp.broadcast_to(chosen[:, C:], (8, C))

    def read_x(i):
        return x_ref[pl.ds(i * R, R)].astype(f32)

    total = lax.fori_loop(0, H // R, lambda i, s: s + fold(read_x(i)), zero8)
    mean1 = group_sum(total_of(total)) * (1.0 / PER_GROUP)

    def square_x(i, s):
        d = read_x(i) - one(mean1)
        return s + fold(d * d)

    var1 = group_sum(total_of(lax.fori_loop(0, H // R, square_x, zero8))) * (1.0 / PER_GROUP)
    rs1 = lax.rsqrt(var1 + norm_eps)
    slope1 = rs1 * (1.0 + gain1)
    clear_edges(a1w)

    def front1(i, carry):
        v = (read_x(i) - one(mean1)) * one(slope1) + one(bias1)
        prob = normal_cdf(v)
        put_windows(a1w, i * R, v * prob)
        g1p[pl.ds(i * R, R)] = gelu_slope(v, prob)
        return carry

    lax.fori_loop(0, H // R, front1, 0)

    pair_forward(pair, k1_ref)

    def conv1(i, s):
        got = pair_conv(a1w, pair, i * Q)
        for parity, place in enumerate(pairs_of(c1, i * Q)):
            value = got[..., parity * C : (parity + 1) * C] + one(cb1)
            place[...] = value
            s = s + fold(value)
        return s

    centre = total_of(lax.fori_loop(0, H // 2 // Q, conv1, zero8)) * (1.0 / CELLS)

    def square_c(i, s):
        d = c1[pl.ds(i * R, R)] - one(centre)
        return s + fold(d * d)

    spread = total_of(lax.fori_loop(0, H // R, square_c, zero8)) * (1.0 / CELLS)

    centre_s = centre * scale + shift
    mean2 = group_sum(centre_s) * (GROUPS / C)
    off = centre_s - mean2
    var2 = group_sum(spread * scale * scale + off * off) * (GROUPS / C)
    rs2 = lax.rsqrt(var2 + norm_eps)

    def unit2(values):
        return (values * one(scale) + one(shift - mean2)) * one(rs2)

    clear_edges(a2w)

    def front2(i, carry):
        v = unit2(c1[pl.ds(i * R, R)]) * one(1.0 + gain2) + one(bias2)
        prob = normal_cdf(v)
        put_windows(a2w, i * R, v * prob)
        g2p[pl.ds(i * R, R)] = gelu_slope(v, prob)
        return carry

    lax.fori_loop(0, H // R, front2, 0)

    pair_forward(pair, k2_ref)

    def conv2(i, carry):
        got = pair_conv(a2w, pair, i * Q)
        for parity, (place, source) in enumerate(zip(pairs_of(drf, i * Q), pairs_of(x_ref, i * Q))):
            r = source[...].astype(f32) + (got[..., parity * C : (parity + 1) * C] + one(cb2))
            place[...] = r.astype(bf16).astype(f32)
        return carry

    lax.fori_loop(0, H // 2 // Q, conv2, 0)
    rw[0:1] = jnp.zeros((1, W // 2, 3 * C), bf16)

    def split(i, carry):
        even = drf[pl.ds(i * R, R), pl.ds(0, W // 2, 2), :]
        odd = drf[pl.ds(i * R, R), pl.ds(1, W // 2, 2), :]
        place = lax.broadcasted_iota(jnp.int32, odd.shape, 1)
        before = jnp.where(place == 0, 0.0, pltpu.roll(odd, 1, 1))
        rw[pl.ds(i * R + 1, R), :, 0:C] = before.astype(bf16)
        rw[pl.ds(i * R + 1, R), :, C : 2 * C] = even.astype(bf16)
        rw[pl.ds(i * R + 1, R), :, 2 * C :] = odd.astype(bf16)
        return carry

    lax.fori_loop(0, H // R, split, 0)

    def down_rows(first, rows):
        view = rw.reshape(H // 2 + 1, 2, W // 2, 3 * C)
        taken = [view[pl.ds(first + t // 2, rows), t % 2] for t in range(3)]
        return jnp.concatenate(taken, axis=-1).reshape(rows * W // 2, TAPS * C)

    kd = jnp.concatenate([kd0_ref[...], kd1_ref[...]], axis=1)
    bias_down = small_run(6, 2)

    def down(i, carry):
        got = mm(down_rows(i * Q, Q), kd) + bias_down
        out_ref[pl.ds(i * Q, Q)] = got.reshape(Q, W // 2, 2 * C).astype(bf16)
        return carry

    lax.fori_loop(0, H // 2 // Q, down, 0)
    @pl.when(cls_ref[0] >= 0)
    def _():
        gkd = mm(down_rows(0, H // 2), cot_ref[...].reshape(CELLS // 4, 2 * C), TN)
        gkd0_ref[...] = gkd[:, :C]
        gkd1_ref[...] = gkd[:, C:]


    cw[H // 2 : H // 2 + 1] = jnp.zeros((1, W // 2, 4 * C), bf16)

    def cot_windows(i, s):
        values = cot_ref[pl.ds(i * Q, Q)].astype(f32)
        place = lax.broadcasted_iota(jnp.int32, values.shape, 1)
        after = jnp.where(place == W // 2 - 1, 0.0, pltpu.roll(values, W // 2 - 1, 1))
        cw[pl.ds(i * Q, Q), :, 0 : 2 * C] = values.astype(bf16)
        cw[pl.ds(i * Q, Q), :, 2 * C :] = after.astype(bf16)
        return s + fold(values)

    gdb = total_of(lax.fori_loop(0, H // 2 // Q, cot_windows, jnp.zeros((8, 2 * C), f32)))

    def tap(i, j):
        return flip(kd[(3 * i + j) * C : (3 * i + j + 1) * C, :])

    none = jnp.zeros((2 * C, C), bf16)
    even_rows = jnp.concatenate([
        jnp.concatenate([tap(1, 1), none], axis=0),
        jnp.concatenate([tap(1, 2), tap(1, 0)], axis=0),
    ], axis=1)
    odd_rows = jnp.concatenate([
        jnp.concatenate([tap(2, 1), none, tap(0, 1), none], axis=0),
        jnp.concatenate([tap(2, 2), tap(2, 0), tap(0, 2), tap(0, 0)], axis=0),
    ], axis=1)

    def back_down(i, s):
        rows = jnp.concatenate([cw[pl.ds(i * Q, Q)], cw[pl.ds(i * Q + 1, Q)]], axis=-1)
        rows = rows.reshape(Q * W // 2, 8 * C)
        view = drf.reshape(H // 2, 2, W, C)
        for parity, got in enumerate((mm(rows[:, : 4 * C], even_rows), mm(rows, odd_rows))):
            got = got.reshape(Q, W // 2, 2 * C)
            view[pl.ds(i * Q, Q), parity, pl.ds(0, W // 2, 2), :] = got[..., :C]
            view[pl.ds(i * Q, Q), parity, pl.ds(1, W // 2, 2), :] = got[..., C:]
        return s

    lax.fori_loop(0, H // 2 // Q, back_down, 0)

    def pull(kernel_ref, slope_ref, units):
        pair_backward(pair, kernel_ref)

        def step(i, s):
            got = pair_conv(tw, pair, i * Q)
            for parity, (place, unit) in enumerate(zip(pairs_of(slope_ref, i * Q), units(i))):
                dn = got[..., parity * C : (parity + 1) * C] * place[...]
                place[...] = dn
                s = s[0] + fold(dn), s[1] + fold(dn * unit)
            return s

        got = lax.fori_loop(0, H // 2 // Q, step, (zero8, zero8))
        return total_of(got[0]), total_of(got[1])

    clear_edges(tw)

    def t2_windows(i, s):
        values = drf[pl.ds(i * R, R)]
        put_windows(tw, i * R, values)
        return s + fold(values)

    gcb2 = total_of(lax.fori_loop(0, H // R, t2_windows, zero8))
    pl.when(cls_ref[0] >= 0)(lambda: kernel_grad(a2w, tw, gk2_ref))
    gb2, gg2 = pull(k2_ref, g2p, lambda i: [unit2(ref[...]) for ref in pairs_of(c1, i * Q)])
    mean_du2 = group_sum(gb2 * (1.0 + gain2)) * (1.0 / PER_GROUP)
    mean_duu2 = group_sum(gg2 * (1.0 + gain2)) * (1.0 / PER_GROUP)

    def t1_windows(i, s):
        values = c1[pl.ds(i * R, R)]
        du = g2p[pl.ds(i * R, R)] * one(1.0 + gain2)
        ds = (du - one(mean_du2) - unit2(values) * one(mean_duu2)) * one(rs2)
        put_windows(tw, i * R, ds * one(scale))
        return s[0] + fold(ds * values), s[1] + fold(ds)

    gsc, gsh = lax.fori_loop(0, H // R, t1_windows, (zero8, zero8))
    gsc, gsh = total_of(gsc), total_of(gsh)
    pl.when(cls_ref[0] >= 0)(lambda: kernel_grad(a1w, tw, gk1_ref))

    def unit1(ref):
        return (ref[...].astype(f32) - one(mean1)) * one(rs1)

    gb1, gg1 = pull(k1_ref, g1p, lambda i: [unit1(ref) for ref in pairs_of(x_ref, i * Q)])
    mean_du1 = group_sum(gb1 * (1.0 + gain1)) * (1.0 / PER_GROUP)
    mean_duu1 = group_sum(gg1 * (1.0 + gain1)) * (1.0 / PER_GROUP)

    def finish(i, carry):
        du = g1p[pl.ds(i * R, R)] * one(1.0 + gain1)
        unit = unit1(x_ref.at[pl.ds(i * R, R)])
        dx = (du - one(mean_du1) - unit * one(mean_duu1)) * one(rs1)
        dx_ref[pl.ds(i * R, R)] = (drf[pl.ds(i * R, R)] + dx).astype(bf16)
        return carry

    lax.fori_loop(0, H // R, finish, 0)

    rows = [gg1, gb1, gsh * scale, gg2, gb2, gcb2, gdb[:, :C], gdb[:, C:]]
    for index, row in enumerate(rows):
        gsmall_ref[index : index + 1, :] = row[0:1]
    both = jnp.concatenate([gsc[0:1], gsh[0:1]], axis=1)
    gclass_ref[...] = jnp.where(mine, both, 0.0)


def vmem_specs(count):
    return [pl.BlockSpec(memory_space=pltpu.VMEM)] * count


def run_block(class_ids, x, cot, kernels, small, mlp):
    shapes = (
        [jax.ShapeDtypeStruct((H // 2, W // 2, 2 * C), bf16), jax.ShapeDtypeStruct((H, W, C), bf16)]
        + [jax.ShapeDtypeStruct((KERNEL_ROWS, C), f32)] * 4
        + [jax.ShapeDtypeStruct((8, C), f32), jax.ShapeDtypeStruct((NCLASS, 2 * C), f32)]
    )
    windows = pltpu.VMEM((H + 2, W, 3 * C), bf16)
    plane = pltpu.VMEM((H, W, C), f32)
    return pl.pallas_call(
        block_body,
        out_shape=shapes,
        in_specs=[pl.BlockSpec(memory_space=pltpu.SMEM)] + vmem_specs(10),
        out_specs=vmem_specs(8),
        scratch_shapes=[
            windows,
            windows,
            windows,
            pltpu.VMEM((H + 2, W // 2, 3 * C), bf16),
            pltpu.VMEM((H // 2 + 1, W // 2, 4 * C), bf16),
            plane,
            plane,
            plane,
            plane,
            pltpu.VMEM((12 * C, 2 * C), bf16),
        ],
        compiler_params=pltpu.CompilerParams(vmem_limit_bytes=VMEM_LIMIT),
        name="block",
    )(class_ids, x, cot, *kernels, small, *mlp)


def mlp_body(table_ref, m1_ref, m2_ref, small_ref, dss_ref, out_ref, tail_ref):
    def small_run(first, count):
        return jnp.concatenate([small_ref[first + i : first + i + 1, :].astype(f32) for i in range(count)], axis=1)

    table = table_ref[...]
    hidden = mm(table, m1_ref[...]) + small_run(8, 4)
    prob = normal_cdf(hidden)
    dss = dss_ref[...]

    def put(first, values):
        parts = values.shape[1] // C
        for part in range(parts):
            out_ref[pl.ds(first + part, values.shape[0], parts), :] = values[:, part * C : (part + 1) * C]

    def outer(left, right):
        lefts = [a for k, a in enumerate(left) for b in right[: 3 - k]]
        rights = [b for k, a in enumerate(left) for b in right[: 3 - k]]
        return mm(jnp.concatenate(lefts, axis=0), jnp.concatenate(rights, axis=0), TN)

    def back(values, weights):
        return sum(mm(part, weights, NT) for part in three(values))

    dp = back(dss, m2_ref[...]) * gelu_slope(hidden, prob)
    put(0, back(dp, m1_ref[...]))
    put(TABLE_ROWS, outer([table], three(dp)))
    put(TABLE_ROWS + M1_ROWS, outer(three(hidden * prob), three(dss)))
    ge1 = jnp.sum(dp, axis=0, keepdims=True)
    ge2 = jnp.sum(dss, axis=0, keepdims=True)
    for i in range(4):
        tail_ref[i : i + 1, :] = ge1[:, i * C : (i + 1) * C]
    for i in range(2):
        tail_ref[4 + i : 5 + i, :] = ge2[:, i * C : (i + 1) * C]
    tail_ref[6:8, :] = jnp.zeros((2, C), f32)


def run_mlp(mlp, small, dss):
    return pl.pallas_call(
        mlp_body,
        out_shape=[jax.ShapeDtypeStruct((MLP_ROWS, C), f32), jax.ShapeDtypeStruct((8, C), f32)],
        in_specs=vmem_specs(5),
        out_specs=vmem_specs(2),
        compiler_params=pltpu.CompilerParams(vmem_limit_bytes=VMEM_LIMIT),
        name="mlp_grad",
    )(*mlp, small, dss)


def adam_update(state_stack, gradient, step_rate, weight_decay):
    weight = state_stack[0]
    first_moment = beta_one * state_stack[1] + (1.0 - beta_one) * gradient
    second = beta_two * state_stack[2] + (1.0 - beta_two) * gradient * gradient
    first_hat = first_moment / (1.0 - beta_one**STEP)
    second_hat = second / (1.0 - beta_two**STEP)
    weight_new = weight - step_rate * (
        first_hat / (jnp.sqrt(second_hat) + adam_eps) + weight_decay * weight
    )
    average = ema_decay * state_stack[3] + (1.0 - ema_decay) * weight_new
    return (jnp.stack([weight_new, first_moment, second, average]), weight_new.astype(bf16))


def exchange(values, axis, size, bit):
    return lax.ppermute(values, axis, [(i, i ^ bit) for i in range(size)])


def stage_list(sizes):
    (outer, outer_size), (inner, inner_size) = sizes
    inner_bits = [1 << k for k in reversed(range(inner_size.bit_length() - 1))]
    outer_bits = [1 << k for k in range(outer_size.bit_length() - 1)]
    inner_stages = [(inner, inner_size, bit, bit) for bit in inner_bits]
    outer_stages = [(outer, outer_size, bit, bit * inner_size) for bit in outer_bits]
    return inner_stages[:-1] + outer_stages + inner_stages[-1:]


def relative(sizes, position):
    order = [0]
    for _, _, _, bit in stage_list(sizes):
        order = order + [k ^ bit for k in order]
    return jnp.asarray(order, jnp.int32) ^ position


def inverse(sizes, position):
    order = [0]
    for _, _, _, bit in stage_list(sizes):
        order = order + [k ^ bit for k in order]
    place = [order.index(k) for k in range(len(order))]
    return jnp.asarray(place, jnp.int32)[jnp.arange(len(order), dtype=jnp.int32) ^ position]


def gather_ring(own, sizes):
    parts = own[None]
    for axis, size, bit, _ in stage_list(sizes):
        parts = jnp.concatenate([parts, exchange(parts, axis, size, bit)])
    return parts


def reduce_ring(blocks, extra, sizes):
    rows = extra.shape[0]
    for axis, size, bit, _ in reversed(stage_list(sizes)):
        half = blocks.shape[0] // 2
        high = extra.astype(bf16)
        low = (extra - high.astype(f32)).astype(bf16)
        width = blocks.shape[1]
        sent = jnp.concatenate([blocks[half:].astype(bf16).reshape(-1, C), high, low])
        got = exchange(sent, axis, size, bit)
        blocks = blocks[:half] + got[: half * width].reshape(half, width, C).astype(f32)
        extra = (
            extra
            + got[half * width : half * width + rows].astype(f32)
            + got[half * width + rows :].astype(f32)
        )
    return blocks[0], extra


def split_mlp(dense):
    return [
        dense[:TABLE_ROWS].reshape(NCLASS, EMB),
        dense[TABLE_ROWS : TABLE_ROWS + M1_ROWS].reshape(EMB, EMB),
        dense[TABLE_ROWS + M1_ROWS :].reshape(EMB, 2 * C),
    ]


def gather_all(sizes, position, conv_own, dense_own, small_own):
    conv_len, dense_len, small_len = conv_own.shape[1], dense_own.shape[0], small_own.shape[0]
    if not whole_rows(sizes, conv_len, dense_len):
        conv = lax.all_gather(conv_own, AXES, axis=1, tiled=True)
        dense = lax.all_gather(dense_own, AXES, axis=0, tiled=True)
        small = lax.all_gather(small_own, AXES, axis=0, tiled=True)
        return [conv[k].reshape(KERNEL_ROWS, C) for k in range(4)], dense.reshape(MLP_ROWS, C), small.reshape(-1, C)
    conv_rows, dense_rows = conv_len // C, dense_len // C
    own_rows = 4 * conv_rows + dense_rows
    own = jnp.concatenate(
        [
            conv_own.reshape(4 * conv_rows, C),
            dense_own.reshape(dense_rows, C),
            jnp.pad(small_own, (0, C - small_len)).reshape(1, C),
        ]
    )
    gathered = gather_ring(own, sizes)[inverse(sizes, position)]
    kernels = [
        gathered[:, k * conv_rows : (k + 1) * conv_rows].reshape(KERNEL_ROWS, C) for k in range(4)
    ]
    dense = gathered[:, 4 * conv_rows : own_rows].reshape(MLP_ROWS, C)
    return kernels, dense, gathered[:, own_rows, :small_len].reshape(-1, C)


def reduce_all(sizes, position, grads, extra, conv_len, dense_len):
    if not whole_rows(sizes, conv_len, dense_len):
        flat = jnp.stack([g.reshape(-1) for g in grads])
        return lax.psum_scatter(flat, AXES, scatter_dimension=1, tiled=True), lax.psum(extra, AXES)
    conv_rows = conv_len // C
    blocks = jnp.concatenate([g.reshape(-1, conv_rows, C) for g in grads], axis=1)
    red, extra = reduce_ring(blocks[relative(sizes, position)], extra, sizes)
    return red.reshape(4, conv_len), extra


def whole_rows(sizes, conv_len, dense_len):
    return conv_len % C == 0 and dense_len % C == 0 and all(n & (n - 1) == 0 for _, n in sizes)


def per_device(sizes, samples, cotangent, class_ids, conv_state, mlp_state, small_state):
    position = lax.axis_index(AXES)
    conv_len, dense_len, small_len = conv_state.shape[2], mlp_state.shape[1], small_state.shape[1]
    kernels, dense, small = gather_all(
        sizes, position, conv_state[0].astype(bf16), mlp_state[0].astype(bf16), small_state[0].astype(bf16)
    )
    mlp = split_mlp(dense)
    out, dx, gk1, gk2, gkd0, gkd1, gsmall, gclass = run_block(
        class_ids, samples[0], cotangent[0], kernels, small, mlp
    )
    extra = jnp.concatenate([gsmall, gclass.reshape(2 * NCLASS, C)])
    conv_red, extra = reduce_all(sizes, position, (gk1, gk2, gkd0, gkd1), extra, conv_len, dense_len)
    dense_grad, tail = run_mlp(mlp, small, extra[8:].reshape(NCLASS, 2 * C))
    dense_red = lax.dynamic_slice_in_dim(dense_grad.reshape(-1), position * dense_len, dense_len)
    small_red = lax.dynamic_slice_in_dim(
        jnp.concatenate([extra[:8], tail]).reshape(-1), position * small_len, small_len
    )
    flat_index = position * dense_len + jnp.arange(dense_len, dtype=jnp.int32)
    dense_rate = jnp.where(flat_index < NCLASS * EMB, rate_table, rate_dense)
    conv_new, conv_copy = adam_update(conv_state, conv_red, rate_conv, decay_weights)
    mlp_new, mlp_copy = adam_update(mlp_state, dense_red, dense_rate, decay_weights)
    small_new, small_copy = adam_update(small_state, small_red, rate_small, 0.0)
    return (out[None], dx[None], conv_new, mlp_new, small_new, conv_copy, mlp_copy, small_copy)


def solution(mesh):
    sizes = tuple((axis, mesh.shape[axis]) for axis in AXES)

    def body(*args):
        return per_device(sizes, *args)

    return jax.shard_map(
        body,
        mesh=mesh,
        in_specs=(
            P(AXES, None, None, None),
            P(AXES, None, None, None),
            P(AXES),
            P(None, None, AXES),
            P(None, AXES),
            P(None, AXES),
        ),
        out_specs=(
            P(AXES, None, None, None),
            P(AXES, None, None, None),
            P(None, None, AXES),
            P(None, AXES),
            P(None, AXES),
            P(None, AXES),
            P(AXES),
            P(AXES),
        ),
        check_vma=False,
    )
```

```python
import functools

import jax
import jax.numpy as jnp
from jax import lax
from jax.experimental import pallas as pl
from jax.experimental.pallas import tpu as pltpu
from jax.sharding import PartitionSpec as P

C = 128
EMB = 512
GROUPS = 8
H = 64
W = 64
NCLASS = 16
STEP = 10
TAPS = 9
CELLS = H * W
PER_GROUP = CELLS * (C // GROUPS)
TABLE_ROWS = NCLASS * EMB // C
M1_ROWS = EMB * EMB // C
M2_ROWS = EMB * 2
MLP_ROWS = TABLE_ROWS + M1_ROWS + M2_ROWS
KERNEL_ROWS = TAPS * C
AXES = ("dp", "fsdp")

beta_one = 0.9
beta_two = 0.999
adam_eps = 1e-08
ema_decay = 0.99
norm_eps = 1e-05
rate_conv = 0.08
rate_table = 0.6
rate_dense = 0.1
rate_small = 0.15
decay_weights = 0.01

f32 = jnp.float32
bf16 = jnp.bfloat16
NN = (((1,), (0,)), ((), ()))
NT = (((1,), (1,)), ((), ()))
TN = (((0,), (0,)), ((), ()))
EXTRA = 8 + 2 * NCLASS
R = 8
Q = 8


def mm(a, b, dims=NN):
    return lax.dot_general(a, b, dims, preferred_element_type=f32)


def three(v):
    high = v.astype(bf16)
    rest = v - high.astype(f32)
    mid = rest.astype(bf16)
    return high, mid, (rest - mid.astype(f32)).astype(bf16)


def group_sum(rows):
    lane = lax.broadcasted_iota(jnp.int32, rows.shape, 1)
    for step in (1, 2, 4, 8):
        up = pltpu.roll(rows, C - step, 1)
        down = pltpu.roll(rows, step, 1)
        rows = rows + jnp.where((lane & step) == 0, up, down)
    return rows


def fold(values):
    return jnp.sum(values.reshape(-1, 8, values.shape[-1]), axis=0)


def total_of(partial):
    return jnp.broadcast_to(jnp.sum(partial, axis=0, keepdims=True), partial.shape)


def one(rows):
    return rows[0:1].reshape(1, 1, C)


def normal_cdf(v):
    return 0.5 * (1.0 + lax.erf(v * 0.7071067811865476))


def gelu_slope(v, prob):
    return prob + v * (jnp.exp(-0.5 * v * v) * 0.3989422804014327)


def put_windows(win_ref, row, values):
    rows = values.shape[0]
    place = lax.broadcasted_iota(jnp.int32, values.shape, 1)
    left = jnp.where(place == 0, 0.0, pltpu.roll(values, 1, 1))
    right = jnp.where(place == W - 1, 0.0, pltpu.roll(values, W - 1, 1))
    win_ref[pl.ds(row + 1, rows), :, 0:C] = left.astype(bf16)
    win_ref[pl.ds(row + 1, rows), :, C : 2 * C] = values.astype(bf16)
    win_ref[pl.ds(row + 1, rows), :, 2 * C : 3 * C] = right.astype(bf16)


def clear_edges(win_ref):
    edge = jnp.zeros((1,) + tuple(win_ref.shape[1:]), win_ref.dtype)
    win_ref[0:1] = edge
    win_ref[H + 1 : H + 2] = edge


def pair_forward(pair_ref, kernel_ref):
    zero = jnp.zeros((3 * C, C), bf16)
    pair_ref[0 : TAPS * C, 0:C] = kernel_ref[...]
    pair_ref[TAPS * C :, 0:C] = zero
    pair_ref[0 : 3 * C, C:] = zero
    pair_ref[3 * C :, C:] = kernel_ref[...]


def flip(block):
    return jnp.transpose(block.astype(f32)).astype(bf16)


def pair_backward(pair_ref, kernel_ref):
    zero = jnp.zeros((3 * C, C), bf16)
    pair_ref[TAPS * C :, 0:C] = zero
    pair_ref[0 : 3 * C, C:] = zero
    for tap in range(TAPS):
        block = flip(kernel_ref[(TAPS - 1 - tap) * C : (TAPS - tap) * C, :])
        pair_ref[tap * C : (tap + 1) * C, 0:C] = block
        pair_ref[(tap + 3) * C : (tap + 4) * C, C:] = block


def pair_conv(win_ref, pair_ref, first):
    view = win_ref.reshape(H // 2 + 1, 2, W, 3 * C)
    taken = [view[pl.ds(first + t // 2, Q), t % 2] for t in range(4)]
    stacked = jnp.concatenate(taken, axis=-1).reshape(Q * W, 12 * C)
    return mm(stacked, pair_ref[...]).reshape(Q, W, 2 * C)


def pairs_of(ref, first):
    view = ref.reshape(H // 2, 2, W, C)
    return [view.at[pl.ds(first, Q), parity] for parity in range(2)]


def kernel_grad(act_ref, win_ref, out_ref):
    left = act_ref[1 : H + 1, :, C : 2 * C].reshape(CELLS, C)
    right = jnp.concatenate([win_ref[t : t + H] for t in range(3)], axis=-1)
    got = mm(left, right.reshape(CELLS, TAPS * C), TN)
    for t in range(TAPS):
        out_ref[t * C : (t + 1) * C, :] = got[:, (TAPS - 1 - t) * C : (TAPS - t) * C]


def position_of(sizes):
    (outer, _), (inner, inner_size) = sizes
    return lax.axis_index(outer) * inner_size + lax.axis_index(inner)


def take_shards(plan, me, parts, conv, dense):
    conv[...] = jnp.zeros(conv.shape, f32)
    dense[...] = jnp.zeros(dense.shape, f32)
    small = jnp.zeros((16, C), f32)
    for (near, turn), part_ref in zip(plan.sources, parts):
        values = part_ref[near].astype(f32)
        owner = me ^ turn
        first = plan.tile_of(owner * plan.conv_rows)
        for k in range(4):
            conv[k, pl.ds(first, plan.conv_pad), :] += values[k * plan.conv_pad : (k + 1) * plan.conv_pad]
        first = plan.tile_of(owner * plan.dense_rows)
        dense[pl.ds(first, plan.dense_pad), :] += values[plan.dense_at : plan.dense_at + plan.dense_pad]
        small = small + values[plan.small_at : plan.small_at + 16]
    return small


def block_body(plan, *refs):
    refs = list(refs)
    cls_ref, x_ref, cot_ref = refs[:3]
    inputs = refs[3 : 3 + plan.inputs]
    out_ref, dx_ref, table_ref, m1_ref, m2_ref, hidden_ref = refs[3 + plan.inputs : 9 + plan.inputs]
    results = refs[9 + plan.inputs : 11 + plan.inputs]
    a1w, a2w, tw, rw, cw, c1, g1p, g2p, drf, pair, conv, dense, kernels, smalls = refs[11 + plan.inputs :]
    me = position_of(plan.sizes)
    if plan.rings:
        parts = [ref for ref in inputs for _ in range(plan.line)]
        smalls[...] = take_shards(plan, me, parts, conv, dense)
        kernels[...] = conv[:, 0:KERNEL_ROWS].astype(bf16)
    else:
        kernels[...] = inputs[0][...]
        dense[0:MLP_ROWS] = inputs[1][...].astype(f32)
        smalls[0:14] = inputs[2][...].astype(f32)

    def lanes(first, rows, parts):
        pieces = [dense[pl.ds(first + part, rows, parts), :] for part in range(parts)]
        return jnp.concatenate(pieces, axis=1).astype(bf16)

    table_ref[...] = lanes(0, NCLASS, EMB // C)
    m1_ref[...] = lanes(TABLE_ROWS, EMB, EMB // C)
    m2_ref[...] = lanes(TABLE_ROWS + M1_ROWS, EMB, 2)
    k1_ref, k2_ref, kd0_ref, kd1_ref = [kernels.at[k] for k in range(4)]
    gk1_ref, gk2_ref, gkd0_ref, gkd1_ref = [conv.at[k] for k in range(4)]

    def small_row(index):
        return jnp.broadcast_to(smalls[index : index + 1, :], (8, C))

    def small_run(first, count):
        return jnp.concatenate([smalls[first + i : first + i + 1, :] for i in range(count)], axis=1)

    def alone(step):
        pl.when(me >= 0)(step)

    gain1, bias1, cb1, gain2, bias2, cb2 = [small_row(i) for i in range(6)]
    zero8 = jnp.zeros((8, C), f32)

    hidden = mm(table_ref[...], m1_ref[...]) + small_run(8, 4)
    hidden_ref[...] = hidden
    act = hidden * normal_cdf(hidden)
    ss = sum(mm(part, m2_ref[...]) for part in three(act)) + small_run(12, 2)
    mine = lax.broadcasted_iota(jnp.int32, (NCLASS, 2 * C), 0) == cls_ref[0]
    chosen = jnp.sum(jnp.where(mine, ss, 0.0), axis=0, keepdims=True)
    scale = jnp.broadcast_to(1.0 + chosen[:, :C], (8, C))
    shift = jnp.broadcast_to(chosen[:, C:], (8, C))

    def read_x(i):
        return x_ref[pl.ds(i * R, R)].astype(f32)

    total = lax.fori_loop(0, H // R, lambda i, s: s + fold(read_x(i)), zero8)
    mean1 = group_sum(total_of(total)) * (1.0 / PER_GROUP)

    def square_x(i, s):
        d = read_x(i) - one(mean1)
        return s + fold(d * d)

    var1 = group_sum(total_of(lax.fori_loop(0, H // R, square_x, zero8))) * (1.0 / PER_GROUP)
    rs1 = lax.rsqrt(var1 + norm_eps)
    slope1 = rs1 * (1.0 + gain1)
    clear_edges(a1w)

    def front1(i, carry):
        v = (read_x(i) - one(mean1)) * one(slope1) + one(bias1)
        prob = normal_cdf(v)
        put_windows(a1w, i * R, v * prob)
        g1p[pl.ds(i * R, R)] = gelu_slope(v, prob)
        return carry

    lax.fori_loop(0, H // R, front1, 0)

    pair_forward(pair, k1_ref)

    def conv1(i, s):
        got = pair_conv(a1w, pair, i * Q)
        for parity, place in enumerate(pairs_of(c1, i * Q)):
            value = got[..., parity * C : (parity + 1) * C] + one(cb1)
            place[...] = value
            s = s + fold(value)
        return s

    centre = total_of(lax.fori_loop(0, H // 2 // Q, conv1, zero8)) * (1.0 / CELLS)

    def square_c(i, s):
        d = c1[pl.ds(i * R, R)] - one(centre)
        return s + fold(d * d)

    spread = total_of(lax.fori_loop(0, H // R, square_c, zero8)) * (1.0 / CELLS)

    centre_s = centre * scale + shift
    mean2 = group_sum(centre_s) * (GROUPS / C)
    off = centre_s - mean2
    var2 = group_sum(spread * scale * scale + off * off) * (GROUPS / C)
    rs2 = lax.rsqrt(var2 + norm_eps)

    def unit2(values):
        return (values * one(scale) + one(shift - mean2)) * one(rs2)

    clear_edges(a2w)

    def front2(i, carry):
        v = unit2(c1[pl.ds(i * R, R)]) * one(1.0 + gain2) + one(bias2)
        prob = normal_cdf(v)
        put_windows(a2w, i * R, v * prob)
        g2p[pl.ds(i * R, R)] = gelu_slope(v, prob)
        return carry

    lax.fori_loop(0, H // R, front2, 0)

    pair_forward(pair, k2_ref)

    def conv2(i, carry):
        got = pair_conv(a2w, pair, i * Q)
        for parity, (place, source) in enumerate(zip(pairs_of(drf, i * Q), pairs_of(x_ref, i * Q))):
            r = source[...].astype(f32) + (got[..., parity * C : (parity + 1) * C] + one(cb2))
            place[...] = r.astype(bf16).astype(f32)
        return carry

    lax.fori_loop(0, H // 2 // Q, conv2, 0)
    rw[0:1] = jnp.zeros((1, W // 2, 3 * C), bf16)

    def split(i, carry):
        even = drf[pl.ds(i * R, R), pl.ds(0, W // 2, 2), :]
        odd = drf[pl.ds(i * R, R), pl.ds(1, W // 2, 2), :]
        place = lax.broadcasted_iota(jnp.int32, odd.shape, 1)
        before = jnp.where(place == 0, 0.0, pltpu.roll(odd, 1, 1))
        rw[pl.ds(i * R + 1, R), :, 0:C] = before.astype(bf16)
        rw[pl.ds(i * R + 1, R), :, C : 2 * C] = even.astype(bf16)
        rw[pl.ds(i * R + 1, R), :, 2 * C :] = odd.astype(bf16)
        return carry

    lax.fori_loop(0, H // R, split, 0)

    def down_rows(first, rows):
        view = rw.reshape(H // 2 + 1, 2, W // 2, 3 * C)
        taken = [view[pl.ds(first + t // 2, rows), t % 2] for t in range(3)]
        return jnp.concatenate(taken, axis=-1).reshape(rows * W // 2, TAPS * C)

    kd = jnp.concatenate([kd0_ref[...], kd1_ref[...]], axis=1)
    bias_down = small_run(6, 2)

    def down(i, carry):
        got = mm(down_rows(i * Q, Q), kd) + bias_down
        out_ref[pl.ds(i * Q, Q)] = got.reshape(Q, W // 2, 2 * C).astype(bf16)
        return carry

    lax.fori_loop(0, H // 2 // Q, down, 0)
    @alone
    def _():
        gkd = mm(down_rows(0, H // 2), cot_ref[...].reshape(CELLS // 4, 2 * C), TN)
        gkd0_ref[0:KERNEL_ROWS] = gkd[:, :C]
        gkd1_ref[0:KERNEL_ROWS] = gkd[:, C:]


    cw[H // 2 : H // 2 + 1] = jnp.zeros((1, W // 2, 4 * C), bf16)

    def cot_windows(i, s):
        values = cot_ref[pl.ds(i * Q, Q)].astype(f32)
        place = lax.broadcasted_iota(jnp.int32, values.shape, 1)
        after = jnp.where(place == W // 2 - 1, 0.0, pltpu.roll(values, W // 2 - 1, 1))
        cw[pl.ds(i * Q, Q), :, 0 : 2 * C] = values.astype(bf16)
        cw[pl.ds(i * Q, Q), :, 2 * C :] = after.astype(bf16)
        return s + fold(values)

    gdb = total_of(lax.fori_loop(0, H // 2 // Q, cot_windows, jnp.zeros((8, 2 * C), f32)))

    def tap(i, j):
        return flip(kd[(3 * i + j) * C : (3 * i + j + 1) * C, :])

    none = jnp.zeros((2 * C, C), bf16)
    even_rows = jnp.concatenate([
        jnp.concatenate([tap(1, 1), none], axis=0),
        jnp.concatenate([tap(1, 2), tap(1, 0)], axis=0),
    ], axis=1)
    odd_rows = jnp.concatenate([
        jnp.concatenate([tap(2, 1), none, tap(0, 1), none], axis=0),
        jnp.concatenate([tap(2, 2), tap(2, 0), tap(0, 2), tap(0, 0)], axis=0),
    ], axis=1)

    def back_down(i, s):
        rows = jnp.concatenate([cw[pl.ds(i * Q, Q)], cw[pl.ds(i * Q + 1, Q)]], axis=-1)
        rows = rows.reshape(Q * W // 2, 8 * C)
        view = drf.reshape(H // 2, 2, W, C)
        for parity, got in enumerate((mm(rows[:, : 4 * C], even_rows), mm(rows, odd_rows))):
            got = got.reshape(Q, W // 2, 2 * C)
            view[pl.ds(i * Q, Q), parity, pl.ds(0, W // 2, 2), :] = got[..., :C]
            view[pl.ds(i * Q, Q), parity, pl.ds(1, W // 2, 2), :] = got[..., C:]
        return s

    lax.fori_loop(0, H // 2 // Q, back_down, 0)

    def pull(kernel_ref, slope_ref, units):
        pair_backward(pair, kernel_ref)

        def step(i, s):
            got = pair_conv(tw, pair, i * Q)
            for parity, (place, unit) in enumerate(zip(pairs_of(slope_ref, i * Q), units(i))):
                dn = got[..., parity * C : (parity + 1) * C] * place[...]
                place[...] = dn
                s = s[0] + fold(dn), s[1] + fold(dn * unit)
            return s

        got = lax.fori_loop(0, H // 2 // Q, step, (zero8, zero8))
        return total_of(got[0]), total_of(got[1])

    clear_edges(tw)

    def t2_windows(i, s):
        values = drf[pl.ds(i * R, R)]
        put_windows(tw, i * R, values)
        return s + fold(values)

    gcb2 = total_of(lax.fori_loop(0, H // R, t2_windows, zero8))
    alone(lambda: kernel_grad(a2w, tw, gk2_ref))
    gb2, gg2 = pull(k2_ref, g2p, lambda i: [unit2(ref[...]) for ref in pairs_of(c1, i * Q)])
    mean_du2 = group_sum(gb2 * (1.0 + gain2)) * (1.0 / PER_GROUP)
    mean_duu2 = group_sum(gg2 * (1.0 + gain2)) * (1.0 / PER_GROUP)

    def t1_windows(i, s):
        values = c1[pl.ds(i * R, R)]
        du = g2p[pl.ds(i * R, R)] * one(1.0 + gain2)
        ds = (du - one(mean_du2) - unit2(values) * one(mean_duu2)) * one(rs2)
        put_windows(tw, i * R, ds * one(scale))
        return s[0] + fold(ds * values), s[1] + fold(ds)

    gsc, gsh = lax.fori_loop(0, H // R, t1_windows, (zero8, zero8))
    gsc, gsh = total_of(gsc), total_of(gsh)
    alone(lambda: kernel_grad(a1w, tw, gk1_ref))

    def unit1(ref):
        return (ref[...].astype(f32) - one(mean1)) * one(rs1)

    gb1, gg1 = pull(k1_ref, g1p, lambda i: [unit1(ref) for ref in pairs_of(x_ref, i * Q)])
    mean_du1 = group_sum(gb1 * (1.0 + gain1)) * (1.0 / PER_GROUP)
    mean_duu1 = group_sum(gg1 * (1.0 + gain1)) * (1.0 / PER_GROUP)

    def finish(i, carry):
        du = g1p[pl.ds(i * R, R)] * one(1.0 + gain1)
        unit = unit1(x_ref.at[pl.ds(i * R, R)])
        dx = (du - one(mean_du1) - unit * one(mean_duu1)) * one(rs1)
        dx_ref[pl.ds(i * R, R)] = (drf[pl.ds(i * R, R)] + dx).astype(bf16)
        return carry

    lax.fori_loop(0, H // R, finish, 0)

    rows = [gg1, gb1, gsh * scale, gg2, gb2, gcb2, gdb[:, :C], gdb[:, C:]]
    rows = [row[0:1] for row in rows]
    rows = rows + [jnp.where(mine[:, :C], row[0:1], 0.0) for row in (gsc, gsh)]
    extra = jnp.concatenate(rows, axis=0)
    if not plan.rings:
        results[0][...] = conv[:, 0:KERNEL_ROWS]
        results[1][...] = extra
        return
    keep_ref, send_ref = results
    for place, (core, turn) in enumerate(plan.targets):
        first = plan.tile_of((me ^ turn) * plan.conv_rows)
        block = jnp.concatenate([conv[k, pl.ds(first, plan.conv_pad), :] for k in range(4)], axis=0)
        at = place % plan.half * plan.width
        if core:
            send_ref[at : at + plan.width] = block.astype(bf16)
        else:
            keep_ref[at : at + plan.width] = block
    keep_ref[plan.half * plan.width :] = extra
    send_ref[plan.half * plan.width :] = two_terms(extra)


def two_terms(extra):
    high = extra.astype(bf16)
    return jnp.concatenate([high.astype(f32), extra - high.astype(f32)], axis=0).astype(bf16)


def vmem_specs(count):
    return [pl.BlockSpec(memory_space=pltpu.VMEM)] * count


def limit(size):
    return pltpu.CompilerParams(vmem_limit_bytes=size << 20)


class Plan:
    def __init__(self, sizes, conv_len, dense_len, small_len):
        (_, outer_size), (_, inner_size) = sizes
        count = outer_size * inner_size
        self.sizes, self.line = sizes, inner_size // 2
        self.conv_len, self.dense_len, self.small_len = conv_len, dense_len, small_len
        self.conv_rows, self.dense_rows = conv_len // C, dense_len // C
        powers = all(n & (n - 1) == 0 for _, n in sizes) and inner_size > 1
        self.rings = powers and conv_len % C == 0 and dense_len % C == 0 and small_len <= C
        self.inputs = 2 * outer_size if self.rings else 3
        self.conv_pad = self.padded(self.conv_rows, count)
        self.dense_pad = self.padded(self.dense_rows, count)
        self.dense_at = 4 * self.conv_pad
        self.small_at = self.dense_at + self.dense_pad
        self.own_rows = -(-(self.small_at + 16) // 16) * 16
        turns = [(core, plane * inner_size + 2 * near + core) for core in (0, 1) for plane in range(outer_size) for near in range(self.line)]
        self.targets = turns
        self.sources = [(place % self.line, turn) for place, (_, turn) in enumerate(turns)]
        self.half = count // 2
        self.width = 4 * self.conv_pad

    def padded(self, rows, count):
        return max(-(-(rows * k % 8 + rows) // 8) * 8 for k in range(count))

    def tile_of(self, row):
        return pl.multiple_of(row // 8 * 8, 8)


def run_block(plan, class_ids, x, cot, inputs):
    struct = jax.ShapeDtypeStruct
    shapes = [
        struct((H // 2, W // 2, 2 * C), bf16),
        struct((H, W, C), bf16),
        struct((NCLASS, EMB), bf16),
        struct((EMB, EMB), bf16),
        struct((EMB, 2 * C), bf16),
        struct((NCLASS, EMB), f32),
    ]
    if plan.rings:
        rows = plan.half * plan.width
        shapes += [struct((rows + EXTRA, C), f32), struct((rows + 2 * EXTRA, C), bf16)]
    else:
        shapes += [struct((4, KERNEL_ROWS, C), f32), struct((EXTRA, C), f32)]
    windows = pltpu.VMEM((H + 2, W, 3 * C), bf16)
    plane = pltpu.VMEM((H, W, C), f32)
    return pl.pallas_call(
        functools.partial(block_body, plan),
        out_shape=shapes,
        in_specs=[pl.BlockSpec(memory_space=pltpu.SMEM)] + vmem_specs(2 + len(inputs)),
        out_specs=vmem_specs(8),
        scratch_shapes=[
            windows,
            windows,
            windows,
            pltpu.VMEM((H + 2, W // 2, 3 * C), bf16),
            pltpu.VMEM((H // 2 + 1, W // 2, 4 * C), bf16),
            plane,
            plane,
            plane,
            plane,
            pltpu.VMEM((12 * C, 2 * C), bf16),
            pltpu.VMEM((4, KERNEL_ROWS + 2 * plan.conv_pad, C), f32),
            pltpu.VMEM((MLP_ROWS + 2 * plan.dense_pad, C), f32),
            pltpu.VMEM((4, KERNEL_ROWS, C), bf16),
            pltpu.VMEM((16, C), f32),
        ],
        compiler_params=limit(48),
        name="block",
    )(class_ids, x, cot, *inputs)


def pack_body(plan, conv_ref, dense_ref, small_ref, out_ref, rows):
    me = position_of(plan.sizes)
    rows[...] = jnp.zeros(rows.shape, f32)
    first = me * plan.conv_rows % 8
    for r in range(plan.conv_rows):
        rows[pl.ds(first + r, 4, plan.conv_pad), :] = conv_ref[0, :, r * C : (r + 1) * C]
    first = plan.dense_at + me * plan.dense_rows % 8
    for r in range(plan.dense_rows):
        rows[pl.ds(first + r, 1), :] = dense_ref[0:1, r * C : (r + 1) * C]
    start = me * plan.small_len
    own = jnp.concatenate([small_ref[0:1, :], jnp.zeros((1, C - plan.small_len), f32)], axis=1)
    own = pltpu.roll(jnp.broadcast_to(own, (16, C)), start % C, 1)
    row = lax.broadcasted_iota(jnp.int32, (16, C), 0)
    lane = lax.broadcasted_iota(jnp.int32, (16, C), 1)
    place = row * C + lane
    mine = (place >= start) & (place < start + plan.small_len)
    rows[plan.small_at : plan.small_at + 16] = jnp.where(mine, own, 0.0)
    out_ref[...] = rows[...].astype(bf16)


def run_pack(plan, conv_state, mlp_state, small_state):
    return pl.pallas_call(
        functools.partial(pack_body, plan),
        out_shape=jax.ShapeDtypeStruct((plan.own_rows, C), bf16),
        in_specs=vmem_specs(3),
        out_specs=pl.BlockSpec(memory_space=pltpu.VMEM),
        scratch_shapes=[pltpu.VMEM((plan.own_rows, C), f32)],
        compiler_params=limit(8),
        name="pack",
    )(conv_state, mlp_state, small_state)


def sum_extra(extra, received, at):
    for ref in received:
        extra = extra + ref[at : at + EXTRA].astype(f32) + ref[at + EXTRA : at + 2 * EXTRA].astype(f32)
    return extra


def merge_body(plan, blocks, groups, *refs):
    keep_ref, received = refs[0], refs[1 : len(refs) - groups]
    outs = refs[len(refs) - groups :]
    size = blocks // groups
    for block in range(blocks):
        at = block * plan.width
        total = keep_ref[at : at + plan.width]
        for ref in received:
            total = total + ref[at : at + plan.width].astype(f32)
        group, place = block // size, block % size * plan.width
        outs[group][place : place + plan.width] = total.astype(outs[group].dtype)
    at = blocks * plan.width
    extra = sum_extra(keep_ref[at : at + EXTRA], received, at)
    outs[0][size * plan.width :] = extra
    for ref in outs[1:]:
        ref[size * plan.width :] = two_terms(extra)


def run_merge(plan, blocks, groups, keep, received):
    rows = blocks // groups * plan.width
    shapes = [jax.ShapeDtypeStruct((rows + EXTRA, C), f32)]
    shapes += [jax.ShapeDtypeStruct((rows + 2 * EXTRA, C), bf16)] * (groups - 1)
    return pl.pallas_call(
        functools.partial(merge_body, plan, blocks, groups),
        out_shape=shapes,
        in_specs=vmem_specs(1 + len(received)),
        out_specs=vmem_specs(groups),
        compiler_params=limit(16),
        name="merge",
    )(keep, *received)


def mlp_grads(table, m1_ref, m2_ref, hidden, dss, out_ref):
    prob = normal_cdf(hidden)

    def put(first, values):
        parts = values.shape[1] // C
        for part in range(parts):
            out_ref[pl.ds(first + part, values.shape[0], parts), :] = values[:, part * C : (part + 1) * C]

    def outer(left, right):
        lefts = [a for k, a in enumerate(left) for b in right[: 3 - k]]
        rights = [b for k, a in enumerate(left) for b in right[: 3 - k]]
        return mm(jnp.concatenate(lefts, axis=0), jnp.concatenate(rights, axis=0), TN)

    def back(values, weights):
        return sum(mm(part, weights, NT) for part in three(values))

    dp = back(dss, m2_ref[...]) * gelu_slope(hidden, prob)
    put(0, back(dp, m1_ref[...]))
    put(TABLE_ROWS, outer([table], three(dp)))
    put(TABLE_ROWS + M1_ROWS, outer(three(hidden * prob), three(dss)))
    ge1 = jnp.sum(dp, axis=0, keepdims=True)
    ge2 = jnp.sum(dss, axis=0, keepdims=True)
    return [ge1[:, i * C : (i + 1) * C] for i in range(4)] + [ge2[:, i * C : (i + 1) * C] for i in range(2)]


def mlp_body(table_ref, m1_ref, m2_ref, hidden_ref, dss_ref, out_ref, tail_ref):
    tail = mlp_grads(table_ref[...], m1_ref, m2_ref, hidden_ref[...], dss_ref[...], out_ref)
    for i, row in enumerate(tail):
        tail_ref[i : i + 1, :] = row


def run_mlp(table, m1, m2, hidden, dss):
    return pl.pallas_call(
        mlp_body,
        out_shape=[jax.ShapeDtypeStruct((MLP_ROWS, C), f32), jax.ShapeDtypeStruct((6, C), f32)],
        in_specs=vmem_specs(5),
        out_specs=vmem_specs(2),
        compiler_params=limit(32),
        name="mlp_grad",
    )(table, m1, m2, hidden, dss)


def adam(weight, first, second, average, gradient, rate, decay):
    first = beta_one * first + (1.0 - beta_one) * gradient
    second = beta_two * second + (1.0 - beta_two) * gradient * gradient
    first_hat = first * (1.0 / (1.0 - beta_one**STEP))
    second_hat = second * (1.0 / (1.0 - beta_two**STEP))
    weight = weight - rate * (first_hat / (jnp.sqrt(second_hat) + adam_eps) + decay * weight)
    return weight, first, second, ema_decay * average + (1.0 - ema_decay) * weight


def update_body(plan, received_count, *refs):
    keep_ref, received = refs[0], refs[1 : 1 + received_count]
    table_ref, m1_ref, m2_ref, hidden_ref, conv_ref, dense_ref, small_ref = refs[1 + received_count : 8 + received_count]
    conv_new, dense_new, small_new, conv_copy, dense_copy, small_copy = refs[8 + received_count : 14 + received_count]
    block, grads, rows, smalls = refs[14 + received_count :]
    me = position_of(plan.sizes)
    total = keep_ref[0 : plan.width]
    for ref in received:
        total = total + ref[0 : plan.width].astype(f32)
    block[...] = total
    extra = sum_extra(keep_ref[plan.width : plan.width + EXTRA], received, plan.width)
    smalls[0:8] = extra[0:8]
    dss = jnp.concatenate([extra[8 : 8 + NCLASS], extra[8 + NCLASS :]], axis=1)
    tail = mlp_grads(table_ref[...], m1_ref, m2_ref, hidden_ref[...], dss, grads)
    for i, row in enumerate(tail):
        smalls[8 + i : 9 + i, :] = row

    first = me * plan.conv_rows % 8
    for r in range(plan.conv_rows):
        at = slice(r * C, (r + 1) * C)
        gradient = block[pl.ds(first + r, 4, plan.conv_pad), :]
        new = adam(*[conv_ref[k, :, at] for k in range(4)], gradient, rate_conv, decay_weights)
        for k in range(4):
            conv_new[k, :, at] = new[k]
        conv_copy[:, at] = new[0].astype(bf16)

    start = me * plan.dense_rows
    for r in range(plan.dense_rows):
        at = slice(r * C, (r + 1) * C)
        gradient = grads[pl.ds(start + r, 1), :]
        rate = jnp.where(start + r < TABLE_ROWS, rate_table, rate_dense)
        new = adam(*[dense_ref[k : k + 1, at] for k in range(4)], gradient, rate, decay_weights)
        for k in range(4):
            dense_new[k : k + 1, at] = new[k]
        rows[r : r + 1, :] = new[0]
    dense_copy[...] = rows[...].astype(bf16)

    start = me * plan.small_len
    lane = lax.broadcasted_iota(jnp.int32, (8, C), 1)
    near = jnp.broadcast_to(smalls[pl.ds(start // C, 1), :], (8, C))
    far = jnp.broadcast_to(smalls[pl.ds(start // C + 1, 1), :], (8, C))
    off = C - start % C
    gradient = jnp.where(lane < off, pltpu.roll(near, off, 1), pltpu.roll(far, off, 1))
    gradient = gradient[0:1, 0 : plan.small_len]
    new = adam(*[small_ref[k : k + 1, :] for k in range(4)], gradient, rate_small, 0.0)
    for k in range(4):
        small_new[k : k + 1, :] = new[k]
    small_copy[...] = new[0].astype(bf16)


def run_update(plan, keep, received, mlp, states):
    struct = jax.ShapeDtypeStruct
    shapes = [struct(state.shape, f32) for state in states]
    shapes += [struct((4, plan.conv_len), bf16), struct((plan.dense_rows, C), bf16), struct((1, plan.small_len), bf16)]
    return pl.pallas_call(
        functools.partial(update_body, plan, len(received)),
        out_shape=shapes,
        in_specs=vmem_specs(1 + len(received) + 4 + 3),
        out_specs=vmem_specs(6),
        scratch_shapes=[
            pltpu.VMEM((plan.width, C), f32),
            pltpu.VMEM((MLP_ROWS, C), f32),
            pltpu.VMEM((plan.dense_rows, C), f32),
            pltpu.VMEM((24, C), f32),
        ],
        compiler_params=limit(24),
        name="update",
    )(keep, *received, *mlp, *states)


def swap(values, axis, size, turn):
    return lax.ppermute(values, axis, [(i, i ^ turn) for i in range(size)])


def gather_ring(plan, own):
    (outer, outer_size), (inner, inner_size) = plan.sizes
    line = jnp.stack([own] + [swap(own, inner, inner_size, 2 * k) for k in range(1, plan.line)])
    planes = [line] + [swap(line, outer, outer_size, k) for k in range(1, outer_size)]
    return planes + [swap(plane, inner, inner_size, 1) for plane in planes]


def reduce_ring(plan, keep, send):
    (outer, outer_size), (inner, inner_size) = plan.sizes
    received = [swap(send, inner, inner_size, 1)]
    keep, *sends = run_merge(plan, plan.half, outer_size, keep, received)
    received = [swap(part, outer, outer_size, k + 1) for k, part in enumerate(sends)]
    keep, *sends = run_merge(plan, plan.line, plan.line, keep, received)
    return keep, [swap(part, inner, inner_size, 2 * (k + 1)) for k, part in enumerate(sends)]


def plain_update(plan, position, grads, extra, mlp, states):
    conv_state, mlp_state, small_state = states
    conv_red = lax.psum_scatter(grads.reshape(4, -1), AXES, scatter_dimension=1, tiled=True)
    extra = lax.psum(extra, AXES)
    dss = jnp.concatenate([extra[8 : 8 + NCLASS], extra[8 + NCLASS :]], axis=1)
    dense_grad, tail = run_mlp(*mlp, dss)
    dense_red = lax.dynamic_slice_in_dim(dense_grad.reshape(-1), position * plan.dense_len, plan.dense_len)
    flat = jnp.concatenate([extra[:8], tail]).reshape(-1)
    small_red = lax.dynamic_slice_in_dim(flat, position * plan.small_len, plan.small_len)
    flat_index = position * plan.dense_len + jnp.arange(plan.dense_len, dtype=jnp.int32)
    dense_rate = jnp.where(flat_index < NCLASS * EMB, rate_table, rate_dense)
    new = [
        jnp.stack(adam(*state, red, rate, decay))
        for state, red, rate, decay in (
            (conv_state, conv_red, rate_conv, decay_weights),
            (mlp_state, dense_red, dense_rate, decay_weights),
            (small_state, small_red, rate_small, 0.0),
        )
    ]
    return new + [state[0].astype(bf16) for state in new]


def per_device(sizes, samples, cotangent, class_ids, *states):
    conv_state, mlp_state, small_state = states
    plan = Plan(sizes, conv_state.shape[2], mlp_state.shape[1], small_state.shape[1])
    if plan.rings:
        inputs = gather_ring(plan, run_pack(plan, *states))
    else:
        conv, dense, small = [state[0].astype(bf16) for state in states]
        inputs = [
            lax.all_gather(conv, AXES, axis=1, tiled=True).reshape(4, KERNEL_ROWS, C),
            lax.all_gather(dense, AXES, axis=0, tiled=True).reshape(MLP_ROWS, C),
            lax.all_gather(small, AXES, axis=0, tiled=True).reshape(-1, C),
        ]
    out, dx, table, m1, m2, hidden, first, second = run_block(
        plan, class_ids, samples[0], cotangent[0], inputs
    )
    mlp = (table, m1, m2, hidden)
    if plan.rings:
        keep, received = reduce_ring(plan, first, second)
        results = run_update(plan, keep, received, mlp, states)
    else:
        results = plain_update(plan, lax.axis_index(AXES), first, second, mlp, states)
    conv_new, mlp_new, small_new, conv_copy, mlp_copy, small_copy = results
    return out[None], dx[None], conv_new, mlp_new, small_new, conv_copy, mlp_copy.reshape(-1), small_copy.reshape(-1)


def solution(mesh):
    sizes = tuple((axis, mesh.shape[axis]) for axis in AXES)

    def body(*args):
        return per_device(sizes, *args)

    return jax.shard_map(
        body,
        mesh=mesh,
        in_specs=(
            P(AXES, None, None, None),
            P(AXES, None, None, None),
            P(AXES),
            P(None, None, AXES),
            P(None, AXES),
            P(None, AXES),
        ),
        out_specs=(
            P(AXES, None, None, None),
            P(AXES, None, None, None),
            P(None, None, AXES),
            P(None, AXES),
            P(None, AXES),
            P(None, AXES),
            P(AXES),
            P(AXES),
        ),
        check_vma=False,
    )
```

```python
import functools

import jax
import jax.numpy as jnp
from jax import lax
from jax.experimental import pallas as pl
from jax.experimental.pallas import tpu as pltpu
from jax.sharding import PartitionSpec as P

C = 128
EMB = 512
GROUPS = 8
H = 64
W = 64
NCLASS = 16
STEP = 10
TAPS = 9
CELLS = H * W
PER_GROUP = CELLS * (C // GROUPS)
TABLE_ROWS = NCLASS * EMB // C
M1_ROWS = EMB * EMB // C
M2_ROWS = EMB * 2
MLP_ROWS = TABLE_ROWS + M1_ROWS + M2_ROWS
KERNEL_ROWS = TAPS * C
AXES = ("dp", "fsdp")

beta_one = 0.9
beta_two = 0.999
adam_eps = 1e-08
ema_decay = 0.99
norm_eps = 1e-05
rate_conv = 0.08
rate_table = 0.6
rate_dense = 0.1
rate_small = 0.15
decay_weights = 0.01

f32 = jnp.float32
bf16 = jnp.bfloat16
NN = (((1,), (0,)), ((), ()))
NT = (((1,), (1,)), ((), ()))
TN = (((0,), (0,)), ((), ()))
EXTRA = 8 + 2 * NCLASS
R = 8
Q = 8


def mm(a, b, dims=NN):
    return lax.dot_general(a, b, dims, preferred_element_type=f32)


def three(v):
    high = v.astype(bf16)
    rest = v - high.astype(f32)
    mid = rest.astype(bf16)
    return high, mid, (rest - mid.astype(f32)).astype(bf16)


def group_sum(rows):
    lane = lax.broadcasted_iota(jnp.int32, rows.shape, 1)
    for step in (1, 2, 4, 8):
        up = pltpu.roll(rows, C - step, 1)
        down = pltpu.roll(rows, step, 1)
        rows = rows + jnp.where((lane & step) == 0, up, down)
    return rows


def fold(values):
    return jnp.sum(values.reshape(-1, 8, values.shape[-1]), axis=0)


def total_of(partial):
    return jnp.broadcast_to(jnp.sum(partial, axis=0, keepdims=True), partial.shape)


def one(rows):
    return rows[0:1].reshape(1, 1, C)


def normal_cdf(v):
    return 0.5 * (1.0 + lax.erf(v * 0.7071067811865476))


def gelu_slope(v, prob):
    return prob + v * (jnp.exp(-0.5 * v * v) * 0.3989422804014327)


def put_windows(win_ref, row, values):
    rows = values.shape[0]
    place = lax.broadcasted_iota(jnp.int32, values.shape, 1)
    left = jnp.where(place == 0, 0.0, pltpu.roll(values, 1, 1))
    right = jnp.where(place == W - 1, 0.0, pltpu.roll(values, W - 1, 1))
    win_ref[pl.ds(row + 1, rows), :, 0:C] = left.astype(bf16)
    win_ref[pl.ds(row + 1, rows), :, C : 2 * C] = values.astype(bf16)
    win_ref[pl.ds(row + 1, rows), :, 2 * C : 3 * C] = right.astype(bf16)


def clear_edges(win_ref):
    edge = jnp.zeros((1,) + tuple(win_ref.shape[1:]), win_ref.dtype)
    win_ref[0:1] = edge
    win_ref[H + 1 : H + 2] = edge


def pair_forward(pair_ref, kernel_ref):
    zero = jnp.zeros((3 * C, C), bf16)
    pair_ref[0 : TAPS * C, 0:C] = kernel_ref[...]
    pair_ref[TAPS * C :, 0:C] = zero
    pair_ref[0 : 3 * C, C:] = zero
    pair_ref[3 * C :, C:] = kernel_ref[...]


def flip(block):
    return jnp.transpose(block.astype(f32)).astype(bf16)


def pair_backward(pair_ref, kernel_ref):
    zero = jnp.zeros((3 * C, C), bf16)
    pair_ref[TAPS * C :, 0:C] = zero
    pair_ref[0 : 3 * C, C:] = zero
    for tap in range(TAPS):
        block = flip(kernel_ref[(TAPS - 1 - tap) * C : (TAPS - tap) * C, :])
        pair_ref[tap * C : (tap + 1) * C, 0:C] = block
        pair_ref[(tap + 3) * C : (tap + 4) * C, C:] = block


def pair_conv(win_ref, pair_ref, first):
    view = win_ref.reshape(H // 2 + 1, 2, W, 3 * C)
    taken = [view[pl.ds(first + t // 2, Q), t % 2] for t in range(4)]
    stacked = jnp.concatenate(taken, axis=-1).reshape(Q * W, 12 * C)
    return mm(stacked, pair_ref[...]).reshape(Q, W, 2 * C)


def pairs_of(ref, first):
    view = ref.reshape(H // 2, 2, W, C)
    return [view.at[pl.ds(first, Q), parity] for parity in range(2)]


def kernel_grad(act_ref, win_ref, out_ref):
    left = act_ref[1 : H + 1, :, C : 2 * C].reshape(CELLS, C)
    right = jnp.concatenate([win_ref[t : t + H] for t in range(3)], axis=-1)
    got = mm(left, right.reshape(CELLS, TAPS * C), TN)
    for t in range(TAPS):
        out_ref[t * C : (t + 1) * C, :] = got[:, (TAPS - 1 - t) * C : (TAPS - t) * C]


def position_of(sizes):
    (outer, _), (inner, inner_size) = sizes
    return lax.axis_index(outer) * inner_size + lax.axis_index(inner)


def prepare_body(x_ref, cot_ref, stats_ref, cw, gdb_ref):
    zero8 = jnp.zeros((8, C), f32)

    def read_x(i):
        return x_ref[pl.ds(i * R, R)].astype(f32)

    total = lax.fori_loop(0, H // R, lambda i, s: s + fold(read_x(i)), zero8)
    mean = group_sum(total_of(total)) * (1.0 / PER_GROUP)

    def square_x(i, s):
        d = read_x(i) - one(mean)
        return s + fold(d * d)

    var = group_sum(total_of(lax.fori_loop(0, H // R, square_x, zero8))) * (1.0 / PER_GROUP)
    stats_ref[0:8] = mean
    stats_ref[8:16] = lax.rsqrt(var + norm_eps)
    cw[H // 2 : H // 2 + 1] = jnp.zeros((1, W // 2, 4 * C), bf16)

    def cot_windows(i, s):
        values = cot_ref[pl.ds(i * Q, Q)].astype(f32)
        place = lax.broadcasted_iota(jnp.int32, values.shape, 1)
        after = jnp.where(place == W // 2 - 1, 0.0, pltpu.roll(values, W // 2 - 1, 1))
        cw[pl.ds(i * Q, Q), :, 0 : 2 * C] = values.astype(bf16)
        cw[pl.ds(i * Q, Q), :, 2 * C :] = after.astype(bf16)
        return s + fold(values)

    gdb_ref[...] = total_of(lax.fori_loop(0, H // 2 // Q, cot_windows, jnp.zeros((8, 2 * C), f32)))


def run_prepare(x, cot):
    struct = jax.ShapeDtypeStruct
    return pl.pallas_call(
        prepare_body,
        out_shape=[struct((16, C), f32), struct((H // 2 + 1, W // 2, 4 * C), bf16), struct((8, 2 * C), f32)],
        in_specs=vmem_specs(2),
        out_specs=vmem_specs(3),
        compiler_params=limit(8),
        cost_estimate=cost(2, 3 << 20),
        name="prepare",
    )(x, cot)


def front_body(plan, *refs):
    count = plan.parts if plan.rings else 2
    x_ref, stats_ref = refs[:2]
    inputs = refs[2 : 2 + count]
    a1w, g1p, c1, moments_ref, k1_ref, smalls, conv, pair = refs[2 + count :]
    if plan.rings:
        me = position_of(plan.sizes)
        conv[...] = jnp.zeros(conv.shape, f32)
        small = jnp.zeros((16, C), f32)
        row = lax.broadcasted_iota(jnp.int32, (16, C), 0)
        lane = lax.broadcasted_iota(jnp.int32, (16, C), 1)
        for part, place, turn in plan.sources:
            owner = me ^ turn
            values = inputs[part][place, 0 : plan.first_rows].astype(f32)
            first = plan.tile_of(owner * plan.conv_rows)
            conv[pl.ds(first, plan.conv_pad), :] += values[: plan.conv_pad]
            at = row * C + lane - owner * plan.small_len
            own = jnp.broadcast_to(values[plan.conv_pad : plan.conv_pad + 1], (16, C))
            small = jnp.where((at >= 0) & (at < plan.small_len), own, small)
        smalls[...] = small
        k1_ref[...] = conv[0:KERNEL_ROWS].astype(bf16)
    else:
        k1_ref[...] = inputs[0][...]
        smalls[0:14] = inputs[1][...].astype(f32)
    gain1, bias1, cb1 = [jnp.broadcast_to(smalls[i : i + 1, :], (8, C)) for i in range(3)]
    mean1 = stats_ref[0:8]
    slope1 = stats_ref[8:16] * (1.0 + gain1)
    zero8 = jnp.zeros((8, C), f32)
    clear_edges(a1w)

    def front1(i, carry):
        v = (x_ref[pl.ds(i * R, R)].astype(f32) - one(mean1)) * one(slope1) + one(bias1)
        prob = normal_cdf(v)
        put_windows(a1w, i * R, v * prob)
        g1p[pl.ds(i * R, R)] = gelu_slope(v, prob)
        return carry

    lax.fori_loop(0, H // R, front1, 0)
    pair_forward(pair, k1_ref)

    def conv1(i, s):
        got = pair_conv(a1w, pair, i * Q)
        for parity, place in enumerate(pairs_of(c1, i * Q)):
            value = got[..., parity * C : (parity + 1) * C] + one(cb1)
            place[...] = value
            s = s + fold(value)
        return s

    centre = total_of(lax.fori_loop(0, H // 2 // Q, conv1, zero8)) * (1.0 / CELLS)

    def square_c(i, s):
        d = c1[pl.ds(i * R, R)] - one(centre)
        return s + fold(d * d)

    moments_ref[0:8] = centre
    moments_ref[8:16] = total_of(lax.fori_loop(0, H // R, square_c, zero8)) * (1.0 / CELLS)


def run_front(plan, x, stats, inputs):
    struct = jax.ShapeDtypeStruct
    return pl.pallas_call(
        functools.partial(front_body, plan),
        out_shape=[
            struct((H + 2, W, 3 * C), bf16),
            struct((H, W, C), f32),
            struct((H, W, C), f32),
            struct((16, C), f32),
            struct((KERNEL_ROWS, C), bf16),
            struct((16, C), f32),
        ],
        in_specs=vmem_specs(2 + len(inputs)),
        out_specs=vmem_specs(6),
        scratch_shapes=[
            pltpu.VMEM((KERNEL_ROWS + 2 * plan.conv_pad, C), f32),
            pltpu.VMEM((12 * C, 2 * C), bf16),
        ],
        compiler_params=limit(20),
        cost_estimate=cost(1300, 8 << 20),
        name="front",
    )(x, stats, *inputs)


def block_body(plan, *refs):
    refs = list(refs)
    cls_ref, x_ref, cot_ref, stats_ref, cw, gdb_ref, a1w, g1p, c1, moments_ref, k1_ref, smalls = refs[:12]
    count = plan.parts if plan.rings else 2
    inputs = refs[12 : 12 + count]
    out_hbm, dx_hbm, table_ref, m1_ref, m2_ref, hidden_ref = refs[12 + count : 18 + count]
    results = refs[18 + count : 20 + count]
    a2w, tw, rw, g2p, drf, pair, conv, dense, kernels, out_ref, dx_ref, out_sem, dx_sem = refs[20 + count :]
    me = position_of(plan.sizes)
    if plan.rings:
        conv[1:4] = jnp.zeros((3,) + conv.shape[1:], f32)
        dense[...] = jnp.zeros(dense.shape, f32)
        for part, place, turn in plan.sources:
            owner = me ^ turn
            values = inputs[part][place, plan.first_rows : plan.own_rows].astype(f32)
            first = plan.tile_of(owner * plan.conv_rows)
            for k in range(3):
                conv[k + 1, pl.ds(first, plan.conv_pad), :] += values[k * plan.conv_pad : (k + 1) * plan.conv_pad]
            first = plan.tile_of(owner * plan.dense_rows)
            dense[pl.ds(first, plan.dense_pad), :] += values[plan.dense_at : plan.dense_at + plan.dense_pad]
        kernels[...] = conv[1:4, 0:KERNEL_ROWS].astype(bf16)
    else:
        kernels[...] = inputs[0][...]
        dense[0:MLP_ROWS] = inputs[1][...].astype(f32)

    def lanes(first, rows, parts):
        pieces = [dense[pl.ds(first + part, rows, parts), :] for part in range(parts)]
        return jnp.concatenate(pieces, axis=1).astype(bf16)

    table_ref[...] = lanes(0, NCLASS, EMB // C)
    m1_ref[...] = lanes(TABLE_ROWS, EMB, EMB // C)
    m2_ref[...] = lanes(TABLE_ROWS + M1_ROWS, EMB, 2)
    k2_ref, kd0_ref, kd1_ref = [kernels.at[k] for k in range(3)]
    gk1_ref, gk2_ref, gkd0_ref, gkd1_ref = [conv.at[k] for k in range(4)]

    def small_row(index):
        return jnp.broadcast_to(smalls[index : index + 1, :], (8, C))

    def small_run(first, count):
        return jnp.concatenate([smalls[first + i : first + i + 1, :] for i in range(count)], axis=1)

    def alone(step):
        pl.when(me >= 0)(step)

    gain1, _, _, gain2, bias2, cb2 = [small_row(i) for i in range(6)]
    zero8 = jnp.zeros((8, C), f32)

    hidden = mm(table_ref[...], m1_ref[...]) + small_run(8, 4)
    hidden_ref[...] = hidden
    act = hidden * normal_cdf(hidden)
    ss = sum(mm(part, m2_ref[...]) for part in three(act)) + small_run(12, 2)
    mine = lax.broadcasted_iota(jnp.int32, (NCLASS, 2 * C), 0) == cls_ref[0]
    chosen = jnp.sum(jnp.where(mine, ss, 0.0), axis=0, keepdims=True)
    scale = jnp.broadcast_to(1.0 + chosen[:, :C], (8, C))
    shift = jnp.broadcast_to(chosen[:, C:], (8, C))

    mean1, rs1 = stats_ref[0:8], stats_ref[8:16]
    centre, spread = moments_ref[0:8], moments_ref[8:16]

    centre_s = centre * scale + shift
    mean2 = group_sum(centre_s) * (GROUPS / C)
    off = centre_s - mean2
    var2 = group_sum(spread * scale * scale + off * off) * (GROUPS / C)
    rs2 = lax.rsqrt(var2 + norm_eps)

    def unit2(values):
        return (values * one(scale) + one(shift - mean2)) * one(rs2)

    clear_edges(a2w)

    def front2(i, carry):
        v = unit2(c1[pl.ds(i * R, R)]) * one(1.0 + gain2) + one(bias2)
        prob = normal_cdf(v)
        put_windows(a2w, i * R, v * prob)
        g2p[pl.ds(i * R, R)] = gelu_slope(v, prob)
        return carry

    lax.fori_loop(0, H // R, front2, 0)

    pair_forward(pair, k2_ref)

    def conv2(i, carry):
        got = pair_conv(a2w, pair, i * Q)
        for parity, (place, source) in enumerate(zip(pairs_of(drf, i * Q), pairs_of(x_ref, i * Q))):
            r = source[...].astype(f32) + (got[..., parity * C : (parity + 1) * C] + one(cb2))
            place[...] = r.astype(bf16).astype(f32)
        return carry

    lax.fori_loop(0, H // 2 // Q, conv2, 0)
    rw[0:1] = jnp.zeros((1, W // 2, 3 * C), bf16)

    def split(i, carry):
        even = drf[pl.ds(i * R, R), pl.ds(0, W // 2, 2), :]
        odd = drf[pl.ds(i * R, R), pl.ds(1, W // 2, 2), :]
        place = lax.broadcasted_iota(jnp.int32, odd.shape, 1)
        before = jnp.where(place == 0, 0.0, pltpu.roll(odd, 1, 1))
        rw[pl.ds(i * R + 1, R), :, 0:C] = before.astype(bf16)
        rw[pl.ds(i * R + 1, R), :, C : 2 * C] = even.astype(bf16)
        rw[pl.ds(i * R + 1, R), :, 2 * C :] = odd.astype(bf16)
        return carry

    lax.fori_loop(0, H // R, split, 0)

    def down_rows(first, rows):
        view = rw.reshape(H // 2 + 1, 2, W // 2, 3 * C)
        taken = [view[pl.ds(first + t // 2, rows), t % 2] for t in range(3)]
        return jnp.concatenate(taken, axis=-1).reshape(rows * W // 2, TAPS * C)

    kd = jnp.concatenate([kd0_ref[...], kd1_ref[...]], axis=1)
    bias_down = small_run(6, 2)

    def down(i, carry):
        got = mm(down_rows(i * Q, Q), kd) + bias_down
        out_ref[pl.ds(i * Q, Q)] = got.reshape(Q, W // 2, 2 * C).astype(bf16)
        return carry

    lax.fori_loop(0, H // 2 // Q, down, 0)
    out_copy = pltpu.make_async_copy(out_ref, out_hbm, out_sem)
    out_copy.start()
    @alone
    def _():
        gkd = mm(down_rows(0, H // 2), cot_ref[...].reshape(CELLS // 4, 2 * C), TN)
        gkd0_ref[0:KERNEL_ROWS] = gkd[:, :C]
        gkd1_ref[0:KERNEL_ROWS] = gkd[:, C:]


    gdb = gdb_ref[...]

    def tap(i, j):
        return flip(kd[(3 * i + j) * C : (3 * i + j + 1) * C, :])

    none = jnp.zeros((2 * C, C), bf16)
    even_rows = jnp.concatenate([
        jnp.concatenate([tap(1, 1), none], axis=0),
        jnp.concatenate([tap(1, 2), tap(1, 0)], axis=0),
    ], axis=1)
    odd_rows = jnp.concatenate([
        jnp.concatenate([tap(2, 1), none, tap(0, 1), none], axis=0),
        jnp.concatenate([tap(2, 2), tap(2, 0), tap(0, 2), tap(0, 0)], axis=0),
    ], axis=1)

    def back_down(i, s):
        rows = jnp.concatenate([cw[pl.ds(i * Q, Q)], cw[pl.ds(i * Q + 1, Q)]], axis=-1)
        rows = rows.reshape(Q * W // 2, 8 * C)
        view = drf.reshape(H // 2, 2, W, C)
        for parity, got in enumerate((mm(rows[:, : 4 * C], even_rows), mm(rows, odd_rows))):
            got = got.reshape(Q, W // 2, 2 * C)
            view[pl.ds(i * Q, Q), parity, pl.ds(0, W // 2, 2), :] = got[..., :C]
            view[pl.ds(i * Q, Q), parity, pl.ds(1, W // 2, 2), :] = got[..., C:]
        return s

    lax.fori_loop(0, H // 2 // Q, back_down, 0)

    def pull(kernel_ref, slope_ref, units):
        pair_backward(pair, kernel_ref)

        def step(i, s):
            got = pair_conv(tw, pair, i * Q)
            for parity, (place, unit) in enumerate(zip(pairs_of(slope_ref, i * Q), units(i))):
                dn = got[..., parity * C : (parity + 1) * C] * place[...]
                place[...] = dn
                s = s[0] + fold(dn), s[1] + fold(dn * unit)
            return s

        got = lax.fori_loop(0, H // 2 // Q, step, (zero8, zero8))
        return total_of(got[0]), total_of(got[1])

    clear_edges(tw)

    def t2_windows(i, s):
        values = drf[pl.ds(i * R, R)]
        put_windows(tw, i * R, values)
        return s + fold(values)

    gcb2 = total_of(lax.fori_loop(0, H // R, t2_windows, zero8))
    alone(lambda: kernel_grad(a2w, tw, gk2_ref))
    gb2, gg2 = pull(k2_ref, g2p, lambda i: [unit2(ref[...]) for ref in pairs_of(c1, i * Q)])
    mean_du2 = group_sum(gb2 * (1.0 + gain2)) * (1.0 / PER_GROUP)
    mean_duu2 = group_sum(gg2 * (1.0 + gain2)) * (1.0 / PER_GROUP)

    def t1_windows(i, s):
        values = c1[pl.ds(i * R, R)]
        du = g2p[pl.ds(i * R, R)] * one(1.0 + gain2)
        ds = (du - one(mean_du2) - unit2(values) * one(mean_duu2)) * one(rs2)
        put_windows(tw, i * R, ds * one(scale))
        return s[0] + fold(ds * values), s[1] + fold(ds)

    gsc, gsh = lax.fori_loop(0, H // R, t1_windows, (zero8, zero8))
    gsc, gsh = total_of(gsc), total_of(gsh)
    alone(lambda: kernel_grad(a1w, tw, gk1_ref))

    def unit1(ref):
        return (ref[...].astype(f32) - one(mean1)) * one(rs1)

    gb1, gg1 = pull(k1_ref, g1p, lambda i: [unit1(ref) for ref in pairs_of(x_ref, i * Q)])
    mean_du1 = group_sum(gb1 * (1.0 + gain1)) * (1.0 / PER_GROUP)
    mean_duu1 = group_sum(gg1 * (1.0 + gain1)) * (1.0 / PER_GROUP)

    def finish(i, carry):
        du = g1p[pl.ds(i * R, R)] * one(1.0 + gain1)
        unit = unit1(x_ref.at[pl.ds(i * R, R)])
        dx = (du - one(mean_du1) - unit * one(mean_duu1)) * one(rs1)
        dx_ref[pl.ds(i * R, R)] = (drf[pl.ds(i * R, R)] + dx).astype(bf16)
        return carry

    dx_copies = []
    for part in range(4):
        lax.fori_loop(part * H // R // 4, (part + 1) * H // R // 4, finish, 0)
        rows = pl.ds(part * H // 4, H // 4)
        dx_copies.append(pltpu.make_async_copy(dx_ref.at[rows], dx_hbm.at[rows], dx_sem.at[part]))
        dx_copies[-1].start()

    rows = [gg1, gb1, gsh * scale, gg2, gb2, gcb2, gdb[:, :C], gdb[:, C:]]
    rows = [row[0:1] for row in rows]
    rows = rows + [jnp.where(mine[:, :C], row[0:1], 0.0) for row in (gsc, gsh)]
    extra = jnp.concatenate(rows, axis=0)
    if plan.rings:
        put_results(plan, me, conv, extra, *results)
    else:
        results[0][...] = conv[:, 0:KERNEL_ROWS]
        results[1][...] = extra
    out_copy.wait()
    for copy in dx_copies:
        copy.wait()


def put_results(plan, me, conv, extra, keep_ref, send_ref):
    for place, (core, turn) in enumerate(plan.targets):
        first = plan.tile_of((me ^ turn) * plan.conv_rows)
        block = jnp.concatenate([conv[k, pl.ds(first, plan.conv_pad), :] for k in range(4)], axis=0)
        at = place % plan.half * plan.width
        if core:
            send_ref[at : at + plan.width] = block.astype(bf16)
        else:
            keep_ref[at : at + plan.width] = block
    keep_ref[plan.half * plan.width :] = extra
    send_ref[plan.half * plan.width :] = two_terms(extra)


def two_terms(extra):
    high = extra.astype(bf16)
    return jnp.concatenate([high.astype(f32), extra - high.astype(f32)], axis=0).astype(bf16)


def vmem_specs(count):
    return [pl.BlockSpec(memory_space=pltpu.VMEM)] * count


def cost(mflops, moved):
    return pl.CostEstimate(flops=mflops << 20, bytes_accessed=moved, transcendentals=0)


def limit(size):
    return pltpu.CompilerParams(vmem_limit_bytes=size << 20)


class Plan:
    def __init__(self, sizes, conv_len, dense_len, small_len):
        (_, outer_size), (_, inner_size) = sizes
        count = outer_size * inner_size
        self.sizes, self.line = sizes, inner_size // 2
        self.conv_len, self.dense_len, self.small_len = conv_len, dense_len, small_len
        self.conv_rows, self.dense_rows = conv_len // C, dense_len // C
        powers = inner_size & (inner_size - 1) == 0 and inner_size >= 4 and outer_size == 4
        self.rings = powers and conv_len % C == 0 and dense_len % C == 0 and small_len <= C
        self.conv_pad = self.padded(self.conv_rows, count)
        self.dense_pad = self.padded(self.dense_rows, count)
        self.first_rows = -(-(self.conv_pad + 8) // 16) * 16
        self.dense_at = 3 * self.conv_pad
        self.own_rows = self.first_rows + -(-(self.dense_at + self.dense_pad) // 16) * 16
        near = [2 * k for k in range(self.line)]
        half = self.line // 2
        held = [
            [k ^ turn for turn in (0, inner_size) for k in near[:half]],
            [k ^ turn for turn in (0, 2 * inner_size) for k in near[half:]],
        ]
        held += [[k ^ 2 * inner_size for k in held[0]], [k ^ inner_size for k in held[1]]]
        held += [[k ^ 1 for k in part] for part in held]
        self.parts = len(held)
        self.sources = [(part, place, turn) for part, turns in enumerate(held) for place, turn in enumerate(turns)]
        self.targets = [
            (core, plane * inner_size + k + core) for core in (0, 1) for plane in range(outer_size) for k in near
        ]
        self.half = count // 2
        self.width = 4 * self.conv_pad

    def padded(self, rows, count):
        return max(-(-(rows * k % 8 + rows) // 8) * 8 for k in range(count))

    def tile_of(self, row):
        return pl.multiple_of(row // 8 * 8, 8)


def run_block(plan, class_ids, x, cot, prepared, fronted, inputs):
    struct = jax.ShapeDtypeStruct
    shapes = [
        struct((H // 2, W // 2, 2 * C), bf16),
        struct((H, W, C), bf16),
        struct((NCLASS, EMB), bf16),
        struct((EMB, EMB), bf16),
        struct((EMB, 2 * C), bf16),
        struct((NCLASS, EMB), f32),
    ]
    if plan.rings:
        rows = plan.half * plan.width
        shapes += [struct((rows + EXTRA, C), f32), struct((rows + 2 * EXTRA, C), bf16)]
    else:
        shapes += [struct((4, KERNEL_ROWS, C), f32), struct((EXTRA, C), f32)]
    windows = pltpu.VMEM((H + 2, W, 3 * C), bf16)
    plane = pltpu.VMEM((H, W, C), f32)
    return pl.pallas_call(
        functools.partial(block_body, plan),
        out_shape=shapes,
        in_specs=[pl.BlockSpec(memory_space=pltpu.SMEM)] + vmem_specs(11 + len(inputs)),
        out_specs=[pl.BlockSpec(memory_space=pltpu.HBM)] * 2 + vmem_specs(6),
        scratch_shapes=[
            windows,
            windows,
            pltpu.VMEM((H + 2, W // 2, 3 * C), bf16),
            plane,
            plane,
            pltpu.VMEM((12 * C, 2 * C), bf16),
            pltpu.VMEM((4, KERNEL_ROWS + 2 * plan.conv_pad, C), f32),
            pltpu.VMEM((MLP_ROWS + 2 * plan.dense_pad, C), f32),
            pltpu.VMEM((3, KERNEL_ROWS, C), bf16),
            pltpu.VMEM((H // 2, W // 2, 2 * C), bf16),
            pltpu.VMEM((H, W, C), bf16),
            pltpu.SemaphoreType.DMA,
            pltpu.SemaphoreType.DMA((4,)),
        ],
        compiler_params=limit(36),
        cost_estimate=cost(9000, 16 << 20),
        name="block",
    )(class_ids, x, cot, *prepared, *fronted, *inputs)


def pack_body(plan, conv_hbm, dense_hbm, small_hbm, out_ref, conv_ref, dense_ref, small_ref, rows, sems):
    pairs = ((conv_hbm.at[0], conv_ref), (dense_hbm, dense_ref), (small_hbm, small_ref))
    copies = [pltpu.make_async_copy(source, target, sems.at[k]) for k, (source, target) in enumerate(pairs)]
    for copy in copies:
        copy.start()
    me = position_of(plan.sizes)
    rows[...] = jnp.zeros(rows.shape, f32)
    starts = [0] + [plan.first_rows + k * plan.conv_pad for k in range(3)]
    first = me * plan.conv_rows % 8
    copies[0].wait()
    for r in range(plan.conv_rows):
        for k in range(4):
            rows[pl.ds(starts[k] + first + r, 1), :] = conv_ref[k : k + 1, r * C : (r + 1) * C]
    copies[1].wait()
    first = plan.first_rows + plan.dense_at + me * plan.dense_rows % 8
    for r in range(plan.dense_rows):
        rows[pl.ds(first + r, 1), :] = dense_ref[0:1, r * C : (r + 1) * C]
    copies[2].wait()
    own = jnp.concatenate([small_ref[0:1, :], jnp.zeros((1, C - plan.small_len), f32)], axis=1)
    own = pltpu.roll(jnp.broadcast_to(own, (8, C)), me * plan.small_len % C, 1)
    rows[plan.conv_pad : plan.conv_pad + 1] = own[0:1]
    out_ref[...] = rows[...].astype(bf16)


def run_pack(plan, conv_state, mlp_state, small_state):
    return pl.pallas_call(
        functools.partial(pack_body, plan),
        out_shape=jax.ShapeDtypeStruct((plan.own_rows, C), bf16),
        in_specs=[pl.BlockSpec(memory_space=pltpu.HBM)] * 3,
        out_specs=pl.BlockSpec(memory_space=pltpu.VMEM),
        scratch_shapes=[
            pltpu.VMEM((4, plan.conv_len), f32),
            pltpu.VMEM((4, plan.dense_len), f32),
            pltpu.VMEM((4, plan.small_len), f32),
            pltpu.VMEM((plan.own_rows, C), f32),
            pltpu.SemaphoreType.DMA((3,)),
        ],
        compiler_params=pltpu.CompilerParams(vmem_limit_bytes=(64 << 20) - (160 << 10)),
        name="pack",
    )(conv_state, mlp_state, small_state)


def sum_extra(extra, received, at):
    for ref in received:
        extra = extra + ref[at : at + EXTRA].astype(f32) + ref[at + EXTRA : at + 2 * EXTRA].astype(f32)
    return extra


def merge_body(plan, blocks, groups, *refs):
    keep_ref, received = refs[0], refs[1 : len(refs) - groups]
    outs = refs[len(refs) - groups :]
    size = blocks // groups
    for block in range(blocks):
        at = block * plan.width
        total = keep_ref[at : at + plan.width]
        for ref in received:
            total = total + ref[at : at + plan.width].astype(f32)
        group, place = block // size, block % size * plan.width
        outs[group][place : place + plan.width] = total.astype(outs[group].dtype)
    at = blocks * plan.width
    extra = sum_extra(keep_ref[at : at + EXTRA], received, at)
    outs[0][size * plan.width :] = extra
    for ref in outs[1:]:
        ref[size * plan.width :] = two_terms(extra)


def run_merge(plan, blocks, groups, keep, received):
    rows = blocks // groups * plan.width
    shapes = [jax.ShapeDtypeStruct((rows + EXTRA, C), f32)]
    shapes += [jax.ShapeDtypeStruct((rows + 2 * EXTRA, C), bf16)] * (groups - 1)
    return pl.pallas_call(
        functools.partial(merge_body, plan, blocks, groups),
        out_shape=shapes,
        in_specs=vmem_specs(1 + len(received)),
        out_specs=vmem_specs(groups),
        compiler_params=limit(16),
        name="merge",
    )(keep, *received)


def mlp_grads(table, m1_ref, m2_ref, hidden, dss, out_ref):
    prob = normal_cdf(hidden)

    def put(first, values):
        parts = values.shape[1] // C
        for part in range(parts):
            out_ref[pl.ds(first + part, values.shape[0], parts), :] = values[:, part * C : (part + 1) * C]

    def outer(left, right):
        lefts = [a for k, a in enumerate(left) for b in right[: 3 - k]]
        rights = [b for k, a in enumerate(left) for b in right[: 3 - k]]
        return mm(jnp.concatenate(lefts, axis=0), jnp.concatenate(rights, axis=0), TN)

    def back(values, weights):
        return sum(mm(part, weights, NT) for part in three(values))

    dp = back(dss, m2_ref[...]) * gelu_slope(hidden, prob)
    put(0, back(dp, m1_ref[...]))
    put(TABLE_ROWS, outer([table], three(dp)))
    put(TABLE_ROWS + M1_ROWS, outer(three(hidden * prob), three(dss)))
    ge1 = jnp.sum(dp, axis=0, keepdims=True)
    ge2 = jnp.sum(dss, axis=0, keepdims=True)
    return [ge1[:, i * C : (i + 1) * C] for i in range(4)] + [ge2[:, i * C : (i + 1) * C] for i in range(2)]


def mlp_body(table_ref, m1_ref, m2_ref, hidden_ref, dss_ref, out_ref, tail_ref):
    tail = mlp_grads(table_ref[...], m1_ref, m2_ref, hidden_ref[...], dss_ref[...], out_ref)
    for i, row in enumerate(tail):
        tail_ref[i : i + 1, :] = row


def run_mlp(table, m1, m2, hidden, dss):
    return pl.pallas_call(
        mlp_body,
        out_shape=[jax.ShapeDtypeStruct((MLP_ROWS, C), f32), jax.ShapeDtypeStruct((6, C), f32)],
        in_specs=vmem_specs(5),
        out_specs=vmem_specs(2),
        compiler_params=limit(32),
        name="mlp_grad",
    )(table, m1, m2, hidden, dss)


def adam(weight, first, second, average, gradient, rate, decay):
    first = beta_one * first + (1.0 - beta_one) * gradient
    second = beta_two * second + (1.0 - beta_two) * gradient * gradient
    first_hat = first * (1.0 / (1.0 - beta_one**STEP))
    second_hat = second * (1.0 / (1.0 - beta_two**STEP))
    weight = weight - rate * (first_hat / (jnp.sqrt(second_hat) + adam_eps) + decay * weight)
    return weight, first, second, ema_decay * average + (1.0 - ema_decay) * weight


def update_body(plan, received_count, *refs):
    keep_ref, received = refs[0], refs[1 : 1 + received_count]
    table_ref, m1_ref, m2_ref, hidden_ref, conv_ref, dense_ref, small_ref = refs[1 + received_count : 8 + received_count]
    conv_new, dense_new, small_new, conv_copy, dense_copy, small_copy = refs[8 + received_count : 14 + received_count]
    block, grads, rows, smalls = refs[14 + received_count :]
    me = position_of(plan.sizes)
    total = keep_ref[0 : plan.width]
    for ref in received:
        total = total + ref[0 : plan.width].astype(f32)
    block[...] = total
    extra = sum_extra(keep_ref[plan.width : plan.width + EXTRA], received, plan.width)
    smalls[0:8] = extra[0:8]
    dss = jnp.concatenate([extra[8 : 8 + NCLASS], extra[8 + NCLASS :]], axis=1)
    tail = mlp_grads(table_ref[...], m1_ref, m2_ref, hidden_ref[...], dss, grads)
    for i, row in enumerate(tail):
        smalls[8 + i : 9 + i, :] = row

    first = me * plan.conv_rows % 8
    for r in range(plan.conv_rows):
        at = slice(r * C, (r + 1) * C)
        gradient = block[pl.ds(first + r, 4, plan.conv_pad), :]
        new = adam(*[conv_ref[k, :, at] for k in range(4)], gradient, rate_conv, decay_weights)
        for k in range(4):
            conv_new[k, :, at] = new[k]
        conv_copy[:, at] = new[0].astype(bf16)

    start = me * plan.dense_rows
    for r in range(plan.dense_rows):
        at = slice(r * C, (r + 1) * C)
        gradient = grads[pl.ds(start + r, 1), :]
        rate = jnp.where(start + r < TABLE_ROWS, rate_table, rate_dense)
        new = adam(*[dense_ref[k : k + 1, at] for k in range(4)], gradient, rate, decay_weights)
        for k in range(4):
            dense_new[k : k + 1, at] = new[k]
        rows[r : r + 1, :] = new[0]
    dense_copy[...] = rows[...].astype(bf16)

    start = me * plan.small_len
    lane = lax.broadcasted_iota(jnp.int32, (8, C), 1)
    near = jnp.broadcast_to(smalls[pl.ds(start // C, 1), :], (8, C))
    far = jnp.broadcast_to(smalls[pl.ds(start // C + 1, 1), :], (8, C))
    off = C - start % C
    gradient = jnp.where(lane < off, pltpu.roll(near, off, 1), pltpu.roll(far, off, 1))
    gradient = gradient[0:1, 0 : plan.small_len]
    new = adam(*[small_ref[k : k + 1, :] for k in range(4)], gradient, rate_small, 0.0)
    for k in range(4):
        small_new[k : k + 1, :] = new[k]
    small_copy[...] = new[0].astype(bf16)


def run_update(plan, keep, received, mlp, states):
    struct = jax.ShapeDtypeStruct
    shapes = [struct(state.shape, f32) for state in states]
    shapes += [struct((4, plan.conv_len), bf16), struct((plan.dense_rows, C), bf16), struct((1, plan.small_len), bf16)]
    return pl.pallas_call(
        functools.partial(update_body, plan, len(received)),
        out_shape=shapes,
        in_specs=vmem_specs(1 + len(received) + 4 + 3),
        out_specs=vmem_specs(6),
        scratch_shapes=[
            pltpu.VMEM((plan.width, C), f32),
            pltpu.VMEM((MLP_ROWS, C), f32),
            pltpu.VMEM((plan.dense_rows, C), f32),
            pltpu.VMEM((24, C), f32),
        ],
        compiler_params=limit(24),
        name="update",
    )(keep, *received, *mlp, *states)


def swap(values, axis, size, turn):
    return lax.ppermute(values, axis, [(i, i ^ turn) for i in range(size)])


def gather_ring(plan, own, prepare):
    (outer, outer_size), (inner, inner_size) = plan.sizes
    line = [own] + [swap(own, inner, inner_size, 2 * k) for k in range(1, plan.line)]
    line, prepared = lax.optimization_barrier((line, prepare()))
    line = jnp.stack(line)
    held = []
    for part, turn in ((line[: plan.line // 2], 1), (line[plan.line // 2 :], 2)):
        held.append(jnp.concatenate([part, swap(part, outer, outer_size, turn)]))
    held = held + [swap(part, outer, outer_size, 2 - k) for k, part in enumerate(held)]
    return prepared, held + [swap(part, inner, inner_size, 1) for part in held]


def reduce_ring(plan, keep, send):
    (outer, outer_size), (inner, inner_size) = plan.sizes
    received = [swap(send, inner, inner_size, 1)]
    keep, *sends = run_merge(plan, plan.half, outer_size, keep, received)
    received = [swap(part, outer, outer_size, k + 1) for k, part in enumerate(sends)]
    keep, *sends = run_merge(plan, plan.line, plan.line, keep, received)
    return keep, [swap(part, inner, inner_size, 2 * (k + 1)) for k, part in enumerate(sends)]


def plain_update(plan, position, grads, extra, mlp, states):
    conv_state, mlp_state, small_state = states
    conv_red = lax.psum_scatter(grads.reshape(4, -1), AXES, scatter_dimension=1, tiled=True)
    extra = lax.psum(extra, AXES)
    dss = jnp.concatenate([extra[8 : 8 + NCLASS], extra[8 + NCLASS :]], axis=1)
    dense_grad, tail = run_mlp(*mlp, dss)
    dense_red = lax.dynamic_slice_in_dim(dense_grad.reshape(-1), position * plan.dense_len, plan.dense_len)
    flat = jnp.concatenate([extra[:8], tail]).reshape(-1)
    small_red = lax.dynamic_slice_in_dim(flat, position * plan.small_len, plan.small_len)
    flat_index = position * plan.dense_len + jnp.arange(plan.dense_len, dtype=jnp.int32)
    dense_rate = jnp.where(flat_index < NCLASS * EMB, rate_table, rate_dense)
    new = [
        jnp.stack(adam(*state, red, rate, decay))
        for state, red, rate, decay in (
            (conv_state, conv_red, rate_conv, decay_weights),
            (mlp_state, dense_red, dense_rate, decay_weights),
            (small_state, small_red, rate_small, 0.0),
        )
    ]
    return new + [state[0].astype(bf16) for state in new]


def per_device(sizes, samples, cotangent, class_ids, *states):
    conv_state, mlp_state, small_state = states
    plan = Plan(sizes, conv_state.shape[2], mlp_state.shape[1], small_state.shape[1])
    x, cot = samples[0], cotangent[0]
    if plan.rings:
        prepared, firsts = gather_ring(plan, run_pack(plan, *states), lambda: run_prepare(x, cot))
        rests = firsts
    else:
        conv, dense, small = [state[0].astype(bf16) for state in states]
        conv = lax.all_gather(conv, AXES, axis=1, tiled=True).reshape(4, KERNEL_ROWS, C)
        firsts = [conv[0], lax.all_gather(small, AXES, axis=0, tiled=True).reshape(-1, C)]
        rests = [conv[1:], lax.all_gather(dense, AXES, axis=0, tiled=True).reshape(MLP_ROWS, C)]
        prepared = run_prepare(x, cot)
    fronted = run_front(plan, x, prepared[0], firsts)
    out, dx, table, m1, m2, hidden, first, second = run_block(plan, class_ids, x, cot, prepared, fronted, rests)
    mlp = (table, m1, m2, hidden)
    if plan.rings:
        keep, received = reduce_ring(plan, first, second)
        results = run_update(plan, keep, received, mlp, states)
    else:
        results = plain_update(plan, lax.axis_index(AXES), first, second, mlp, states)
    conv_new, mlp_new, small_new, conv_copy, mlp_copy, small_copy = results
    return out[None], dx[None], conv_new, mlp_new, small_new, conv_copy, mlp_copy.reshape(-1), small_copy.reshape(-1)


def solution(mesh):
    sizes = tuple((axis, mesh.shape[axis]) for axis in AXES)

    def body(*args):
        return per_device(sizes, *args)

    return jax.shard_map(
        body,
        mesh=mesh,
        in_specs=(
            P(AXES, None, None, None),
            P(AXES, None, None, None),
            P(AXES),
            P(None, None, AXES),
            P(None, AXES),
            P(None, AXES),
        ),
        out_specs=(
            P(AXES, None, None, None),
            P(AXES, None, None, None),
            P(None, None, AXES),
            P(None, AXES),
            P(None, AXES),
            P(None, AXES),
            P(AXES),
            P(AXES),
        ),
        check_vma=False,
    )
```

```python
import functools

import jax
import jax.numpy as jnp
from jax import lax
from jax.experimental import pallas as pl
from jax.experimental.pallas import tpu as pltpu
from jax.sharding import PartitionSpec as P

C = 128
EMB = 512
GROUPS = 8
H = 64
W = 64
NCLASS = 16
STEP = 10
TAPS = 9
CELLS = H * W
PER_GROUP = CELLS * (C // GROUPS)
TABLE_ROWS = NCLASS * EMB // C
M1_ROWS = EMB * EMB // C
M2_ROWS = EMB * 2
MLP_ROWS = TABLE_ROWS + M1_ROWS + M2_ROWS
KERNEL_ROWS = TAPS * C
AXES = ("dp", "fsdp")

beta_one = 0.9
beta_two = 0.999
adam_eps = 1e-08
ema_decay = 0.99
norm_eps = 1e-05
rate_conv = 0.08
rate_table = 0.6
rate_dense = 0.1
rate_small = 0.15
decay_weights = 0.01

f32 = jnp.float32
bf16 = jnp.bfloat16
NN = (((1,), (0,)), ((), ()))
NT = (((1,), (1,)), ((), ()))
TN = (((0,), (0,)), ((), ()))
EXTRA = 8 + 2 * NCLASS
R = 8
Q = 4
STEPS = H // R
PART = CELLS // STEPS


def each(count, step, carry):
    for index in range(count):
        carry = step(index, carry)
    return carry


def mm(a, b, dims=NN):
    return lax.dot_general(a, b, dims, preferred_element_type=f32)


def three(v):
    high = v.astype(bf16)
    rest = v - high.astype(f32)
    mid = rest.astype(bf16)
    return high, mid, (rest - mid.astype(f32)).astype(bf16)


def group_sum(rows):
    lane = lax.broadcasted_iota(jnp.int32, rows.shape, 1)
    for step in (1, 2, 4, 8):
        up = pltpu.roll(rows, C - step, 1)
        down = pltpu.roll(rows, step, 1)
        rows = rows + jnp.where((lane & step) == 0, up, down)
    return rows


def fold(values):
    return jnp.sum(values.reshape(-1, 8, values.shape[-1]), axis=0)


def total_of(partial):
    return jnp.broadcast_to(jnp.sum(partial, axis=0, keepdims=True), partial.shape)


def one(rows):
    return rows[0:1].reshape(1, 1, C)


def normal_cdf(v):
    return 0.5 * (1.0 + lax.erf(v * 0.7071067811865476))


def gelu_slope(v, prob):
    return prob + v * (jnp.exp(-0.5 * v * v) * 0.3989422804014327)


def put_windows(win_ref, row, values):
    rows = values.shape[0]
    place = lax.broadcasted_iota(jnp.int32, values.shape, 1)
    left = jnp.where(place == 0, 0.0, pltpu.roll(values, 1, 1))
    right = jnp.where(place == W - 1, 0.0, pltpu.roll(values, W - 1, 1))
    win_ref[pl.ds(row + 1, rows), :, 0:C] = left.astype(bf16)
    win_ref[pl.ds(row + 1, rows), :, C : 2 * C] = values.astype(bf16)
    win_ref[pl.ds(row + 1, rows), :, 2 * C : 3 * C] = right.astype(bf16)


def clear_edges(win_ref):
    edge = jnp.zeros((1,) + tuple(win_ref.shape[1:]), win_ref.dtype)
    win_ref[0:1] = edge
    win_ref[H + 1 : H + 2] = edge


def pair_forward(pair_ref, kernel_ref):
    zero = jnp.zeros((3 * C, C), bf16)
    pair_ref[0 : TAPS * C, 0:C] = kernel_ref[...]
    pair_ref[TAPS * C :, 0:C] = zero
    pair_ref[0 : 3 * C, C:] = zero
    pair_ref[3 * C :, C:] = kernel_ref[...]


def flip(block):
    return jnp.transpose(block.astype(f32)).astype(bf16)


def pair_backward(pair_ref, kernel_ref):
    zero = jnp.zeros((3 * C, C), bf16)
    pair_ref[TAPS * C :, 0:C] = zero
    pair_ref[0 : 3 * C, C:] = zero
    for tap in range(TAPS):
        block = flip(kernel_ref[(TAPS - 1 - tap) * C : (TAPS - tap) * C, :])
        pair_ref[tap * C : (tap + 1) * C, 0:C] = block
        pair_ref[(tap + 3) * C : (tap + 4) * C, C:] = block


def pair_conv(win_ref, pair_ref, first):
    view = win_ref.reshape(H // 2 + 1, 2, W, 3 * C)
    taken = [view[pl.ds(first + t // 2, Q), t % 2] for t in range(4)]
    stacked = jnp.concatenate(taken, axis=-1).reshape(Q * W, 12 * C)
    return mm(stacked, pair_ref[...]).reshape(Q, W, 2 * C)


def pairs_of(ref, first):
    view = ref.reshape(H // 2, 2, W, C)
    return [view.at[pl.ds(first, Q), parity] for parity in range(2)]


def kernel_grad(act_ref, win_ref, out_ref):
    left = act_ref[1 : H + 1, :, C : 2 * C].reshape(CELLS, C)
    right = jnp.concatenate([win_ref[t : t + H] for t in range(3)], axis=-1)
    got = mm(left, right.reshape(CELLS, TAPS * C), TN)
    for t in range(TAPS):
        out_ref[t * C : (t + 1) * C, :] = got[:, (TAPS - 1 - t) * C : (TAPS - t) * C]


def position_of(sizes):
    (outer, _), (inner, inner_size) = sizes
    return lax.axis_index(outer) * inner_size + lax.axis_index(inner)


def prepare_body(x_ref, cot_ref, own_ref, stats_ref, cw, gdb_ref, near_ref):
    near_ref[...] = own_ref[...]
    zero8 = jnp.zeros((8, C), f32)

    def read_x(i):
        return x_ref[pl.ds(i * R, R)].astype(f32)

    total = each(H // R, lambda i, s: s + fold(read_x(i)), zero8)
    mean = group_sum(total_of(total)) * (1.0 / PER_GROUP)

    def square_x(i, s):
        d = read_x(i) - one(mean)
        return s + fold(d * d)

    var = group_sum(total_of(each(H // R, square_x, zero8))) * (1.0 / PER_GROUP)
    stats_ref[0:8] = mean
    stats_ref[8:16] = lax.rsqrt(var + norm_eps)
    cw[H // 2 : H // 2 + 1] = jnp.zeros((1, W // 2, 4 * C), bf16)

    def cot_windows(i, s):
        values = cot_ref[pl.ds(i * R, R)].astype(f32)
        place = lax.broadcasted_iota(jnp.int32, values.shape, 1)
        after = jnp.where(place == W // 2 - 1, 0.0, pltpu.roll(values, W // 2 - 1, 1))
        cw[pl.ds(i * R, R), :, 0 : 2 * C] = values.astype(bf16)
        cw[pl.ds(i * R, R), :, 2 * C :] = after.astype(bf16)
        return s + fold(values)

    gdb_ref[...] = total_of(each(H // 2 // R, cot_windows, jnp.zeros((8, 2 * C), f32)))


def run_prepare(x, cot, own):
    struct = jax.ShapeDtypeStruct
    return pl.pallas_call(
        prepare_body,
        out_shape=[struct((16, C), f32), struct((H // 2 + 1, W // 2, 4 * C), bf16), struct((8, 2 * C), f32), struct(own.shape, bf16)],
        in_specs=vmem_specs(3),
        out_specs=vmem_specs(4),
        compiler_params=limit(8),
        cost_estimate=cost(2, 3 << 20),
        name="prepare",
    )(x, cot, own)


def block_body(plan, *refs):
    refs = list(refs)
    count = 8 if plan.rings else 4
    cls_ref, x_ref, cot_ref, stats_ref, cw, gdb_ref = refs[:6]
    inputs = refs[6 : 6 + count]
    out_hbm, slope1_ref, drf, factors_ref, table_ref, m1_ref, m2_ref, hidden_ref = refs[6 + count : 14 + count]
    results = refs[14 + count : 16 + count]
    a1w, a2w, t1w, t2w, rw, c1, g1p, g2p, rf, pairs, conv, dense, kernels, smalls, out_ref, out_sem = refs[16 + count :]
    me = position_of(plan.sizes)
    k1_ref, k2_ref, kd0_ref, kd1_ref = [kernels.at[k] for k in range(4)]
    pair1, pair2, back1, back2 = [pairs.at[k] for k in range(4)]
    zero8 = jnp.zeros((8, C), f32)

    if plan.rings:
        shards = list(plan.sources(me))
        conv[...] = jnp.zeros(conv.shape, f32)
        dense[...] = jnp.zeros(dense.shape, f32)
        small = jnp.zeros((16, C), f32)
        row = lax.broadcasted_iota(jnp.int32, (16, C), 0)
        lane = lax.broadcasted_iota(jnp.int32, (16, C), 1)
        for part, place, owner in shards:
            values = inputs[part][place, 0 : plan.first_rows].astype(f32)
            first = plan.tile_of(owner * plan.conv_rows)
            conv[0, pl.ds(first, plan.conv_pad), :] += values[: plan.conv_pad]
            at = row * C + lane - owner * plan.small_len
            own = jnp.broadcast_to(values[plan.conv_pad : plan.conv_pad + 1], (16, C))
            small = jnp.where((at >= 0) & (at < plan.small_len), own, small)
        smalls[...] = small
        k1_ref[...] = conv[0, 0:KERNEL_ROWS].astype(bf16)
    else:
        k1_ref[...] = inputs[0][...]
        smalls[0:14] = inputs[1][...].astype(f32)

    def take_rest(step, steps):
        if not plan.rings:
            return
        for part, place, owner in shards[step::steps]:
            values = inputs[part][place, plan.first_rows : plan.own_rows].astype(f32)
            first = plan.tile_of(owner * plan.conv_rows)
            for k in range(3):
                conv[k + 1, pl.ds(first, plan.conv_pad), :] += values[k * plan.conv_pad : (k + 1) * plan.conv_pad]
            first = plan.tile_of(owner * plan.dense_rows)
            dense[pl.ds(first, plan.dense_pad), :] += values[plan.dense_at : plan.dense_at + plan.dense_pad]

    def small_row(index):
        return jnp.broadcast_to(smalls[index : index + 1, :], (8, C))

    def small_run(first, count):
        return jnp.concatenate([smalls[first + i : first + i + 1, :] for i in range(count)], axis=1)

    gain1, bias1, cb1, gain2, bias2, cb2 = [small_row(i) for i in range(6)]
    mean1, rs1 = stats_ref[0:8], stats_ref[8:16]
    slope1 = rs1 * (1.0 + gain1)

    pair_forward(pair1, k1_ref)
    clear_edges(a1w)

    def front1(i):
        v = (x_ref[pl.ds(i * R, R)].astype(f32) - one(mean1)) * one(slope1) + one(bias1)
        prob = normal_cdf(v)
        put_windows(a1w, i * R, v * prob)
        g1p[pl.ds(i * R, R)] = gelu_slope(v, prob)

    moments = []

    def conv1(i):
        got = pair_conv(a1w, pair1, i * Q)
        values = [got[..., parity * C : (parity + 1) * C] + one(cb1) for parity in range(2)]
        for place, value in zip(pairs_of(c1, i * Q), values):
            place[...] = value
        centre = total_of(fold(values[0]) + fold(values[1])) * (1.0 / PART)
        off = [value - one(centre) for value in values]
        moments.append((centre, fold(off[0] * off[0]) + fold(off[1] * off[1])))

    front1(0)
    for i in range(STEPS):
        if i + 1 < STEPS:
            front1(i + 1)
        conv1(i)
        take_rest(i, STEPS)
    centre = sum(part[0] for part in moments) * (1.0 / STEPS)
    spread = sum(total_of(part[1]) + PART * (part[0] - centre) * (part[0] - centre) for part in moments) * (1.0 / CELLS)

    if plan.rings:
        kernels[1:4] = conv[1:4, 0:KERNEL_ROWS].astype(bf16)
    else:
        kernels[1:4] = inputs[2][...]
        dense[0:MLP_ROWS] = inputs[3][...].astype(f32)

    def lanes(first, rows, parts):
        pieces = [dense[pl.ds(first + part, rows, parts), :] for part in range(parts)]
        return jnp.concatenate(pieces, axis=1).astype(bf16)

    table_ref[...] = lanes(0, NCLASS, EMB // C)
    m1_ref[...] = lanes(TABLE_ROWS, EMB, EMB // C)
    m2_ref[...] = lanes(TABLE_ROWS + M1_ROWS, EMB, 2)
    hidden = mm(table_ref[...], m1_ref[...]) + small_run(8, 4)
    hidden_ref[...] = hidden
    act = hidden * normal_cdf(hidden)
    ss = sum(mm(part, m2_ref[...]) for part in three(act)) + small_run(12, 2)
    mine = lax.broadcasted_iota(jnp.int32, (NCLASS, 2 * C), 0) == cls_ref[0]
    chosen = jnp.sum(jnp.where(mine, ss, 0.0), axis=0, keepdims=True)
    scale = jnp.broadcast_to(1.0 + chosen[:, :C], (8, C))
    shift = jnp.broadcast_to(chosen[:, C:], (8, C))
    pair_forward(pair2, k2_ref)

    centre_s = centre * scale + shift
    mean2 = group_sum(centre_s) * (GROUPS / C)
    off = centre_s - mean2
    var2 = group_sum(spread * scale * scale + off * off) * (GROUPS / C)
    rs2 = lax.rsqrt(var2 + norm_eps)

    def unit2(values):
        return (values * one(scale) + one(shift - mean2)) * one(rs2)

    clear_edges(a2w)

    def front2(i):
        v = unit2(c1[pl.ds(i * R, R)]) * one(1.0 + gain2) + one(bias2)
        prob = normal_cdf(v)
        put_windows(a2w, i * R, v * prob)
        g2p[pl.ds(i * R, R)] = gelu_slope(v, prob)

    rw[0:1] = jnp.zeros((1, W // 2, 3 * C), bf16)

    def conv2(i):
        got = pair_conv(a2w, pair2, i * Q)
        for parity, (place, source) in enumerate(zip(pairs_of(rf, i * Q), pairs_of(x_ref, i * Q))):
            r = source[...].astype(f32) + (got[..., parity * C : (parity + 1) * C] + one(cb2))
            place[...] = r.astype(bf16).astype(f32)
        even = rf[pl.ds(i * R, R), pl.ds(0, W // 2, 2), :]
        odd = rf[pl.ds(i * R, R), pl.ds(1, W // 2, 2), :]
        place = lax.broadcasted_iota(jnp.int32, odd.shape, 1)
        before = jnp.where(place == 0, 0.0, pltpu.roll(odd, 1, 1))
        rw[pl.ds(i * R + 1, R), :, 0:C] = before.astype(bf16)
        rw[pl.ds(i * R + 1, R), :, C : 2 * C] = even.astype(bf16)
        rw[pl.ds(i * R + 1, R), :, 2 * C :] = odd.astype(bf16)

    def down_rows(first, rows):
        view = rw.reshape(H // 2 + 1, 2, W // 2, 3 * C)
        taken = [view[pl.ds(first + t // 2, rows), t % 2] for t in range(3)]
        return jnp.concatenate(taken, axis=-1).reshape(rows * W // 2, TAPS * C)

    kd = jnp.concatenate([kd0_ref[...], kd1_ref[...]], axis=1)
    bias_down = small_run(6, 2)

    def down(i):
        got = mm(down_rows(i * R, R), kd) + bias_down
        out_ref[pl.ds(i * R, R)] = got.reshape(R, W // 2, 2 * C).astype(bf16)

    front2(0)
    for i in range(STEPS):
        if i + 1 < STEPS:
            front2(i + 1)
        conv2(i)
        if i % 2 == 1:
            down(i // 2)
    out_copy = pltpu.make_async_copy(out_ref, out_hbm, out_sem)
    out_copy.start()

    def tap(i, j):
        return flip(kd[(3 * i + j) * C : (3 * i + j + 1) * C, :])

    none = jnp.zeros((2 * C, C), bf16)
    even_rows = jnp.concatenate([
        jnp.concatenate([tap(1, 1), none], axis=0),
        jnp.concatenate([tap(1, 2), tap(1, 0)], axis=0),
    ], axis=1)
    odd_rows = jnp.concatenate([
        jnp.concatenate([tap(2, 1), none, tap(0, 1), none], axis=0),
        jnp.concatenate([tap(2, 2), tap(2, 0), tap(0, 2), tap(0, 0)], axis=0),
    ], axis=1)
    clear_edges(t2w)

    def back_down(i):
        rows = jnp.concatenate([cw[pl.ds(i * R, R)], cw[pl.ds(i * R + 1, R)]], axis=-1)
        rows = rows.reshape(R * W // 2, 8 * C)
        view = drf.reshape(H // 2, 2, W, C)
        for parity, got in enumerate((mm(rows[:, : 4 * C], even_rows), mm(rows, odd_rows))):
            got = got.reshape(R, W // 2, 2 * C)
            view[pl.ds(i * R, R), parity, pl.ds(0, W // 2, 2), :] = got[..., :C]
            view[pl.ds(i * R, R), parity, pl.ds(1, W // 2, 2), :] = got[..., C:]

    def t2_windows(i):
        values = drf[pl.ds(i * R, R)]
        put_windows(t2w, i * R, values)
        return fold(values)

    gcb2 = zero8
    for i in range(H // 2 // R):
        back_down(i)
        gcb2 = gcb2 + t2_windows(2 * i) + t2_windows(2 * i + 1)
    gcb2 = total_of(gcb2)

    gkd = mm(down_rows(0, H // 2), cot_ref[...].reshape(CELLS // 4, 2 * C), TN)
    conv[2, 0:KERNEL_ROWS] = gkd[:, :C]
    conv[3, 0:KERNEL_ROWS] = gkd[:, C:]

    def pull(i, s, win_ref, back_ref, slope_ref, out_slope_ref, units):
        got = pair_conv(win_ref, back_ref, i * Q)
        places = zip(pairs_of(slope_ref, i * Q), pairs_of(out_slope_ref, i * Q), units)
        for parity, (place, out_place, unit) in enumerate(places):
            dn = got[..., parity * C : (parity + 1) * C] * place[...]
            out_place[...] = dn
            s = s[0] + fold(dn), s[1] + fold(dn * unit)
        return s

    pair_backward(back2, k2_ref)
    sums = (zero8, zero8)
    for i in range(STEPS):
        sums = pull(i, sums, t2w, back2, g2p, g2p, [unit2(ref[...]) for ref in pairs_of(c1, i * Q)])
    gb2, gg2 = [total_of(part) for part in sums]
    mean_du2 = group_sum(gb2 * (1.0 + gain2)) * (1.0 / PER_GROUP)
    mean_duu2 = group_sum(gg2 * (1.0 + gain2)) * (1.0 / PER_GROUP)
    kernel_grad(a2w, t2w, conv.at[1])

    pair_backward(back1, k1_ref)
    clear_edges(t1w)

    def t1_windows(i, s):
        values = c1[pl.ds(i * R, R)]
        du = g2p[pl.ds(i * R, R)] * one(1.0 + gain2)
        ds = (du - one(mean_du2) - unit2(values) * one(mean_duu2)) * one(rs2)
        put_windows(t1w, i * R, ds * one(scale))
        return s[0] + fold(ds * values), s[1] + fold(ds)

    def unit1(ref):
        return (ref[...].astype(f32) - one(mean1)) * one(rs1)

    class_sums = t1_windows(0, (zero8, zero8))
    sums = (zero8, zero8)
    for i in range(STEPS):
        if i + 1 < STEPS:
            class_sums = t1_windows(i + 1, class_sums)
        sums = pull(i, sums, t1w, back1, g1p, slope1_ref, [unit1(ref) for ref in pairs_of(x_ref, i * Q)])
    gsc, gsh = [total_of(part) for part in class_sums]
    gb1, gg1 = [total_of(part) for part in sums]
    mean_du1 = group_sum(gb1 * (1.0 + gain1)) * (1.0 / PER_GROUP)
    mean_duu1 = group_sum(gg1 * (1.0 + gain1)) * (1.0 / PER_GROUP)
    for index, row in enumerate((1.0 + gain1, mean_du1, mean_duu1)):
        factors_ref[8 * index : 8 * index + 8] = row
    gdb = gdb_ref[...]
    rows = [gg1, gb1, gsh * scale, gg2, gb2, gcb2, gdb[:, :C], gdb[:, C:]]
    rows = [row[0:1] for row in rows]
    rows = rows + [jnp.where(mine[:, :C], row[0:1], 0.0) for row in (gsc, gsh)]
    extra = jnp.concatenate(rows, axis=0)
    if plan.rings:
        for k in (2, 3, 1):
            put_results(plan, me, k, conv, *results)
        kernel_grad(a1w, t1w, conv.at[0])
        put_results(plan, me, 0, conv, *results)
        keep_ref, send_ref = results
        keep_ref[plan.half * plan.width :] = extra
        send_ref[plan.half * plan.width :] = two_terms(extra)
    else:
        kernel_grad(a1w, t1w, conv.at[0])
        results[0][...] = conv[:, 0:KERNEL_ROWS]
        results[1][...] = extra
    out_copy.wait()


def finish_body(x_ref, stats_ref, slope_ref, grad_ref, factors_ref, dx_hbm, dx_ref, sems):
    mean, scale = stats_ref[0:8], stats_ref[8:16]
    gain, mean_du, mean_duu = [factors_ref[8 * k : 8 * k + 8] for k in range(3)]

    def finish(i, carry):
        du = slope_ref[pl.ds(i * R, R)] * one(gain)
        unit = (x_ref[pl.ds(i * R, R)].astype(f32) - one(mean)) * one(scale)
        dx = (du - one(mean_du) - unit * one(mean_duu)) * one(scale)
        dx_ref[pl.ds(i * R, R)] = (grad_ref[pl.ds(i * R, R)] + dx).astype(bf16)
        return carry

    copies = []
    for part in range(4):
        lax.fori_loop(part * H // R // 4, (part + 1) * H // R // 4, finish, 0)
        rows = pl.ds(part * H // 4, H // 4)
        copies.append(pltpu.make_async_copy(dx_ref.at[rows], dx_hbm.at[rows], sems.at[part]))
        copies[-1].start()
    for copy in copies:
        copy.wait()


def run_finish(x, stats, slope, grad, factors):
    return pl.pallas_call(
        finish_body,
        out_shape=jax.ShapeDtypeStruct((H, W, C), bf16),
        in_specs=vmem_specs(5),
        out_specs=pl.BlockSpec(memory_space=pltpu.HBM),
        scratch_shapes=[pltpu.VMEM((H, W, C), bf16), pltpu.SemaphoreType.DMA((4,))],
        compiler_params=limit(8),
        cost_estimate=cost(2, 6 << 20),
        name="finish",
    )(x, stats, slope, grad, factors)


def put_results(plan, me, k, conv, keep_ref, send_ref):
    pad = plan.conv_pad
    for core, result in enumerate((keep_ref, send_ref)):
        owners = plan.targets(me ^ core)
        parts = [conv[k, pl.ds(plan.tile_of(owner * plan.conv_rows), pad), :] for owner in owners]
        for place in range(0, len(parts), 2):
            two = jnp.concatenate(parts[place : place + 2], axis=0)
            at = (k * plan.half + place) * pad
            result[at : at + 2 * pad] = two.astype(result.dtype)


def two_terms(extra):
    high = extra.astype(bf16)
    return jnp.concatenate([high.astype(f32), extra - high.astype(f32)], axis=0).astype(bf16)


def vmem_specs(count):
    return [pl.BlockSpec(memory_space=pltpu.VMEM)] * count


def cost(mflops, moved):
    return pl.CostEstimate(flops=mflops << 20, bytes_accessed=moved, transcendentals=0)


def limit(size):
    return pltpu.CompilerParams(vmem_limit_bytes=size << 20)


class Plan:
    def __init__(self, sizes, conv_len, dense_len, small_len):
        (_, outer_size), (_, inner_size) = sizes
        count = outer_size * inner_size
        self.sizes, self.line = sizes, inner_size // 2
        self.conv_len, self.dense_len, self.small_len = conv_len, dense_len, small_len
        self.conv_rows, self.dense_rows = conv_len // C, dense_len // C
        powers = inner_size & (inner_size - 1) == 0 and inner_size >= 4 and outer_size == 4
        self.rings = powers and conv_len % C == 0 and dense_len % C == 0 and small_len <= C
        self.conv_pad = self.padded(self.conv_rows, count)
        self.dense_pad = self.padded(self.dense_rows, count)
        self.first_rows = -(-(self.conv_pad + 8) // 16) * 16
        self.dense_at = 3 * self.conv_pad
        self.rest_rows = -(-(self.dense_at + self.dense_pad) // 16) * 16
        self.own_rows = self.first_rows + self.rest_rows
        self.inner = inner_size
        self.half = count // 2
        self.width = 4 * self.conv_pad

    def sources(self, me):
        near = [2 * k for k in range(self.line)]
        low, high = near[: self.line // 2], near[self.line // 2 :]
        held = [low + [k ^ self.inner for k in low], high + [k ^ 2 * self.inner for k in high]]
        held += [[k ^ 2 * self.inner for k in held[0]], [k ^ self.inner for k in held[1]]]
        held += [[k ^ 1 for k in part] for part in held]
        for part, turns in enumerate(held):
            for place, turn in enumerate(turns):
                yield part, place, me ^ turn

    def targets(self, own):
        return [own ^ (plane * self.inner + 2 * k) for plane in range(4) for k in range(self.line)]

    def padded(self, rows, count):
        return max(-(-(rows * k % 8 + rows) // 8) * 8 for k in range(count))

    def tile_of(self, row):
        return pl.multiple_of(row // 8 * 8, 8)


def run_block(plan, class_ids, x, cot, prepared, inputs):
    struct = jax.ShapeDtypeStruct
    shapes = [
        struct((H // 2, W // 2, 2 * C), bf16),
        struct((H, W, C), f32),
        struct((H, W, C), f32),
        struct((24, C), f32),
        struct((NCLASS, EMB), bf16),
        struct((EMB, EMB), bf16),
        struct((EMB, 2 * C), bf16),
        struct((NCLASS, EMB), f32),
    ]
    if plan.rings:
        rows = plan.half * plan.width
        shapes += [struct((rows + EXTRA, C), f32), struct((rows + 2 * EXTRA, C), bf16)]
    else:
        shapes += [struct((4, KERNEL_ROWS, C), f32), struct((EXTRA, C), f32)]
    windows = pltpu.VMEM((H + 2, W, 3 * C), bf16)
    plane = pltpu.VMEM((H, W, C), f32)
    return pl.pallas_call(
        functools.partial(block_body, plan),
        out_shape=shapes,
        in_specs=[pl.BlockSpec(memory_space=pltpu.SMEM)] + vmem_specs(5 + len(inputs)),
        out_specs=[pl.BlockSpec(memory_space=pltpu.HBM)] + vmem_specs(9),
        scratch_shapes=[
            windows,
            windows,
            windows,
            windows,
            pltpu.VMEM((H + 2, W // 2, 3 * C), bf16),
            plane,
            plane,
            plane,
            plane,
            pltpu.VMEM((4, 12 * C, 2 * C), bf16),
            pltpu.VMEM((4, KERNEL_ROWS + 2 * plan.conv_pad, C), f32),
            pltpu.VMEM((MLP_ROWS + 2 * plan.dense_pad, C), f32),
            pltpu.VMEM((4, KERNEL_ROWS, C), bf16),
            pltpu.VMEM((16, C), f32),
            pltpu.VMEM((H // 2, W // 2, 2 * C), bf16),
            pltpu.SemaphoreType.DMA,
        ],
        compiler_params=limit(44),
        cost_estimate=cost(9000, 16 << 20),
        name="block",
    )(class_ids, x, cot, *prepared, *inputs)


def pack_body(plan, conv_hbm, dense_hbm, small_hbm, out_ref, conv_ref, dense_ref, small_ref, rows, sems):
    pairs = ((conv_hbm.at[0], conv_ref), (dense_hbm, dense_ref), (small_hbm, small_ref))
    copies = [pltpu.make_async_copy(source, target, sems.at[k]) for k, (source, target) in enumerate(pairs)]
    for copy in copies:
        copy.start()
    me = position_of(plan.sizes)
    rows[...] = jnp.zeros(rows.shape, f32)
    starts = [0] + [plan.first_rows + k * plan.conv_pad for k in range(3)]
    first = me * plan.conv_rows % 8
    copies[0].wait()
    for r in range(plan.conv_rows):
        for k in range(4):
            rows[pl.ds(starts[k] + first + r, 1), :] = conv_ref[k : k + 1, r * C : (r + 1) * C]
    copies[1].wait()
    first = plan.first_rows + plan.dense_at + me * plan.dense_rows % 8
    for r in range(plan.dense_rows):
        rows[pl.ds(first + r, 1), :] = dense_ref[0:1, r * C : (r + 1) * C]
    copies[2].wait()
    own = jnp.concatenate([small_ref[0:1, :], jnp.zeros((1, C - plan.small_len), f32)], axis=1)
    own = pltpu.roll(jnp.broadcast_to(own, (8, C)), me * plan.small_len % C, 1)
    rows[plan.conv_pad : plan.conv_pad + 1] = own[0:1]
    out_ref[...] = rows[...].astype(bf16)


def run_pack(plan, conv_state, mlp_state, small_state):
    return pl.pallas_call(
        functools.partial(pack_body, plan),
        out_shape=jax.ShapeDtypeStruct((plan.own_rows, C), bf16),
        in_specs=[pl.BlockSpec(memory_space=pltpu.HBM)] * 3,
        out_specs=pl.BlockSpec(memory_space=pltpu.VMEM),
        scratch_shapes=[
            pltpu.VMEM((4, plan.conv_len), f32),
            pltpu.VMEM((4, plan.dense_len), f32),
            pltpu.VMEM((4, plan.small_len), f32),
            pltpu.VMEM((plan.own_rows, C), f32),
            pltpu.SemaphoreType.DMA((3,)),
        ],
        compiler_params=pltpu.CompilerParams(vmem_limit_bytes=(64 << 20) - (190 << 10)),
        name="pack",
    )(conv_state, mlp_state, small_state)


def sum_extra(extra, received, at):
    for ref in received:
        extra = extra + ref[at : at + EXTRA].astype(f32) + ref[at + EXTRA : at + 2 * EXTRA].astype(f32)
    return extra


def merge_body(plan, blocks, groups, *refs):
    keep_ref, received = refs[0], refs[1 : len(refs) - groups]
    outs = refs[len(refs) - groups :]
    size = blocks // groups * plan.conv_pad
    for group, out in enumerate(outs):
        parts = []
        for k in range(4):
            at = k * blocks * plan.conv_pad + group * size
            total = keep_ref[at : at + size]
            for ref in received:
                total = total + ref[at : at + size].astype(f32)
            parts.append(total)
        out[0 : 4 * size] = jnp.concatenate(parts, axis=0).astype(out.dtype)
    at = blocks * plan.width
    extra = sum_extra(keep_ref[at : at + EXTRA], received, at)
    outs[0][4 * size :] = extra
    for ref in outs[1:]:
        ref[4 * size :] = two_terms(extra)


def run_merge(plan, blocks, groups, keep, received):
    rows = blocks // groups * plan.width
    shapes = [jax.ShapeDtypeStruct((rows + EXTRA, C), f32)]
    shapes += [jax.ShapeDtypeStruct((rows + 2 * EXTRA, C), bf16)] * (groups - 1)
    return pl.pallas_call(
        functools.partial(merge_body, plan, blocks, groups),
        out_shape=shapes,
        in_specs=vmem_specs(1 + len(received)),
        out_specs=vmem_specs(groups),
        compiler_params=limit(16),
        name="merge",
    )(keep, *received)


def mlp_grads(table, m1_ref, m2_ref, hidden, dss, out_ref):
    prob = normal_cdf(hidden)

    def put(first, values):
        parts = values.shape[1] // C
        for part in range(parts):
            out_ref[pl.ds(first + part, values.shape[0], parts), :] = values[:, part * C : (part + 1) * C]

    def outer(left, right):
        lefts = [a for k, a in enumerate(left) for b in right[: 3 - k]]
        rights = [b for k, a in enumerate(left) for b in right[: 3 - k]]
        return mm(jnp.concatenate(lefts, axis=0), jnp.concatenate(rights, axis=0), TN)

    def back(values, weights):
        return sum(mm(part, weights, NT) for part in three(values))

    dp = back(dss, m2_ref[...]) * gelu_slope(hidden, prob)
    put(0, back(dp, m1_ref[...]))
    put(TABLE_ROWS, outer([table], three(dp)))
    put(TABLE_ROWS + M1_ROWS, outer(three(hidden * prob), three(dss)))
    ge1 = jnp.sum(dp, axis=0, keepdims=True)
    ge2 = jnp.sum(dss, axis=0, keepdims=True)
    return [ge1[:, i * C : (i + 1) * C] for i in range(4)] + [ge2[:, i * C : (i + 1) * C] for i in range(2)]


def mlp_body(table_ref, m1_ref, m2_ref, hidden_ref, dss_ref, out_ref, tail_ref):
    tail = mlp_grads(table_ref[...], m1_ref, m2_ref, hidden_ref[...], dss_ref[...], out_ref)
    for i, row in enumerate(tail):
        tail_ref[i : i + 1, :] = row


def run_mlp(table, m1, m2, hidden, dss):
    return pl.pallas_call(
        mlp_body,
        out_shape=[jax.ShapeDtypeStruct((MLP_ROWS, C), f32), jax.ShapeDtypeStruct((6, C), f32)],
        in_specs=vmem_specs(5),
        out_specs=vmem_specs(2),
        compiler_params=limit(32),
        name="mlp_grad",
    )(table, m1, m2, hidden, dss)


def adam(weight, first, second, average, gradient, rate, decay):
    first = beta_one * first + (1.0 - beta_one) * gradient
    second = beta_two * second + (1.0 - beta_two) * gradient * gradient
    first_hat = first * (1.0 / (1.0 - beta_one**STEP))
    second_hat = second * (1.0 / (1.0 - beta_two**STEP))
    weight = weight - rate * (first_hat / (jnp.sqrt(second_hat) + adam_eps) + decay * weight)
    return weight, first, second, ema_decay * average + (1.0 - ema_decay) * weight


def update_body(plan, received_count, *refs):
    keep_ref, received = refs[0], refs[1 : 1 + received_count]
    table_ref, m1_ref, m2_ref, hidden_ref, conv_ref, dense_ref, small_ref = refs[1 + received_count : 8 + received_count]
    conv_new, dense_new, small_new, conv_copy, dense_copy, small_copy = refs[8 + received_count : 14 + received_count]
    block, grads, rows, smalls = refs[14 + received_count :]
    me = position_of(plan.sizes)
    total = keep_ref[0 : plan.width]
    for ref in received:
        total = total + ref[0 : plan.width].astype(f32)
    block[...] = total
    extra = sum_extra(keep_ref[plan.width : plan.width + EXTRA], received, plan.width)
    smalls[0:8] = extra[0:8]
    dss = jnp.concatenate([extra[8 : 8 + NCLASS], extra[8 + NCLASS :]], axis=1)
    tail = mlp_grads(table_ref[...], m1_ref, m2_ref, hidden_ref[...], dss, grads)
    for i, row in enumerate(tail):
        smalls[8 + i : 9 + i, :] = row

    first = me * plan.conv_rows % 8
    for r in range(plan.conv_rows):
        at = slice(r * C, (r + 1) * C)
        gradient = block[pl.ds(first + r, 4, plan.conv_pad), :]
        new = adam(*[conv_ref[k, :, at] for k in range(4)], gradient, rate_conv, decay_weights)
        for k in range(4):
            conv_new[k, :, at] = new[k]
        conv_copy[:, at] = new[0].astype(bf16)

    start = me * plan.dense_rows
    for r in range(plan.dense_rows):
        at = slice(r * C, (r + 1) * C)
        gradient = grads[pl.ds(start + r, 1), :]
        rate = jnp.where(start + r < TABLE_ROWS, rate_table, rate_dense)
        new = adam(*[dense_ref[k : k + 1, at] for k in range(4)], gradient, rate, decay_weights)
        for k in range(4):
            dense_new[k : k + 1, at] = new[k]
        rows[r : r + 1, :] = new[0]
    dense_copy[...] = rows[...].astype(bf16)

    start = me * plan.small_len
    lane = lax.broadcasted_iota(jnp.int32, (8, C), 1)
    near = jnp.broadcast_to(smalls[pl.ds(start // C, 1), :], (8, C))
    far = jnp.broadcast_to(smalls[pl.ds(start // C + 1, 1), :], (8, C))
    off = C - start % C
    gradient = jnp.where(lane < off, pltpu.roll(near, off, 1), pltpu.roll(far, off, 1))
    gradient = gradient[0:1, 0 : plan.small_len]
    new = adam(*[small_ref[k : k + 1, :] for k in range(4)], gradient, rate_small, 0.0)
    for k in range(4):
        small_new[k : k + 1, :] = new[k]
    small_copy[...] = new[0].astype(bf16)


def run_update(plan, keep, received, mlp, states):
    struct = jax.ShapeDtypeStruct
    shapes = [struct(state.shape, f32) for state in states]
    shapes += [struct((4, plan.conv_len), bf16), struct((plan.dense_rows, C), bf16), struct((1, plan.small_len), bf16)]
    return pl.pallas_call(
        functools.partial(update_body, plan, len(received)),
        out_shape=shapes,
        in_specs=vmem_specs(1 + len(received) + 4 + 3),
        out_specs=vmem_specs(6),
        scratch_shapes=[
            pltpu.VMEM((plan.width, C), f32),
            pltpu.VMEM((MLP_ROWS, C), f32),
            pltpu.VMEM((plan.dense_rows, C), f32),
            pltpu.VMEM((24, C), f32),
        ],
        compiler_params=limit(24),
        name="update",
    )(keep, *received, *mlp, *states)


def swap(values, axis, size, turn):
    return lax.ppermute(values, axis, [(i, i ^ turn) for i in range(size)])


def gather_ring(plan, own, prepare):
    (outer, outer_size), (inner, inner_size) = plan.sizes
    line = [swap(own, inner, inner_size, 2 * k) for k in range(1, plan.line)]
    line, (*prepared, own) = lax.optimization_barrier((line, prepare(own)))
    line = [own] + line
    half = plan.line // 2
    held = []
    for part, turn in ((jnp.stack(line[:half]), 1), (jnp.stack(line[half:]), 2)):
        held.append(jnp.concatenate([part, swap(part, outer, outer_size, turn)]))
    held = held + [swap(part, outer, outer_size, 2 - k) for k, part in enumerate(held)]
    return prepared, held + [swap(part, inner, inner_size, 1) for part in held]


def reduce_ring(plan, keep, send):
    (outer, outer_size), (inner, inner_size) = plan.sizes
    received = [swap(send, inner, inner_size, 1)]
    keep, *sends = run_merge(plan, outer_size * plan.line, outer_size, keep, received)
    received = [swap(part, outer, outer_size, k + 1) for k, part in enumerate(sends)]
    keep, *sends = run_merge(plan, plan.line, plan.line, keep, received)
    return keep, [swap(part, inner, inner_size, 2 * (k + 1)) for k, part in enumerate(sends)]


def plain_update(plan, position, grads, extra, mlp, states):
    conv_state, mlp_state, small_state = states
    conv_red = lax.psum_scatter(grads.reshape(4, -1), AXES, scatter_dimension=1, tiled=True)
    extra = lax.psum(extra, AXES)
    dss = jnp.concatenate([extra[8 : 8 + NCLASS], extra[8 + NCLASS :]], axis=1)
    dense_grad, tail = run_mlp(*mlp, dss)
    dense_red = lax.dynamic_slice_in_dim(dense_grad.reshape(-1), position * plan.dense_len, plan.dense_len)
    flat = jnp.concatenate([extra[:8], tail]).reshape(-1)
    small_red = lax.dynamic_slice_in_dim(flat, position * plan.small_len, plan.small_len)
    flat_index = position * plan.dense_len + jnp.arange(plan.dense_len, dtype=jnp.int32)
    dense_rate = jnp.where(flat_index < NCLASS * EMB, rate_table, rate_dense)
    new = [
        jnp.stack(adam(*state, red, rate, decay))
        for state, red, rate, decay in (
            (conv_state, conv_red, rate_conv, decay_weights),
            (mlp_state, dense_red, dense_rate, decay_weights),
            (small_state, small_red, rate_small, 0.0),
        )
    ]
    return new + [state[0].astype(bf16) for state in new]


def per_device(sizes, samples, cotangent, class_ids, *states):
    conv_state, mlp_state, small_state = states
    plan = Plan(sizes, conv_state.shape[2], mlp_state.shape[1], small_state.shape[1])
    x, cot = samples[0], cotangent[0]
    if plan.rings:
        prepared, inputs = gather_ring(plan, run_pack(plan, *states), lambda own: run_prepare(x, cot, own))
    else:
        conv, dense, small = [state[0].astype(bf16) for state in states]
        conv = lax.all_gather(conv, AXES, axis=1, tiled=True).reshape(4, KERNEL_ROWS, C)
        small = lax.all_gather(small, AXES, axis=0, tiled=True).reshape(-1, C)
        dense = lax.all_gather(dense, AXES, axis=0, tiled=True).reshape(MLP_ROWS, C)
        inputs = [conv[0], small, conv[1:], dense]
        prepared = run_prepare(x, cot, small)[:3]
    out, slope, grad, factors, table, m1, m2, hidden, first, second = run_block(
        plan, class_ids, x, cot, prepared, inputs
    )
    dx = run_finish(x, prepared[0], slope, grad, factors)
    mlp = (table, m1, m2, hidden)
    if plan.rings:
        keep, received = reduce_ring(plan, first, second)
        results = run_update(plan, keep, received, mlp, states)
    else:
        results = plain_update(plan, lax.axis_index(AXES), first, second, mlp, states)
    conv_new, mlp_new, small_new, conv_copy, mlp_copy, small_copy = results
    return out[None], dx[None], conv_new, mlp_new, small_new, conv_copy, mlp_copy.reshape(-1), small_copy.reshape(-1)


def solution(mesh):
    sizes = tuple((axis, mesh.shape[axis]) for axis in AXES)

    def body(*args):
        return per_device(sizes, *args)

    return jax.shard_map(
        body,
        mesh=mesh,
        in_specs=(
            P(AXES, None, None, None),
            P(AXES, None, None, None),
            P(AXES),
            P(None, None, AXES),
            P(None, AXES),
            P(None, AXES),
        ),
        out_specs=(
            P(AXES, None, None, None),
            P(AXES, None, None, None),
            P(None, None, AXES),
            P(None, AXES),
            P(None, AXES),
            P(None, AXES),
            P(AXES),
            P(AXES),
        ),
        check_vma=False,
    )
```

```python
import functools

import jax
import jax.numpy as jnp
from jax import lax
from jax.experimental import pallas as pl
from jax.experimental.pallas import tpu as pltpu
from jax.sharding import PartitionSpec as P

C = 128
EMB = 512
GROUPS = 8
H = 64
W = 64
NCLASS = 16
STEP = 10
TAPS = 9
CELLS = H * W
PER_GROUP = CELLS * (C // GROUPS)
TABLE_ROWS = NCLASS * EMB // C
M1_ROWS = EMB * EMB // C
M2_ROWS = EMB * 2
MLP_ROWS = TABLE_ROWS + M1_ROWS + M2_ROWS
KERNEL_ROWS = TAPS * C
AXES = ("dp", "fsdp")

beta_one = 0.9
beta_two = 0.999
adam_eps = 1e-08
ema_decay = 0.99
norm_eps = 1e-05
rate_conv = 0.08
rate_table = 0.6
rate_dense = 0.1
rate_small = 0.15
decay_weights = 0.01

f32 = jnp.float32
bf16 = jnp.bfloat16
NN = (((1,), (0,)), ((), ()))
NT = (((1,), (1,)), ((), ()))
TN = (((0,), (0,)), ((), ()))
EXTRA = -(-(8 + 2 * NCLASS) // 16) * 16
PAIRS = ((2, 3), (1, 0))
R = 4
Q = 2
STEPS = H // R
PART = CELLS // STEPS


def each(count, step, carry):
    for index in range(count):
        carry = step(index, carry)
    return carry


def mm(a, b, dims=NN):
    return lax.dot_general(a, b, dims, preferred_element_type=f32)


def three(v):
    high = v.astype(bf16)
    rest = v - high.astype(f32)
    mid = rest.astype(bf16)
    return high, mid, (rest - mid.astype(f32)).astype(bf16)


def exact(values, weights, dims=NN):
    rows = values.shape[0]
    got = mm(jnp.concatenate(three(values), axis=0), weights, dims)
    return got[:rows] + got[rows : 2 * rows] + got[2 * rows :]


def group_sum(rows):
    lane = lax.broadcasted_iota(jnp.int32, rows.shape, 1)
    for step in (1, 2, 4, 8):
        up = pltpu.roll(rows, C - step, 1)
        down = pltpu.roll(rows, step, 1)
        rows = rows + jnp.where((lane & step) == 0, up, down)
    return rows


def fold(values):
    return jnp.sum(values.reshape(-1, 8, values.shape[-1]), axis=0)


def total_of(partial):
    return jnp.broadcast_to(jnp.sum(partial, axis=0, keepdims=True), partial.shape)


def one(rows):
    return rows[0:1].reshape(1, 1, C)


def normal_cdf(v):
    return 0.5 * (1.0 + lax.erf(v * 0.7071067811865476))


def gelu_slope(v, prob):
    return prob + v * (jnp.exp(-0.5 * v * v) * 0.3989422804014327)


def put_windows(win_ref, row, values):
    rows = values.shape[0]
    place = lax.broadcasted_iota(jnp.int32, values.shape, 1)
    left = jnp.where(place == 0, 0.0, pltpu.roll(values, 1, 1))
    right = jnp.where(place == W - 1, 0.0, pltpu.roll(values, W - 1, 1))
    win_ref[pl.ds(row + 1, rows), :, 0:C] = left.astype(bf16)
    win_ref[pl.ds(row + 1, rows), :, C : 2 * C] = values.astype(bf16)
    win_ref[pl.ds(row + 1, rows), :, 2 * C : 3 * C] = right.astype(bf16)


def clear_edges(win_ref):
    edge = jnp.zeros((1,) + tuple(win_ref.shape[1:]), win_ref.dtype)
    win_ref[0:1] = edge
    win_ref[H + 1 : H + 2] = edge


def pair_forward(pair_ref, kernel_ref):
    zero = jnp.zeros((3 * C, C), bf16)
    pair_ref[0 : TAPS * C, 0:C] = kernel_ref[...]
    pair_ref[TAPS * C :, 0:C] = zero
    pair_ref[0 : 3 * C, C:] = zero
    pair_ref[3 * C :, C:] = kernel_ref[...]


def flip(block):
    return jnp.transpose(block.astype(f32)).astype(bf16)


def pair_backward(pair_ref, kernel_ref):
    zero = jnp.zeros((3 * C, C), bf16)
    pair_ref[TAPS * C :, 0:C] = zero
    pair_ref[0 : 3 * C, C:] = zero
    for tap in range(TAPS):
        block = flip(kernel_ref[(TAPS - 1 - tap) * C : (TAPS - tap) * C, :])
        pair_ref[tap * C : (tap + 1) * C, 0:C] = block
        pair_ref[(tap + 3) * C : (tap + 4) * C, C:] = block


def pair_conv(win_ref, pair_ref, first):
    view = win_ref.reshape(H // 2 + 1, 2, W, 3 * C)
    taken = [view[pl.ds(first + t // 2, Q), t % 2] for t in range(4)]
    stacked = jnp.concatenate(taken, axis=-1).reshape(Q * W, 12 * C)
    return mm(stacked, pair_ref[...]).reshape(Q, W, 2 * C)


def pairs_of(ref, first):
    view = ref.reshape(H // 2, 2, W, C)
    return [view.at[pl.ds(first, Q), parity] for parity in range(2)]


def kernel_grad(act_ref, win_ref, out_ref):
    left = act_ref[1 : H + 1, :, C : 2 * C].reshape(CELLS, C)
    right = jnp.concatenate([win_ref[t : t + H] for t in range(3)], axis=-1)
    got = mm(left, right.reshape(CELLS, TAPS * C), TN)
    for t in range(TAPS):
        out_ref[t * C : (t + 1) * C, :] = got[:, (TAPS - 1 - t) * C : (TAPS - t) * C]


def position_of(sizes):
    (outer, _), (inner, inner_size) = sizes
    return lax.axis_index(outer) * inner_size + lax.axis_index(inner)


def prepare_body(x_ref, cot_ref, own_ref, stats_ref, cw, gdb_ref, near_ref):
    near_ref[...] = own_ref[...]
    zero8 = jnp.zeros((8, C), f32)

    def read_x(i):
        return x_ref[pl.ds(i * R, R)].astype(f32)

    total = each(H // R, lambda i, s: s + fold(read_x(i)), zero8)
    mean = group_sum(total_of(total)) * (1.0 / PER_GROUP)

    def square_x(i, s):
        d = read_x(i) - one(mean)
        return s + fold(d * d)

    var = group_sum(total_of(each(H // R, square_x, zero8))) * (1.0 / PER_GROUP)
    stats_ref[0:8] = mean
    stats_ref[8:16] = lax.rsqrt(var + norm_eps)
    cw[H // 2 : H // 2 + 1] = jnp.zeros((1, W // 2, 4 * C), bf16)

    def cot_windows(i, s):
        values = cot_ref[pl.ds(i * R, R)].astype(f32)
        place = lax.broadcasted_iota(jnp.int32, values.shape, 1)
        after = jnp.where(place == W // 2 - 1, 0.0, pltpu.roll(values, W // 2 - 1, 1))
        cw[pl.ds(i * R, R), :, 0 : 2 * C] = values.astype(bf16)
        cw[pl.ds(i * R, R), :, 2 * C :] = after.astype(bf16)
        return s + fold(values)

    gdb_ref[...] = total_of(each(H // 2 // R, cot_windows, jnp.zeros((8, 2 * C), f32)))


def run_prepare(x, cot, own):
    struct = jax.ShapeDtypeStruct
    return pl.pallas_call(
        prepare_body,
        out_shape=[struct((16, C), f32), struct((H // 2 + 1, W // 2, 4 * C), bf16), struct((8, 2 * C), f32), struct(own.shape, bf16)],
        in_specs=vmem_specs(3),
        out_specs=vmem_specs(4),
        compiler_params=limit(8),
        cost_estimate=cost(2, 3 << 20),
        name="prepare",
    )(x, cot, own)


def block_body(plan, *refs):
    refs = list(refs)
    count = 8 if plan.rings else 4
    cls_ref, x_ref, cot_ref, stats_ref, cw, gdb_ref = refs[:6]
    inputs = refs[6 : 6 + count]
    rw, kernels, smalls, slope1_ref, drf, factors_ref, table_ref, m1_ref, m2_ref, hidden_ref = refs[6 + count : 16 + count]
    results = refs[16 + count : 18 + count]
    a1w, a2w, t1w, t2w, c1, g1p, g2p, rf, pairs, conv, dense = refs[18 + count :]
    kernels_f = conv
    me = position_of(plan.sizes)
    k1_ref, k2_ref, kd0_ref, kd1_ref = [kernels.at[k] for k in range(4)]
    pair1, pair2, back1, back2 = [pairs.at[k] for k in range(4)]
    zero8 = jnp.zeros((8, C), f32)

    def take(k, part, place, owner):
        odd = owner & 1
        first = owner // 2 * plan.pair_rows
        full = plan.full
        mine = inputs[part][place, k * full : (k + 1) * full]
        mate = inputs[part + 4][place, k * full : (k + 1) * full]
        kernels_f[k, pl.ds(pl.multiple_of(first + (full + 8) * odd, 8), full), :] = mine.astype(f32)
        kernels_f[k, pl.ds(pl.multiple_of(first + (full + 8) * (1 - odd), 8), full), :] = mate.astype(f32)
        halves = [inputs[p][place, 4 * full : 4 * full + 16].astype(f32) for p in (part, part + 4)]
        halves = [v[8 * (k // 2) : 8 * (k // 2) + 8] for v in halves]
        if k % 2 == 1:
            halves = [pltpu.roll(v, 4, 0) for v in halves]
        kernels_f[k, pl.ds(pl.multiple_of(first + full, 8), 8), :] = jnp.where(own_half(odd), *halves)

    if plan.rings:
        shards = plan.sources(me)
        small = jnp.zeros((16, C), f32)
        row = lax.broadcasted_iota(jnp.int32, (16, C), 0)
        lane = lax.broadcasted_iota(jnp.int32, (16, C), 1)
        for part, place, owner in shards:
            take(0, part, place, owner)
            for p, device in ((part, owner), (part + 4, owner ^ 1)):
                at = row * C + lane - device * plan.small_len
                own = inputs[p][place, plan.small_at - 8 : plan.small_at + 8].astype(f32)[8:9]
                small = jnp.where((at >= 0) & (at < plan.small_len), jnp.broadcast_to(own, (16, C)), small)
        smalls[...] = small
        k1_ref[...] = kernels_f[0].astype(bf16)
    else:
        k1_ref[...] = inputs[0][...]
        smalls[0:14] = inputs[1][...].astype(f32)

    def take_rest(step, steps):
        if not plan.rings:
            return
        if step == 0:
            dense[...] = jnp.zeros(dense.shape, f32)
        for part, place, owner in shards[step::steps]:
            for k in (1, 2, 3):
                take(k, part, place, owner)
            for p, device in ((part, owner), (part + 4, owner ^ 1)):
                values = inputs[p][place, plan.dense_at : plan.small_at + 8].astype(f32)
                first = plan.tile_of(device * plan.dense_rows)
                dense[pl.ds(first, plan.dense_pad), :] += values[: plan.dense_pad]

    def small_row(index):
        return jnp.broadcast_to(smalls[index : index + 1, :], (8, C))

    def small_run(first, count):
        return jnp.concatenate([smalls[first + i : first + i + 1, :] for i in range(count)], axis=1)

    gain1, bias1, cb1, gain2, bias2, cb2 = [small_row(i) for i in range(6)]
    mean1, rs1 = stats_ref[0:8], stats_ref[8:16]
    slope1 = rs1 * (1.0 + gain1)

    pair_forward(pair1, k1_ref)
    clear_edges(a1w)

    def front1(i):
        v = (x_ref[pl.ds(i * R, R)].astype(f32) - one(mean1)) * one(slope1) + one(bias1)
        prob = normal_cdf(v)
        put_windows(a1w, i * R, v * prob)
        g1p[pl.ds(i * R, R)] = gelu_slope(v, prob)

    moments = []

    def conv1(i):
        got = pair_conv(a1w, pair1, i * Q)
        values = [got[..., parity * C : (parity + 1) * C] + one(cb1) for parity in range(2)]
        for place, value in zip(pairs_of(c1, i * Q), values):
            place[...] = value
        centre = total_of(fold(values[0]) + fold(values[1])) * (1.0 / PART)
        off = [value - one(centre) for value in values]
        moments.append((centre, fold(off[0] * off[0]) + fold(off[1] * off[1])))

    front1(0)
    for i in range(STEPS):
        if i + 1 < STEPS:
            front1(i + 1)
        conv1(i)
        take_rest(i, STEPS)
    centre = sum(part[0] for part in moments) * (1.0 / STEPS)
    spread = sum(total_of(part[1]) + PART * (part[0] - centre) * (part[0] - centre) for part in moments) * (1.0 / CELLS)

    if plan.rings:
        kernels[1:4] = conv[1:4].astype(bf16)
    else:
        kernels[1:4] = inputs[2][...]
        dense[0:MLP_ROWS] = inputs[3][...].astype(f32)

    def lanes(first, rows, parts):
        pieces = [dense[pl.ds(first + part, rows, parts), :] for part in range(parts)]
        return jnp.concatenate(pieces, axis=1).astype(bf16)

    table_ref[...] = lanes(0, NCLASS, EMB // C)
    m1_ref[...] = lanes(TABLE_ROWS, EMB, EMB // C)
    m2_ref[...] = lanes(TABLE_ROWS + M1_ROWS, EMB, 2)
    hidden = mm(table_ref[...], m1_ref[...]) + small_run(8, 4)
    hidden_ref[...] = hidden
    act = hidden * normal_cdf(hidden)
    ss = exact(act, m2_ref[...]) + small_run(12, 2)
    mine = lax.broadcasted_iota(jnp.int32, (NCLASS, 2 * C), 0) == cls_ref[0]
    chosen = jnp.sum(jnp.where(mine, ss, 0.0), axis=0, keepdims=True)
    scale = jnp.broadcast_to(1.0 + chosen[:, :C], (8, C))
    shift = jnp.broadcast_to(chosen[:, C:], (8, C))
    pair_forward(pair2, k2_ref)

    kd = jnp.concatenate([kd0_ref[...], kd1_ref[...]], axis=1)

    def tap(i, j):
        return flip(kd[(3 * i + j) * C : (3 * i + j + 1) * C, :])

    none = jnp.zeros((2 * C, C), bf16)
    even_rows = jnp.concatenate([
        jnp.concatenate([tap(1, 1), none], axis=0),
        jnp.concatenate([tap(1, 2), tap(1, 0)], axis=0),
    ], axis=1)
    odd_rows = jnp.concatenate([
        jnp.concatenate([tap(2, 1), none, tap(0, 1), none], axis=0),
        jnp.concatenate([tap(2, 2), tap(2, 0), tap(0, 2), tap(0, 0)], axis=0),
    ], axis=1)
    clear_edges(t2w)

    def back_down(i):
        rows = jnp.concatenate([cw[pl.ds(i * R, R)], cw[pl.ds(i * R + 1, R)]], axis=-1)
        rows = rows.reshape(R * W // 2, 8 * C)
        view = drf.reshape(H // 2, 2, W, C)
        for parity, got in enumerate((mm(rows[:, : 4 * C], even_rows), mm(rows, odd_rows))):
            got = got.reshape(R, W // 2, 2 * C)
            view[pl.ds(i * R, R), parity, pl.ds(0, W // 2, 2), :] = got[..., :C]
            view[pl.ds(i * R, R), parity, pl.ds(1, W // 2, 2), :] = got[..., C:]

    def t2_windows(i):
        values = drf[pl.ds(i * R, R)]
        put_windows(t2w, i * R, values)
        return fold(values)

    gcb2 = zero8
    for i in range(H // 2 // R):
        back_down(i)
        gcb2 = gcb2 + t2_windows(2 * i) + t2_windows(2 * i + 1)
    gcb2 = total_of(gcb2)

    centre_s = centre * scale + shift
    mean2 = group_sum(centre_s) * (GROUPS / C)
    off = centre_s - mean2
    var2 = group_sum(spread * scale * scale + off * off) * (GROUPS / C)
    rs2 = lax.rsqrt(var2 + norm_eps)

    def unit2(values):
        return (values * one(scale) + one(shift - mean2)) * one(rs2)

    clear_edges(a2w)

    def front2(i):
        v = unit2(c1[pl.ds(i * R, R)]) * one(1.0 + gain2) + one(bias2)
        prob = normal_cdf(v)
        put_windows(a2w, i * R, v * prob)
        g2p[pl.ds(i * R, R)] = gelu_slope(v, prob)

    rw[0:1] = jnp.zeros((1, W // 2, 3 * C), bf16)

    def conv2(i):
        got = pair_conv(a2w, pair2, i * Q)
        for parity, (place, source) in enumerate(zip(pairs_of(rf, i * Q), pairs_of(x_ref, i * Q))):
            r = source[...].astype(f32) + (got[..., parity * C : (parity + 1) * C] + one(cb2))
            place[...] = r.astype(bf16).astype(f32)
        even = rf[pl.ds(i * R, R), pl.ds(0, W // 2, 2), :]
        odd = rf[pl.ds(i * R, R), pl.ds(1, W // 2, 2), :]
        place = lax.broadcasted_iota(jnp.int32, odd.shape, 1)
        before = jnp.where(place == 0, 0.0, pltpu.roll(odd, 1, 1))
        rw[pl.ds(i * R + 1, R), :, 0:C] = before.astype(bf16)
        rw[pl.ds(i * R + 1, R), :, C : 2 * C] = even.astype(bf16)
        rw[pl.ds(i * R + 1, R), :, 2 * C :] = odd.astype(bf16)

    front2(0)
    for i in range(STEPS):
        if i + 1 < STEPS:
            front2(i + 1)
        conv2(i)

    gkd = mm(down_rows(rw, 0, H // 2), cot_ref[...].reshape(CELLS // 4, 2 * C), TN)
    conv[2] = gkd[:, :C]
    conv[3] = gkd[:, C:]

    def pull(i, s, win_ref, back_ref, slope_ref, out_slope_ref, units):
        got = pair_conv(win_ref, back_ref, i * Q)
        places = zip(pairs_of(slope_ref, i * Q), pairs_of(out_slope_ref, i * Q), units)
        for parity, (place, out_place, unit) in enumerate(places):
            dn = got[..., parity * C : (parity + 1) * C] * place[...]
            out_place[...] = dn
            s = s[0] + fold(dn), s[1] + fold(dn * unit)
        return s

    pair_backward(back2, k2_ref)
    sums = (zero8, zero8)
    for i in range(STEPS):
        sums = pull(i, sums, t2w, back2, g2p, g2p, [unit2(ref[...]) for ref in pairs_of(c1, i * Q)])
    gb2, gg2 = [total_of(part) for part in sums]
    mean_du2 = group_sum(gb2 * (1.0 + gain2)) * (1.0 / PER_GROUP)
    mean_duu2 = group_sum(gg2 * (1.0 + gain2)) * (1.0 / PER_GROUP)
    kernel_grad(a2w, t2w, conv.at[1])

    pair_backward(back1, k1_ref)
    clear_edges(t1w)

    def t1_windows(i, s):
        values = c1[pl.ds(i * R, R)]
        du = g2p[pl.ds(i * R, R)] * one(1.0 + gain2)
        ds = (du - one(mean_du2) - unit2(values) * one(mean_duu2)) * one(rs2)
        put_windows(t1w, i * R, ds * one(scale))
        return s[0] + fold(ds * values), s[1] + fold(ds)

    def unit1(ref):
        return (ref[...].astype(f32) - one(mean1)) * one(rs1)

    class_sums = t1_windows(0, (zero8, zero8))
    sums = (zero8, zero8)
    for i in range(STEPS):
        if i + 1 < STEPS:
            class_sums = t1_windows(i + 1, class_sums)
        sums = pull(i, sums, t1w, back1, g1p, slope1_ref, [unit1(ref) for ref in pairs_of(x_ref, i * Q)])
    gsc, gsh = [total_of(part) for part in class_sums]
    gb1, gg1 = [total_of(part) for part in sums]
    mean_du1 = group_sum(gb1 * (1.0 + gain1)) * (1.0 / PER_GROUP)
    mean_duu1 = group_sum(gg1 * (1.0 + gain1)) * (1.0 / PER_GROUP)
    for index, row in enumerate((1.0 + gain1, mean_du1, mean_duu1)):
        factors_ref[8 * index : 8 * index + 8] = row
    gdb = gdb_ref[...]
    rows = [gg1, gb1, gsh * scale, gg2, gb2, gcb2, gdb[:, :C], gdb[:, C:]]
    rows = [row[0:1] for row in rows]
    rows = rows + [jnp.where(mine[:, :C], row[0:1], 0.0) for row in (gsc, gsh)]
    extra = jnp.concatenate(rows + [jnp.zeros((EXTRA - len(rows) - 2 * NCLASS + 2, C), f32)], axis=0)
    if plan.rings:
        put_results(plan, me, 0, conv, *results)
        kernel_grad(a1w, t1w, conv.at[0])
        put_results(plan, me, 1, conv, *results)
        for ref in results:
            ref[plan.half * 2 * plan.pair_rows :] = extra.astype(ref.dtype)
    else:
        kernel_grad(a1w, t1w, conv.at[0])
        results[0][...] = conv[...]
        results[1][...] = extra


def down_rows(rw, first, rows):
    view = rw.reshape(H // 2 + 1, 2, W // 2, 3 * C)
    taken = [view[pl.ds(first + t // 2, rows), t % 2] for t in range(3)]
    return jnp.concatenate(taken, axis=-1).reshape(rows * W // 2, TAPS * C)


def down_body(rw, kernels, smalls, out_hbm, out_ref, sems):
    kd = jnp.concatenate([kernels[2], kernels[3]], axis=1)
    bias = jnp.concatenate([smalls[6:7, :], smalls[7:8, :]], axis=1)
    copies = []
    for part in range(4):
        rows = slice(part * H // 8, (part + 1) * H // 8)
        got = mm(down_rows(rw, part * H // 8, H // 8), kd) + bias
        out_ref[rows] = got.reshape(H // 8, W // 2, 2 * C).astype(bf16)
        copies.append(pltpu.make_async_copy(out_ref.at[rows], out_hbm.at[rows], sems.at[part]))
        copies[-1].start()
    for copy in copies:
        copy.wait()


def run_down(rw, kernels, smalls):
    shape = (H // 2, W // 2, 2 * C)
    return pl.pallas_call(
        down_body,
        out_shape=jax.ShapeDtypeStruct(shape, bf16),
        in_specs=vmem_specs(3),
        out_specs=pl.BlockSpec(memory_space=pltpu.HBM),
        scratch_shapes=[pltpu.VMEM(shape, bf16), pltpu.SemaphoreType.DMA((4,))],
        compiler_params=limit(8),
        cost_estimate=cost(604, 3 << 20),
        name="down",
    )(rw, kernels, smalls)


def finish_body(x_ref, stats_ref, slope_ref, grad_ref, factors_ref, dx_hbm, dx_ref, sems):
    mean, scale = stats_ref[0:8], stats_ref[8:16]
    gain, mean_du, mean_duu = [factors_ref[8 * k : 8 * k + 8] for k in range(3)]

    def finish(i, carry):
        du = slope_ref[pl.ds(i * R, R)] * one(gain)
        unit = (x_ref[pl.ds(i * R, R)].astype(f32) - one(mean)) * one(scale)
        dx = (du - one(mean_du) - unit * one(mean_duu)) * one(scale)
        dx_ref[pl.ds(i * R, R)] = (grad_ref[pl.ds(i * R, R)] + dx).astype(bf16)
        return carry

    copies = []
    for part in range(4):
        lax.fori_loop(part * H // R // 4, (part + 1) * H // R // 4, finish, 0)
        rows = pl.ds(part * H // 4, H // 4)
        copies.append(pltpu.make_async_copy(dx_ref.at[rows], dx_hbm.at[rows], sems.at[part]))
        copies[-1].start()
    for copy in copies:
        copy.wait()


def run_finish(x, stats, slope, grad, factors):
    return pl.pallas_call(
        finish_body,
        out_shape=jax.ShapeDtypeStruct((H, W, C), bf16),
        in_specs=vmem_specs(5),
        out_specs=pl.BlockSpec(memory_space=pltpu.HBM),
        scratch_shapes=[pltpu.VMEM((H, W, C), bf16), pltpu.SemaphoreType.DMA((4,))],
        compiler_params=limit(8),
        cost_estimate=cost(2, 6 << 20),
        name="finish",
    )(x, stats, slope, grad, factors)


def own_half(odd):
    return (lax.broadcasted_iota(jnp.int32, (8, C), 0) < 4) == (odd == 0)


def put_results(plan, me, index, conv, keep_ref, send_ref):
    left, right = PAIRS[index]
    for core, result in enumerate((keep_ref, send_ref)):
        odd = (me ^ core) & 1
        parts = []
        for owner in plan.targets(me ^ core):
            full, half = plan.places(odd, plan.tile_of(owner * plan.conv_rows))
            parts += [conv[k, pl.ds(full, plan.full), :] for k in (left, right)]
            halves = [conv[k, pl.ds(half, 8), :] for k in (left, right)]
            parts.append(jnp.where(own_half(odd), halves[0], pltpu.roll(halves[1], 4, 0)))
        rows = 2 * plan.pair_rows
        for place in range(0, plan.half, 2):
            two = jnp.concatenate(parts[3 * place : 3 * place + 6], axis=0)
            at = (index * plan.half + place) * plan.pair_rows
            result[at : at + rows] = two.astype(result.dtype)


def vmem_specs(count):
    return [pl.BlockSpec(memory_space=pltpu.VMEM)] * count


def cost(mflops, moved):
    return pl.CostEstimate(flops=mflops << 20, bytes_accessed=moved, transcendentals=0)


def limit(size):
    return pltpu.CompilerParams(vmem_limit_bytes=size << 20)


class Plan:
    def __init__(self, sizes, conv_len, dense_len, small_len):
        (_, outer_size), (_, inner_size) = sizes
        count = outer_size * inner_size
        self.sizes, self.line = sizes, inner_size // 2
        self.conv_len, self.dense_len, self.small_len = conv_len, dense_len, small_len
        self.conv_rows, self.dense_rows = conv_len // C, dense_len // C
        powers = inner_size & (inner_size - 1) == 0 and inner_size >= 4 and outer_size == 4
        self.rings = powers and conv_len % C == 0 and dense_len % C == 0 and small_len <= C and self.conv_rows % 8 == 4
        self.dense_pad = max(-(-(self.dense_rows * k % 8 + self.dense_rows) // 8) * 8 for k in range(count))
        self.full = self.conv_rows - 4
        self.window = self.conv_rows + 4
        self.pair_rows = 2 * self.conv_rows
        self.dense_at = 4 * self.full + 16
        self.small_at = self.dense_at + self.dense_pad
        self.own_rows = -(-(self.small_at + 8) // 16) * 16
        self.inner = inner_size
        self.half = count // 2

    def sources(self, me):
        near = [2 * k for k in range(self.line)]
        low, high = near[: self.line // 2], near[self.line // 2 :]
        held = [low + [k ^ self.inner for k in low], high + [k ^ 2 * self.inner for k in high]]
        held += [[k ^ 2 * self.inner for k in held[0]], [k ^ self.inner for k in held[1]]]
        return [(part, place, me ^ turn) for part, turns in enumerate(held) for place, turn in enumerate(turns)]

    def targets(self, own):
        return [own ^ (plane * self.inner + 2 * k) for plane in range(4) for k in range(self.line)]

    def tile_of(self, row):
        return pl.multiple_of(row // 8 * 8, 8)

    def places(self, odd, first=0):
        return pl.multiple_of(first + 8 * odd, 8), pl.multiple_of(first + self.full * (1 - odd), 8)


def run_block(plan, class_ids, x, cot, prepared, inputs):
    struct = jax.ShapeDtypeStruct
    shapes = [
        struct((H + 2, W // 2, 3 * C), bf16),
        struct((4, KERNEL_ROWS, C), bf16),
        struct((16, C), f32),
        struct((H, W, C), f32),
        struct((H, W, C), f32),
        struct((24, C), f32),
        struct((NCLASS, EMB), bf16),
        struct((EMB, EMB), bf16),
        struct((EMB, 2 * C), bf16),
        struct((NCLASS, EMB), f32),
    ]
    if plan.rings:
        rows = plan.half * 2 * plan.pair_rows
        shapes += [struct((rows + EXTRA, C), f32), struct((rows + EXTRA, C), bf16)]
    else:
        shapes += [struct((4, KERNEL_ROWS, C), f32), struct((EXTRA, C), f32)]
    windows = pltpu.VMEM((H + 2, W, 3 * C), bf16)
    plane = pltpu.VMEM((H, W, C), f32)
    return pl.pallas_call(
        functools.partial(block_body, plan),
        out_shape=shapes,
        in_specs=[pl.BlockSpec(memory_space=pltpu.SMEM)] + vmem_specs(5 + len(inputs)),
        out_specs=vmem_specs(12),
        scratch_shapes=[
            windows,
            windows,
            windows,
            windows,
            plane,
            plane,
            plane,
            plane,
            pltpu.VMEM((4, 12 * C, 2 * C), bf16),
            pltpu.VMEM((4, KERNEL_ROWS, C), f32),
            pltpu.VMEM((MLP_ROWS + 2 * plan.dense_pad, C), f32),
        ],
        compiler_params=limit(40),
        cost_estimate=cost(9000, 16 << 20),
        name="block",
    )(class_ids, x, cot, *prepared, *inputs)


def pack_body(plan, conv_hbm, dense_hbm, small_hbm, out_ref, conv_ref, dense_ref, small_ref, windows, rows, sems):
    pairs = ((conv_hbm.at[0], conv_ref), (dense_hbm, dense_ref), (small_hbm, small_ref))
    copies = [pltpu.make_async_copy(source, target, sems.at[k]) for k, (source, target) in enumerate(pairs)]
    for copy in copies:
        copy.start()
    me = position_of(plan.sizes)
    odd = me & 1
    windows[...] = jnp.zeros(windows.shape, f32)
    rows[...] = jnp.zeros(rows.shape, f32)
    copies[0].wait()
    for r in range(plan.conv_rows):
        for k in range(4):
            windows[pl.ds(k * plan.window + 4 * odd + r, 1), :] = conv_ref[k : k + 1, r * C : (r + 1) * C]
    halves = []
    for k in range(4):
        full, half = plan.places(odd, k * plan.window)
        rows[k * plan.full : (k + 1) * plan.full] = windows[pl.ds(full, plan.full), :]
        halves.append(windows[pl.ds(half, 8), :])
    for k in (0, 2):
        at = 4 * plan.full + 4 * k
        rows[at : at + 8] = jnp.where(own_half(odd), halves[k], pltpu.roll(halves[k + 1], 4, 0))
    copies[1].wait()
    first = plan.dense_at + me * plan.dense_rows % 8
    for r in range(plan.dense_rows):
        rows[pl.ds(first + r, 1), :] = dense_ref[0:1, r * C : (r + 1) * C]
    copies[2].wait()
    own = jnp.concatenate([small_ref[0:1, :], jnp.zeros((1, C - plan.small_len), f32)], axis=1)
    own = pltpu.roll(jnp.broadcast_to(own, (8, C)), me * plan.small_len % C, 1)
    rows[plan.small_at : plan.small_at + 1] = own[0:1]
    out_ref[...] = rows[...].astype(bf16)


def run_pack(plan, conv_state, mlp_state, small_state):
    return pl.pallas_call(
        functools.partial(pack_body, plan),
        out_shape=jax.ShapeDtypeStruct((plan.own_rows, C), bf16),
        in_specs=[pl.BlockSpec(memory_space=pltpu.HBM)] * 3,
        out_specs=pl.BlockSpec(memory_space=pltpu.VMEM),
        scratch_shapes=[
            pltpu.VMEM((4, plan.conv_len), f32),
            pltpu.VMEM((4, plan.dense_len), f32),
            pltpu.VMEM((4, plan.small_len), f32),
            pltpu.VMEM((4 * plan.window, C), f32),
            pltpu.VMEM((plan.own_rows, C), f32),
            pltpu.SemaphoreType.DMA((3,)),
        ],
        compiler_params=pltpu.CompilerParams(vmem_limit_bytes=(64 << 20) - (190 << 10)),
        name="pack",
    )(conv_state, mlp_state, small_state)


def merge_body(plan, blocks, groups, *refs):
    keep_ref, received = refs[0], refs[1 : len(refs) - groups]
    outs = refs[len(refs) - groups :]

    def sums(at, size):
        total = keep_ref[at : at + size]
        for ref in received:
            total = total + ref[at : at + size].astype(f32)
        return total

    size = blocks // groups * plan.pair_rows
    extra = sums(2 * blocks * plan.pair_rows, EXTRA)
    for group, out in enumerate(outs):
        parts = [sums(k * blocks * plan.pair_rows + group * size, size) for k in range(2)]
        out[...] = jnp.concatenate(parts + [extra], axis=0).astype(out.dtype)


def run_merge(plan, blocks, groups, keep, received):
    rows = blocks // groups * 2 * plan.pair_rows + EXTRA
    shapes = [jax.ShapeDtypeStruct((rows, C), f32 if group == 0 else bf16) for group in range(groups)]
    return pl.pallas_call(
        functools.partial(merge_body, plan, blocks, groups),
        out_shape=shapes,
        in_specs=vmem_specs(1 + len(received)),
        out_specs=vmem_specs(groups),
        compiler_params=limit(16),
        name="merge",
    )(keep, *received)


def mlp_grads(table, m1_ref, m2_ref, hidden, dss, out_ref):
    prob = normal_cdf(hidden)

    def put(first, values):
        parts = values.shape[1] // C
        for part in range(parts):
            out_ref[pl.ds(first + part, values.shape[0], parts), :] = values[:, part * C : (part + 1) * C]

    def outer(left, right):
        lefts = [a for k, a in enumerate(left) for b in right[: 3 - k]]
        rights = [b for k, a in enumerate(left) for b in right[: 3 - k]]
        return mm(jnp.concatenate(lefts, axis=0), jnp.concatenate(rights, axis=0), TN)

    dp = exact(dss, m2_ref[...], NT) * gelu_slope(hidden, prob)
    put(0, exact(dp, m1_ref[...], NT))
    put(TABLE_ROWS, outer([table], three(dp)))
    put(TABLE_ROWS + M1_ROWS, outer(three(hidden * prob), three(dss)))
    ge1 = jnp.sum(dp, axis=0, keepdims=True)
    ge2 = jnp.sum(dss, axis=0, keepdims=True)
    return [ge1[:, i * C : (i + 1) * C] for i in range(4)] + [ge2[:, i * C : (i + 1) * C] for i in range(2)]


def mlp_body(table_ref, m1_ref, m2_ref, hidden_ref, dss_ref, out_ref, tail_ref):
    tail = mlp_grads(table_ref[...], m1_ref, m2_ref, hidden_ref[...], dss_ref[...], out_ref)
    for i, row in enumerate(tail):
        tail_ref[i : i + 1, :] = row


def run_mlp(table, m1, m2, hidden, dss):
    return pl.pallas_call(
        mlp_body,
        out_shape=[jax.ShapeDtypeStruct((MLP_ROWS, C), f32), jax.ShapeDtypeStruct((6, C), f32)],
        in_specs=vmem_specs(5),
        out_specs=vmem_specs(2),
        compiler_params=limit(32),
        name="mlp_grad",
    )(table, m1, m2, hidden, dss)


def adam(weight, first, second, average, gradient, rate, decay):
    first = beta_one * first + (1.0 - beta_one) * gradient
    second = beta_two * second + (1.0 - beta_two) * gradient * gradient
    first_hat = first * (1.0 / (1.0 - beta_one**STEP))
    second_hat = second * (1.0 / (1.0 - beta_two**STEP))
    weight = weight - rate * (first_hat / (jnp.sqrt(second_hat) + adam_eps) + decay * weight)
    return weight, first, second, ema_decay * average + (1.0 - ema_decay) * weight


def update_body(plan, received_count, *refs):
    keep_ref, received = refs[0], refs[1 : 1 + received_count]
    table_ref, m1_ref, m2_ref, hidden_ref, conv_ref, dense_ref, small_ref = refs[1 + received_count : 8 + received_count]
    conv_new, dense_new, small_new, conv_copy, dense_copy, small_copy = refs[8 + received_count : 14 + received_count]
    block, grads, rows, smalls = refs[14 + received_count :]
    me = position_of(plan.sizes)
    total = keep_ref[...]
    for ref in received:
        total = total + ref[...].astype(f32)
    odd = me & 1
    for index, pair in enumerate(PAIRS):
        at = index * plan.pair_rows
        rest = total[at + 2 * plan.full : at + plan.pair_rows]
        for side, k in enumerate(pair):
            full, half = plan.places(odd, k * plan.window)
            block[pl.ds(full, plan.full), :] = total[at + side * plan.full : at + (side + 1) * plan.full]
            block[pl.ds(half, 8), :] = pltpu.roll(rest, 4, 0) if side else rest
    extra = total[2 * plan.pair_rows :]
    smalls[0:8] = extra[0:8]
    dss = jnp.concatenate([extra[8 : 8 + NCLASS], extra[8 + NCLASS : 8 + 2 * NCLASS]], axis=1)
    tail = mlp_grads(table_ref[...], m1_ref, m2_ref, hidden_ref[...], dss, grads)
    for i, row in enumerate(tail):
        smalls[8 + i : 9 + i, :] = row

    for r in range(plan.conv_rows):
        at = slice(r * C, (r + 1) * C)
        gradient = block[pl.ds(4 * odd + r, 4, plan.window), :]
        new = adam(*[conv_ref[k, :, at] for k in range(4)], gradient, rate_conv, decay_weights)
        for k in range(4):
            conv_new[k, :, at] = new[k]
        conv_copy[:, at] = new[0].astype(bf16)

    start = me * plan.dense_rows
    for r in range(plan.dense_rows):
        at = slice(r * C, (r + 1) * C)
        gradient = grads[pl.ds(start + r, 1), :]
        rate = jnp.where(start + r < TABLE_ROWS, rate_table, rate_dense)
        new = adam(*[dense_ref[k : k + 1, at] for k in range(4)], gradient, rate, decay_weights)
        for k in range(4):
            dense_new[k : k + 1, at] = new[k]
        rows[r : r + 1, :] = new[0]
    dense_copy[...] = rows[...].astype(bf16)

    start = me * plan.small_len
    lane = lax.broadcasted_iota(jnp.int32, (8, C), 1)
    near = jnp.broadcast_to(smalls[pl.ds(start // C, 1), :], (8, C))
    far = jnp.broadcast_to(smalls[pl.ds(start // C + 1, 1), :], (8, C))
    off = C - start % C
    gradient = jnp.where(lane < off, pltpu.roll(near, off, 1), pltpu.roll(far, off, 1))
    gradient = gradient[0:1, 0 : plan.small_len]
    new = adam(*[small_ref[k : k + 1, :] for k in range(4)], gradient, rate_small, 0.0)
    for k in range(4):
        small_new[k : k + 1, :] = new[k]
    small_copy[...] = new[0].astype(bf16)


def run_update(plan, keep, received, mlp, states):
    struct = jax.ShapeDtypeStruct
    shapes = [struct(state.shape, f32) for state in states]
    shapes += [struct((4, plan.conv_len), bf16), struct((plan.dense_rows, C), bf16), struct((1, plan.small_len), bf16)]
    return pl.pallas_call(
        functools.partial(update_body, plan, len(received)),
        out_shape=shapes,
        in_specs=vmem_specs(1 + len(received) + 4 + 3),
        out_specs=vmem_specs(6),
        scratch_shapes=[
            pltpu.VMEM((4 * plan.window, C), f32),
            pltpu.VMEM((MLP_ROWS, C), f32),
            pltpu.VMEM((plan.dense_rows, C), f32),
            pltpu.VMEM((24, C), f32),
        ],
        compiler_params=limit(24),
        name="update",
    )(keep, *received, *mlp, *states)


def swap(values, axis, size, turn):
    return lax.ppermute(values, axis, [(i, i ^ turn) for i in range(size)])


def gather_ring(plan, own, prepare):
    (outer, outer_size), (inner, inner_size) = plan.sizes
    line = [swap(own, inner, inner_size, 2 * k) for k in range(1, plan.line)]
    line, (*prepared, own) = lax.optimization_barrier((line, prepare(own)))
    line = [own] + line
    half = plan.line // 2
    held = []
    for part, turn in ((jnp.stack(line[:half]), 1), (jnp.stack(line[half:]), 2)):
        held.append(jnp.concatenate([part, swap(part, outer, outer_size, turn)]))
    held = held + [swap(part, outer, outer_size, 2 - k) for k, part in enumerate(held)]
    return prepared, held + [swap(part, inner, inner_size, 1) for part in held]


def reduce_ring(plan, keep, send, beside):
    (outer, outer_size), (inner, inner_size) = plan.sizes
    received = [swap(send, inner, inner_size, 1)]
    keep, *sends = run_merge(plan, outer_size * plan.line, outer_size, keep, received)
    received = [swap(part, outer, outer_size, k + 1) for k, part in enumerate(sends)]
    received, beside = lax.optimization_barrier((received, beside))
    keep, *sends = run_merge(plan, plan.line, plan.line, keep, received)
    return beside, keep, [swap(part, inner, inner_size, 2 * (k + 1)) for k, part in enumerate(sends)]


def plain_update(plan, position, grads, extra, mlp, states):
    conv_state, mlp_state, small_state = states
    conv_red = lax.psum_scatter(grads.reshape(4, -1), AXES, scatter_dimension=1, tiled=True)
    extra = lax.psum(extra, AXES)
    dss = jnp.concatenate([extra[8 : 8 + NCLASS], extra[8 + NCLASS : 8 + 2 * NCLASS]], axis=1)
    dense_grad, tail = run_mlp(*mlp, dss)
    dense_red = lax.dynamic_slice_in_dim(dense_grad.reshape(-1), position * plan.dense_len, plan.dense_len)
    flat = jnp.concatenate([extra[:8], tail]).reshape(-1)
    small_red = lax.dynamic_slice_in_dim(flat, position * plan.small_len, plan.small_len)
    flat_index = position * plan.dense_len + jnp.arange(plan.dense_len, dtype=jnp.int32)
    dense_rate = jnp.where(flat_index < NCLASS * EMB, rate_table, rate_dense)
    new = [
        jnp.stack(adam(*state, red, rate, decay))
        for state, red, rate, decay in (
            (conv_state, conv_red, rate_conv, decay_weights),
            (mlp_state, dense_red, dense_rate, decay_weights),
            (small_state, small_red, rate_small, 0.0),
        )
    ]
    return new + [state[0].astype(bf16) for state in new]


def per_device(sizes, samples, cotangent, class_ids, *states):
    conv_state, mlp_state, small_state = states
    plan = Plan(sizes, conv_state.shape[2], mlp_state.shape[1], small_state.shape[1])
    x, cot = samples[0], cotangent[0]
    if plan.rings:
        prepared, inputs = gather_ring(plan, run_pack(plan, *states), lambda own: run_prepare(x, cot, own))
    else:
        conv, dense, small = [state[0].astype(bf16) for state in states]
        conv = lax.all_gather(conv, AXES, axis=1, tiled=True).reshape(4, KERNEL_ROWS, C)
        small = lax.all_gather(small, AXES, axis=0, tiled=True).reshape(-1, C)
        dense = lax.all_gather(dense, AXES, axis=0, tiled=True).reshape(MLP_ROWS, C)
        inputs = [conv[0], small, conv[1:], dense]
        prepared = run_prepare(x, cot, small)[:3]
    rw, kernels, smalls, slope, grad, factors, table, m1, m2, hidden, first, second = run_block(
        plan, class_ids, x, cot, prepared, inputs
    )
    out = run_down(rw, kernels, smalls)
    dx = run_finish(x, prepared[0], slope, grad, factors)
    mlp = (table, m1, m2, hidden)
    if plan.rings:
        (out, dx), keep, received = reduce_ring(plan, first, second, (out, dx))
        results = run_update(plan, keep, received, mlp, states)
    else:
        results = plain_update(plan, lax.axis_index(AXES), first, second, mlp, states)
    conv_new, mlp_new, small_new, conv_copy, mlp_copy, small_copy = results
    return out[None], dx[None], conv_new, mlp_new, small_new, conv_copy, mlp_copy.reshape(-1), small_copy.reshape(-1)


def solution(mesh):
    sizes = tuple((axis, mesh.shape[axis]) for axis in AXES)

    def body(*args):
        return per_device(sizes, *args)

    return jax.shard_map(
        body,
        mesh=mesh,
        in_specs=(
            P(AXES, None, None, None),
            P(AXES, None, None, None),
            P(AXES),
            P(None, None, AXES),
            P(None, AXES),
            P(None, AXES),
        ),
        out_specs=(
            P(AXES, None, None, None),
            P(AXES, None, None, None),
            P(None, None, AXES),
            P(None, AXES),
            P(None, AXES),
            P(None, AXES),
            P(AXES),
            P(AXES),
        ),
        check_vma=False,
    )
```

```python
import functools

import jax
import jax.numpy as jnp
from jax import lax
from jax.experimental import pallas as pl
from jax.experimental.pallas import tpu as pltpu
from jax.sharding import PartitionSpec as P

C = 128
EMB = 512
GROUPS = 8
H = 64
W = 64
NCLASS = 16
STEP = 10
TAPS = 9
CELLS = H * W
PER_GROUP = CELLS * (C // GROUPS)
TABLE_ROWS = NCLASS * EMB // C
M1_ROWS = EMB * EMB // C
M2_ROWS = EMB * 2
MLP_ROWS = TABLE_ROWS + M1_ROWS + M2_ROWS
KERNEL_ROWS = TAPS * C
AXES = ("dp", "fsdp")

beta_one = 0.9
beta_two = 0.999
adam_eps = 1e-08
ema_decay = 0.99
norm_eps = 1e-05
rate_conv = 0.08
rate_table = 0.6
rate_dense = 0.1
rate_small = 0.15
decay_weights = 0.01

f32 = jnp.float32
bf16 = jnp.bfloat16
NN = (((1,), (0,)), ((), ()))
NT = (((1,), (1,)), ((), ()))
TN = (((0,), (0,)), ((), ()))
EXTRA = -(-(8 + 2 * NCLASS) // 16) * 16
PAIRS = ((2, 3), (1, 0))
R = 4
Q = 2
STEPS = H // R
PART = CELLS // STEPS


def each(count, step, carry):
    for index in range(count):
        carry = step(index, carry)
    return carry


def mm(a, b, dims=NN):
    return lax.dot_general(a, b, dims, preferred_element_type=f32)


def three(v):
    high = v.astype(bf16)
    rest = v - high.astype(f32)
    mid = rest.astype(bf16)
    return high, mid, (rest - mid.astype(f32)).astype(bf16)


def exact(values, weights, dims=NN):
    rows = values.shape[0]
    got = mm(jnp.concatenate(three(values), axis=0), weights, dims)
    return got[:rows] + got[rows : 2 * rows] + got[2 * rows :]


def group_sum(rows):
    lane = lax.broadcasted_iota(jnp.int32, rows.shape, 1)
    for step in (1, 2, 4, 8):
        up = pltpu.roll(rows, C - step, 1)
        down = pltpu.roll(rows, step, 1)
        rows = rows + jnp.where((lane & step) == 0, up, down)
    return rows


def fold(values):
    return jnp.sum(values.reshape(-1, 8, values.shape[-1]), axis=0)


def total_of(partial):
    return jnp.broadcast_to(jnp.sum(partial, axis=0, keepdims=True), partial.shape)


def one(rows):
    return rows[0:1].reshape(1, 1, C)


def normal_cdf(v):
    return 0.5 * (1.0 + lax.erf(v * 0.7071067811865476))


def gelu_slope(v, prob):
    return prob + v * (jnp.exp(-0.5 * v * v) * 0.3989422804014327)


def put_windows(win_ref, row, values):
    rows = values.shape[0]
    place = lax.broadcasted_iota(jnp.int32, values.shape, 1)
    left = jnp.where(place == 0, 0.0, pltpu.roll(values, 1, 1))
    right = jnp.where(place == W - 1, 0.0, pltpu.roll(values, W - 1, 1))
    win_ref[pl.ds(row + 1, rows), :, 0:C] = left.astype(bf16)
    win_ref[pl.ds(row + 1, rows), :, C : 2 * C] = values.astype(bf16)
    win_ref[pl.ds(row + 1, rows), :, 2 * C : 3 * C] = right.astype(bf16)


def clear_edges(win_ref):
    edge = jnp.zeros((1,) + tuple(win_ref.shape[1:]), win_ref.dtype)
    win_ref[0:1] = edge
    win_ref[H + 1 : H + 2] = edge


def pair_forward(pair_ref, kernel_ref):
    zero = jnp.zeros((3 * C, C), bf16)
    pair_ref[0 : TAPS * C, 0:C] = kernel_ref[...]
    pair_ref[TAPS * C :, 0:C] = zero
    pair_ref[0 : 3 * C, C:] = zero
    pair_ref[3 * C :, C:] = kernel_ref[...]


def flip(block):
    return jnp.transpose(block.astype(f32)).astype(bf16)


def pair_backward(pair_ref, kernel_ref):
    zero = jnp.zeros((3 * C, C), bf16)
    pair_ref[TAPS * C :, 0:C] = zero
    pair_ref[0 : 3 * C, C:] = zero
    for tap in range(TAPS):
        block = flip(kernel_ref[(TAPS - 1 - tap) * C : (TAPS - tap) * C, :])
        pair_ref[tap * C : (tap + 1) * C, 0:C] = block
        pair_ref[(tap + 3) * C : (tap + 4) * C, C:] = block


def pair_conv(win_ref, pair_ref, first):
    view = win_ref.reshape(H // 2 + 1, 2, W, 3 * C)
    taken = [view[pl.ds(first + t // 2, Q), t % 2] for t in range(4)]
    stacked = jnp.concatenate(taken, axis=-1).reshape(Q * W, 12 * C)
    return mm(stacked, pair_ref[...]).reshape(Q, W, 2 * C)


def pairs_of(ref, first):
    view = ref.reshape(H // 2, 2, W, C)
    return [view.at[pl.ds(first, Q), parity] for parity in range(2)]


def kernel_grad(act_ref, win_ref, out_ref):
    left = act_ref[1 : H + 1, :, C : 2 * C].reshape(CELLS, C)
    right = jnp.concatenate([win_ref[t : t + H] for t in range(3)], axis=-1)
    got = mm(left, right.reshape(CELLS, TAPS * C), TN)
    for t in range(TAPS):
        out_ref[t * C : (t + 1) * C, :] = got[:, (TAPS - 1 - t) * C : (TAPS - t) * C]


def position_of(sizes):
    (outer, _), (inner, inner_size) = sizes
    return lax.axis_index(outer) * inner_size + lax.axis_index(inner)


def prepare_body(x_ref, cot_ref, own_ref, stats_ref, cw, gdb_ref, near_ref):
    near_ref[...] = own_ref[...]
    zero8 = jnp.zeros((8, C), f32)

    def read_x(i):
        return x_ref[pl.ds(i * R, R)].astype(f32)

    total = each(H // R, lambda i, s: s + fold(read_x(i)), zero8)
    mean = group_sum(total_of(total)) * (1.0 / PER_GROUP)

    def square_x(i, s):
        d = read_x(i) - one(mean)
        return s + fold(d * d)

    var = group_sum(total_of(each(H // R, square_x, zero8))) * (1.0 / PER_GROUP)
    stats_ref[0:8] = mean
    stats_ref[8:16] = lax.rsqrt(var + norm_eps)
    cw[H // 2 : H // 2 + 1] = jnp.zeros((1, W // 2, 4 * C), bf16)

    def cot_windows(i, s):
        values = cot_ref[pl.ds(i * R, R)].astype(f32)
        place = lax.broadcasted_iota(jnp.int32, values.shape, 1)
        after = jnp.where(place == W // 2 - 1, 0.0, pltpu.roll(values, W // 2 - 1, 1))
        cw[pl.ds(i * R, R), :, 0 : 2 * C] = values.astype(bf16)
        cw[pl.ds(i * R, R), :, 2 * C :] = after.astype(bf16)
        return s + fold(values)

    gdb_ref[...] = total_of(each(H // 2 // R, cot_windows, jnp.zeros((8, 2 * C), f32)))


def run_prepare(x, cot, own):
    struct = jax.ShapeDtypeStruct
    return pl.pallas_call(
        prepare_body,
        out_shape=[struct((16, C), f32), struct((H // 2 + 1, W // 2, 4 * C), bf16), struct((8, 2 * C), f32), struct(own.shape, bf16)],
        in_specs=vmem_specs(3),
        out_specs=vmem_specs(4),
        compiler_params=limit(8),
        cost_estimate=cost(2, 3 << 20),
        name="prepare",
    )(x, cot, own)


def block_body(plan, *refs):
    refs = list(refs)
    count = 8 if plan.rings else 4
    cls_ref, x_ref, cot_ref, stats_ref, cw, gdb_ref = refs[:6]
    inputs = refs[6 : 6 + count]
    rw, kernels, smalls, slope1_ref, drf, factors_ref, table_ref, m1_ref, m2_ref, hidden_ref = refs[6 + count : 16 + count]
    results = refs[16 + count : 18 + count]
    a1w, a2w, t1w, t2w, c1, g1p, g2p, rf, pairs, conv, dense = refs[18 + count :]
    kernels_f = conv
    me = position_of(plan.sizes)
    k1_ref, k2_ref, kd0_ref, kd1_ref = [kernels.at[k] for k in range(4)]
    pair1, pair2, back1, back2 = [pairs.at[k] for k in range(4)]
    zero8 = jnp.zeros((8, C), f32)

    def take(k, part, place, owner):
        odd = owner & 1
        first = owner // 2 * plan.pair_rows
        full = plan.full
        mine = inputs[part][place, k * full : (k + 1) * full]
        mate = inputs[part + 4][place, k * full : (k + 1) * full]
        kernels_f[k, pl.ds(pl.multiple_of(first + (full + 8) * odd, 8), full), :] = mine.astype(f32)
        kernels_f[k, pl.ds(pl.multiple_of(first + (full + 8) * (1 - odd), 8), full), :] = mate.astype(f32)
        halves = [inputs[p][place, 4 * full : 4 * full + 16].astype(f32) for p in (part, part + 4)]
        halves = [v[8 * (k // 2) : 8 * (k // 2) + 8] for v in halves]
        if k % 2 == 1:
            halves = [pltpu.roll(v, 4, 0) for v in halves]
        kernels_f[k, pl.ds(pl.multiple_of(first + full, 8), 8), :] = jnp.where(own_half(odd), *halves)

    if plan.rings:
        shards = plan.sources(me)
        small = jnp.zeros((16, C), f32)
        row = lax.broadcasted_iota(jnp.int32, (16, C), 0)
        lane = lax.broadcasted_iota(jnp.int32, (16, C), 1)
        for part, place, owner in shards:
            take(0, part, place, owner)
            for p, device in ((part, owner), (part + 4, owner ^ 1)):
                at = row * C + lane - device * plan.small_len
                own = inputs[p][place, plan.small_at - 8 : plan.small_at + 8].astype(f32)[8:9]
                small = jnp.where((at >= 0) & (at < plan.small_len), jnp.broadcast_to(own, (16, C)), small)
        smalls[...] = small
        k1_ref[...] = kernels_f[0].astype(bf16)
    else:
        k1_ref[...] = inputs[0][...]
        smalls[0:14] = inputs[1][...].astype(f32)

    def take_rest(step, steps):
        if not plan.rings:
            return
        if step == 0:
            dense[...] = jnp.zeros(dense.shape, f32)
        for part, place, owner in shards[step::steps]:
            for k in (1, 2, 3):
                take(k, part, place, owner)
            for p, device in ((part, owner), (part + 4, owner ^ 1)):
                values = inputs[p][place, plan.dense_at : plan.small_at + 8].astype(f32)
                first = plan.tile_of(device * plan.dense_rows)
                dense[pl.ds(first, plan.dense_pad), :] += values[: plan.dense_pad]

    def small_row(index):
        return jnp.broadcast_to(smalls[index : index + 1, :], (8, C))

    def small_run(first, count):
        return jnp.concatenate([smalls[first + i : first + i + 1, :] for i in range(count)], axis=1)

    gain1, bias1, cb1, gain2, bias2, cb2 = [small_row(i) for i in range(6)]
    mean1, rs1 = stats_ref[0:8], stats_ref[8:16]
    slope1 = rs1 * (1.0 + gain1)

    pair_forward(pair1, k1_ref)
    clear_edges(a1w)

    def front1(i):
        v = (x_ref[pl.ds(i * R, R)].astype(f32) - one(mean1)) * one(slope1) + one(bias1)
        prob = normal_cdf(v)
        put_windows(a1w, i * R, v * prob)
        g1p[pl.ds(i * R, R)] = gelu_slope(v, prob)

    moments = []

    def conv1(i):
        got = pair_conv(a1w, pair1, i * Q)
        values = [got[..., parity * C : (parity + 1) * C] + one(cb1) for parity in range(2)]
        for place, value in zip(pairs_of(c1, i * Q), values):
            place[...] = value
        centre = total_of(fold(values[0]) + fold(values[1])) * (1.0 / PART)
        off = [value - one(centre) for value in values]
        moments.append((centre, fold(off[0] * off[0]) + fold(off[1] * off[1])))

    front1(0)
    for i in range(STEPS):
        if i + 1 < STEPS:
            front1(i + 1)
        conv1(i)
        take_rest(i, STEPS)
    centre = sum(part[0] for part in moments) * (1.0 / STEPS)
    spread = sum(total_of(part[1]) + PART * (part[0] - centre) * (part[0] - centre) for part in moments) * (1.0 / CELLS)

    if plan.rings:
        kernels[1:4] = conv[1:4].astype(bf16)
    else:
        kernels[1:4] = inputs[2][...]
        dense[0:MLP_ROWS] = inputs[3][...].astype(f32)

    def lanes(first, rows, parts):
        pieces = [dense[pl.ds(first + part, rows, parts), :] for part in range(parts)]
        return jnp.concatenate(pieces, axis=1).astype(bf16)

    table_ref[...] = lanes(0, NCLASS, EMB // C)
    m1_ref[...] = lanes(TABLE_ROWS, EMB, EMB // C)
    m2_ref[...] = lanes(TABLE_ROWS + M1_ROWS, EMB, 2)
    hidden = mm(table_ref[...], m1_ref[...]) + small_run(8, 4)
    hidden_ref[...] = hidden
    act = hidden * normal_cdf(hidden)
    ss = exact(act, m2_ref[...]) + small_run(12, 2)
    mine = lax.broadcasted_iota(jnp.int32, (NCLASS, 2 * C), 0) == cls_ref[0]
    chosen = jnp.sum(jnp.where(mine, ss, 0.0), axis=0, keepdims=True)
    scale = jnp.broadcast_to(1.0 + chosen[:, :C], (8, C))
    shift = jnp.broadcast_to(chosen[:, C:], (8, C))
    pair_forward(pair2, k2_ref)

    kd = jnp.concatenate([kd0_ref[...], kd1_ref[...]], axis=1)

    def tap(i, j):
        return flip(kd[(3 * i + j) * C : (3 * i + j + 1) * C, :])

    none = jnp.zeros((2 * C, C), bf16)
    even_rows = jnp.concatenate([
        jnp.concatenate([tap(1, 1), none], axis=0),
        jnp.concatenate([tap(1, 2), tap(1, 0)], axis=0),
    ], axis=1)
    odd_rows = jnp.concatenate([
        jnp.concatenate([tap(2, 1), none, tap(0, 1), none], axis=0),
        jnp.concatenate([tap(2, 2), tap(2, 0), tap(0, 2), tap(0, 0)], axis=0),
    ], axis=1)
    clear_edges(t2w)

    def back_down(i):
        rows = jnp.concatenate([cw[pl.ds(i * R, R)], cw[pl.ds(i * R + 1, R)]], axis=-1)
        rows = rows.reshape(R * W // 2, 8 * C)
        view = drf.reshape(H // 2, 2, W, C)
        for parity, got in enumerate((mm(rows[:, : 4 * C], even_rows), mm(rows, odd_rows))):
            got = got.reshape(R, W // 2, 2 * C)
            view[pl.ds(i * R, R), parity, pl.ds(0, W // 2, 2), :] = got[..., :C]
            view[pl.ds(i * R, R), parity, pl.ds(1, W // 2, 2), :] = got[..., C:]

    def t2_windows(i):
        values = drf[pl.ds(i * R, R)]
        put_windows(t2w, i * R, values)
        return fold(values)

    gcb2 = zero8
    for i in range(H // 2 // R):
        back_down(i)
        gcb2 = gcb2 + t2_windows(2 * i) + t2_windows(2 * i + 1)
    gcb2 = total_of(gcb2)

    centre_s = centre * scale + shift
    mean2 = group_sum(centre_s) * (GROUPS / C)
    off = centre_s - mean2
    var2 = group_sum(spread * scale * scale + off * off) * (GROUPS / C)
    rs2 = lax.rsqrt(var2 + norm_eps)

    def unit2(values):
        return (values * one(scale) + one(shift - mean2)) * one(rs2)

    clear_edges(a2w)

    def front2(i):
        v = unit2(c1[pl.ds(i * R, R)]) * one(1.0 + gain2) + one(bias2)
        prob = normal_cdf(v)
        put_windows(a2w, i * R, v * prob)
        g2p[pl.ds(i * R, R)] = gelu_slope(v, prob)

    rw[0:1] = jnp.zeros((1, W // 2, 3 * C), bf16)

    def conv2(i):
        got = pair_conv(a2w, pair2, i * Q)
        for parity, (place, source) in enumerate(zip(pairs_of(rf, i * Q), pairs_of(x_ref, i * Q))):
            r = source[...].astype(f32) + (got[..., parity * C : (parity + 1) * C] + one(cb2))
            place[...] = r.astype(bf16).astype(f32)
        even = rf[pl.ds(i * R, R), pl.ds(0, W // 2, 2), :]
        odd = rf[pl.ds(i * R, R), pl.ds(1, W // 2, 2), :]
        place = lax.broadcasted_iota(jnp.int32, odd.shape, 1)
        before = jnp.where(place == 0, 0.0, pltpu.roll(odd, 1, 1))
        rw[pl.ds(i * R + 1, R), :, 0:C] = before.astype(bf16)
        rw[pl.ds(i * R + 1, R), :, C : 2 * C] = even.astype(bf16)
        rw[pl.ds(i * R + 1, R), :, 2 * C :] = odd.astype(bf16)

    front2(0)
    for i in range(STEPS):
        if i + 1 < STEPS:
            front2(i + 1)
        conv2(i)

    gkd = mm(down_rows(rw, 0, H // 2), cot_ref[...].reshape(CELLS // 4, 2 * C), TN)
    conv[2] = gkd[:, :C]
    conv[3] = gkd[:, C:]

    def pull(i, s, win_ref, back_ref, slope_ref, out_slope_ref, units):
        got = pair_conv(win_ref, back_ref, i * Q)
        places = zip(pairs_of(slope_ref, i * Q), pairs_of(out_slope_ref, i * Q), units)
        for parity, (place, out_place, unit) in enumerate(places):
            dn = got[..., parity * C : (parity + 1) * C] * place[...]
            out_place[...] = dn
            s = s[0] + fold(dn), s[1] + fold(dn * unit)
        return s

    pair_backward(back2, k2_ref)
    sums = (zero8, zero8)
    for i in range(STEPS):
        sums = pull(i, sums, t2w, back2, g2p, g2p, [unit2(ref[...]) for ref in pairs_of(c1, i * Q)])
    gb2, gg2 = [total_of(part) for part in sums]
    mean_du2 = group_sum(gb2 * (1.0 + gain2)) * (1.0 / PER_GROUP)
    mean_duu2 = group_sum(gg2 * (1.0 + gain2)) * (1.0 / PER_GROUP)
    kernel_grad(a2w, t2w, conv.at[1])

    pair_backward(back1, k1_ref)
    clear_edges(t1w)

    def t1_windows(i, s):
        values = c1[pl.ds(i * R, R)]
        du = g2p[pl.ds(i * R, R)] * one(1.0 + gain2)
        ds = (du - one(mean_du2) - unit2(values) * one(mean_duu2)) * one(rs2)
        put_windows(t1w, i * R, ds * one(scale))
        return s[0] + fold(ds * values), s[1] + fold(ds)

    def unit1(ref):
        return (ref[...].astype(f32) - one(mean1)) * one(rs1)

    class_sums = t1_windows(0, (zero8, zero8))
    sums = (zero8, zero8)
    for i in range(STEPS):
        if i + 1 < STEPS:
            class_sums = t1_windows(i + 1, class_sums)
        sums = pull(i, sums, t1w, back1, g1p, slope1_ref, [unit1(ref) for ref in pairs_of(x_ref, i * Q)])
    gsc, gsh = [total_of(part) for part in class_sums]
    gb1, gg1 = [total_of(part) for part in sums]
    mean_du1 = group_sum(gb1 * (1.0 + gain1)) * (1.0 / PER_GROUP)
    mean_duu1 = group_sum(gg1 * (1.0 + gain1)) * (1.0 / PER_GROUP)
    for index, row in enumerate((1.0 + gain1, mean_du1, mean_duu1)):
        factors_ref[8 * index : 8 * index + 8] = row
    gdb = gdb_ref[...]
    rows = [gg1, gb1, gsh * scale, gg2, gb2, gcb2, gdb[:, :C], gdb[:, C:]]
    rows = [row[0:1] for row in rows]
    rows = rows + [jnp.where(mine[:, :C], row[0:1], 0.0) for row in (gsc, gsh)]
    extra = jnp.concatenate(rows + [jnp.zeros((EXTRA - len(rows) - 2 * NCLASS + 2, C), f32)], axis=0)
    if plan.rings:
        put_results(plan, me, 0, conv, *results)
        kernel_grad(a1w, t1w, conv.at[0])
        put_results(plan, me, 1, conv, *results)
        for ref in results:
            ref[plan.half * 2 * plan.pair_rows :] = extra.astype(ref.dtype)
    else:
        kernel_grad(a1w, t1w, conv.at[0])
        results[0][...] = conv[...]
        results[1][...] = extra


def down_rows(rw, first, rows):
    view = rw.reshape(H // 2 + 1, 2, W // 2, 3 * C)
    taken = [view[pl.ds(first + t // 2, rows), t % 2] for t in range(3)]
    return jnp.concatenate(taken, axis=-1).reshape(rows * W // 2, TAPS * C)


def down_body(rw, kernels, smalls, out_hbm, out_ref, sems):
    kd = jnp.concatenate([kernels[2], kernels[3]], axis=1)
    bias = jnp.concatenate([smalls[6:7, :], smalls[7:8, :]], axis=1)
    copies = []
    for part in range(4):
        rows = slice(part * H // 8, (part + 1) * H // 8)
        got = mm(down_rows(rw, part * H // 8, H // 8), kd) + bias
        out_ref[rows] = got.reshape(H // 8, W // 2, 2 * C).astype(bf16)
        copies.append(pltpu.make_async_copy(out_ref.at[rows], out_hbm.at[rows], sems.at[part]))
        copies[-1].start()
    for copy in copies:
        copy.wait()


def run_down(rw, kernels, smalls):
    shape = (H // 2, W // 2, 2 * C)
    return pl.pallas_call(
        down_body,
        out_shape=jax.ShapeDtypeStruct(shape, bf16),
        in_specs=vmem_specs(3),
        out_specs=pl.BlockSpec(memory_space=pltpu.HBM),
        scratch_shapes=[pltpu.VMEM(shape, bf16), pltpu.SemaphoreType.DMA((4,))],
        compiler_params=limit(8),
        cost_estimate=cost(604, 3 << 20),
        name="down",
    )(rw, kernels, smalls)


def finish_body(x_ref, stats_ref, slope_ref, grad_ref, factors_ref, dx_hbm, dx_ref, sems):
    mean, scale = stats_ref[0:8], stats_ref[8:16]
    gain, mean_du, mean_duu = [factors_ref[8 * k : 8 * k + 8] for k in range(3)]

    def finish(i, carry):
        du = slope_ref[pl.ds(i * R, R)] * one(gain)
        unit = (x_ref[pl.ds(i * R, R)].astype(f32) - one(mean)) * one(scale)
        dx = (du - one(mean_du) - unit * one(mean_duu)) * one(scale)
        dx_ref[pl.ds(i * R, R)] = (grad_ref[pl.ds(i * R, R)] + dx).astype(bf16)
        return carry

    copies = []
    for part in range(4):
        lax.fori_loop(part * H // R // 4, (part + 1) * H // R // 4, finish, 0)
        rows = pl.ds(part * H // 4, H // 4)
        copies.append(pltpu.make_async_copy(dx_ref.at[rows], dx_hbm.at[rows], sems.at[part]))
        copies[-1].start()
    for copy in copies:
        copy.wait()


def run_finish(x, stats, slope, grad, factors):
    return pl.pallas_call(
        finish_body,
        out_shape=jax.ShapeDtypeStruct((H, W, C), bf16),
        in_specs=vmem_specs(5),
        out_specs=pl.BlockSpec(memory_space=pltpu.HBM),
        scratch_shapes=[pltpu.VMEM((H, W, C), bf16), pltpu.SemaphoreType.DMA((4,))],
        compiler_params=limit(8),
        cost_estimate=cost(2, 6 << 20),
        name="finish",
    )(x, stats, slope, grad, factors)


def own_half(odd):
    return (lax.broadcasted_iota(jnp.int32, (8, C), 0) < 4) == (odd == 0)


def put_results(plan, me, index, conv, keep_ref, send_ref):
    left, right = PAIRS[index]
    for core, result in enumerate((keep_ref, send_ref)):
        odd = (me ^ core) & 1
        parts = []
        for owner in plan.targets(me ^ core):
            full, half = plan.places(odd, plan.tile_of(owner * plan.conv_rows))
            parts += [conv[k, pl.ds(full, plan.full), :] for k in (left, right)]
            halves = [conv[k, pl.ds(half, 8), :] for k in (left, right)]
            parts.append(jnp.where(own_half(odd), halves[0], pltpu.roll(halves[1], 4, 0)))
        rows = 2 * plan.pair_rows
        for place in range(0, plan.half, 2):
            two = jnp.concatenate(parts[3 * place : 3 * place + 6], axis=0)
            at = (index * plan.half + place) * plan.pair_rows
            result[at : at + rows] = two.astype(result.dtype)


def vmem_specs(count):
    return [pl.BlockSpec(memory_space=pltpu.VMEM)] * count


def cost(mflops, moved):
    return pl.CostEstimate(flops=mflops << 20, bytes_accessed=moved, transcendentals=0)


def limit(size):
    return pltpu.CompilerParams(vmem_limit_bytes=size << 20)


class Plan:
    def __init__(self, sizes, conv_len, dense_len, small_len):
        (_, outer_size), (_, inner_size) = sizes
        count = outer_size * inner_size
        self.sizes, self.line = sizes, inner_size // 2
        self.conv_len, self.dense_len, self.small_len = conv_len, dense_len, small_len
        self.conv_rows, self.dense_rows = conv_len // C, dense_len // C
        powers = inner_size & (inner_size - 1) == 0 and inner_size >= 4 and outer_size == 4
        self.rings = powers and conv_len % C == 0 and dense_len % C == 0 and small_len <= C and self.conv_rows % 8 == 4
        self.dense_pad = max(-(-(self.dense_rows * k % 8 + self.dense_rows) // 8) * 8 for k in range(count))
        self.full = self.conv_rows - 4
        self.window = self.conv_rows + 4
        self.pair_rows = 2 * self.conv_rows
        self.dense_at = 4 * self.full + 16
        self.small_at = self.dense_at + self.dense_pad
        self.own_rows = -(-(self.small_at + 8) // 16) * 16
        self.inner = inner_size
        self.half = count // 2

    def sources(self, me):
        near = [2 * k for k in range(self.line)]
        low, high = near[: self.line // 2], near[self.line // 2 :]
        held = [low + [k ^ self.inner for k in low], high + [k ^ 2 * self.inner for k in high]]
        held += [[k ^ 2 * self.inner for k in held[0]], [k ^ self.inner for k in held[1]]]
        return [(part, place, me ^ turn) for part, turns in enumerate(held) for place, turn in enumerate(turns)]

    def targets(self, own):
        return [own ^ (plane * self.inner + 2 * k) for plane in range(4) for k in range(self.line)]

    def tile_of(self, row):
        return pl.multiple_of(row // 8 * 8, 8)

    def places(self, odd, first=0):
        return pl.multiple_of(first + 8 * odd, 8), pl.multiple_of(first + self.full * (1 - odd), 8)


def run_block(plan, class_ids, x, cot, prepared, inputs):
    struct = jax.ShapeDtypeStruct
    shapes = [
        struct((H + 2, W // 2, 3 * C), bf16),
        struct((4, KERNEL_ROWS, C), bf16),
        struct((16, C), f32),
        struct((H, W, C), f32),
        struct((H, W, C), f32),
        struct((24, C), f32),
        struct((NCLASS, EMB), bf16),
        struct((EMB, EMB), bf16),
        struct((EMB, 2 * C), bf16),
        struct((NCLASS, EMB), f32),
    ]
    if plan.rings:
        rows = plan.half * 2 * plan.pair_rows
        shapes += [struct((rows + EXTRA, C), f32), struct((rows + EXTRA, C), bf16)]
    else:
        shapes += [struct((4, KERNEL_ROWS, C), f32), struct((EXTRA, C), f32)]
    windows = pltpu.VMEM((H + 2, W, 3 * C), bf16)
    plane = pltpu.VMEM((H, W, C), f32)
    return pl.pallas_call(
        functools.partial(block_body, plan),
        out_shape=shapes,
        in_specs=[pl.BlockSpec(memory_space=pltpu.SMEM)] + vmem_specs(5 + len(inputs)),
        out_specs=vmem_specs(12),
        scratch_shapes=[
            windows,
            windows,
            windows,
            windows,
            plane,
            plane,
            plane,
            plane,
            pltpu.VMEM((4, 12 * C, 2 * C), bf16),
            pltpu.VMEM((4, KERNEL_ROWS, C), f32),
            pltpu.VMEM((MLP_ROWS + 2 * plan.dense_pad, C), f32),
        ],
        compiler_params=limit(40),
        cost_estimate=cost(9000, 16 << 20),
        name="block",
    )(class_ids, x, cot, *prepared, *inputs)


def pack_body(plan, conv_hbm, dense_hbm, small_hbm, out_ref, conv_ref, dense_ref, small_ref, windows, rows, sems):
    pairs = ((conv_hbm.at[0], conv_ref), (dense_hbm, dense_ref), (small_hbm, small_ref))
    copies = [pltpu.make_async_copy(source, target, sems.at[k]) for k, (source, target) in enumerate(pairs)]
    for copy in copies:
        copy.start()
    me = position_of(plan.sizes)
    odd = me & 1
    windows[...] = jnp.zeros(windows.shape, f32)
    rows[...] = jnp.zeros(rows.shape, f32)
    copies[0].wait()
    for r in range(plan.conv_rows):
        for k in range(4):
            windows[pl.ds(k * plan.window + 4 * odd + r, 1), :] = conv_ref[k : k + 1, r * C : (r + 1) * C]
    halves = []
    for k in range(4):
        full, half = plan.places(odd, k * plan.window)
        rows[k * plan.full : (k + 1) * plan.full] = windows[pl.ds(full, plan.full), :]
        halves.append(windows[pl.ds(half, 8), :])
    for k in (0, 2):
        at = 4 * plan.full + 4 * k
        rows[at : at + 8] = jnp.where(own_half(odd), halves[k], pltpu.roll(halves[k + 1], 4, 0))
    copies[1].wait()
    first = plan.dense_at + me * plan.dense_rows % 8
    for r in range(plan.dense_rows):
        rows[pl.ds(first + r, 1), :] = dense_ref[0:1, r * C : (r + 1) * C]
    copies[2].wait()
    own = jnp.concatenate([small_ref[0:1, :], jnp.zeros((1, C - plan.small_len), f32)], axis=1)
    own = pltpu.roll(jnp.broadcast_to(own, (8, C)), me * plan.small_len % C, 1)
    rows[plan.small_at : plan.small_at + 1] = own[0:1]
    out_ref[...] = rows[...].astype(bf16)


def run_pack(plan, conv_state, mlp_state, small_state):
    return pl.pallas_call(
        functools.partial(pack_body, plan),
        out_shape=jax.ShapeDtypeStruct((plan.own_rows, C), bf16),
        in_specs=[pl.BlockSpec(memory_space=pltpu.HBM)] * 3,
        out_specs=pl.BlockSpec(memory_space=pltpu.VMEM),
        scratch_shapes=[
            pltpu.VMEM((4, plan.conv_len), f32),
            pltpu.VMEM((4, plan.dense_len), f32),
            pltpu.VMEM((4, plan.small_len), f32),
            pltpu.VMEM((4 * plan.window, C), f32),
            pltpu.VMEM((plan.own_rows, C), f32),
            pltpu.SemaphoreType.DMA((3,)),
        ],
        compiler_params=pltpu.CompilerParams(vmem_limit_bytes=(64 << 20) - (190 << 10)),
        name="pack",
    )(conv_state, mlp_state, small_state)


def merge_body(plan, blocks, groups, *refs):
    keep_ref, received = refs[0], refs[1 : len(refs) - groups]
    outs = refs[len(refs) - groups :]

    def sums(at, size):
        total = keep_ref[at : at + size]
        for ref in received:
            total = total + ref[at : at + size].astype(f32)
        return total

    size = blocks // groups * plan.pair_rows
    extra = sums(2 * blocks * plan.pair_rows, EXTRA)
    for group, out in enumerate(outs):
        parts = [sums(k * blocks * plan.pair_rows + group * size, size) for k in range(2)]
        out[...] = jnp.concatenate(parts + [extra], axis=0).astype(out.dtype)


def run_merge(plan, blocks, groups, keep, received):
    rows = blocks // groups * 2 * plan.pair_rows + EXTRA
    shapes = [jax.ShapeDtypeStruct((rows, C), f32 if group == 0 else bf16) for group in range(groups)]
    return pl.pallas_call(
        functools.partial(merge_body, plan, blocks, groups),
        out_shape=shapes,
        in_specs=vmem_specs(1 + len(received)),
        out_specs=vmem_specs(groups),
        compiler_params=limit(16),
        name="merge",
    )(keep, *received)


def mlp_grads(table, m1_ref, m2_ref, hidden, dss, out_ref):
    prob = normal_cdf(hidden)

    def put(first, values):
        parts = values.shape[1] // C
        for part in range(parts):
            out_ref[pl.ds(first + part, values.shape[0], parts), :] = values[:, part * C : (part + 1) * C]

    def outer(left, right):
        lefts = [a for k, a in enumerate(left) for b in right[: 3 - k]]
        rights = [b for k, a in enumerate(left) for b in right[: 3 - k]]
        return mm(jnp.concatenate(lefts, axis=0), jnp.concatenate(rights, axis=0), TN)

    dp = exact(dss, m2_ref[...], NT) * gelu_slope(hidden, prob)
    put(0, exact(dp, m1_ref[...], NT))
    put(TABLE_ROWS, outer([table], three(dp)))
    put(TABLE_ROWS + M1_ROWS, outer(three(hidden * prob), three(dss)))
    ge1 = jnp.sum(dp, axis=0, keepdims=True)
    ge2 = jnp.sum(dss, axis=0, keepdims=True)
    return [ge1[:, i * C : (i + 1) * C] for i in range(4)] + [ge2[:, i * C : (i + 1) * C] for i in range(2)]


def mlp_body(table_ref, m1_ref, m2_ref, hidden_ref, dss_ref, out_ref, tail_ref):
    tail = mlp_grads(table_ref[...], m1_ref, m2_ref, hidden_ref[...], dss_ref[...], out_ref)
    for i, row in enumerate(tail):
        tail_ref[i : i + 1, :] = row


def run_mlp(table, m1, m2, hidden, dss):
    return pl.pallas_call(
        mlp_body,
        out_shape=[jax.ShapeDtypeStruct((MLP_ROWS, C), f32), jax.ShapeDtypeStruct((6, C), f32)],
        in_specs=vmem_specs(5),
        out_specs=vmem_specs(2),
        compiler_params=limit(32),
        name="mlp_grad",
    )(table, m1, m2, hidden, dss)


def adam(weight, first, second, average, gradient, rate, decay):
    first = beta_one * first + (1.0 - beta_one) * gradient
    second = beta_two * second + (1.0 - beta_two) * gradient * gradient
    first_hat = first * (1.0 / (1.0 - beta_one**STEP))
    second_hat = second * (1.0 / (1.0 - beta_two**STEP))
    weight = weight - rate * (first_hat / (jnp.sqrt(second_hat) + adam_eps) + decay * weight)
    return weight, first, second, ema_decay * average + (1.0 - ema_decay) * weight


def update_body(plan, received_count, *refs):
    keep_ref, received = refs[0], refs[1 : 1 + received_count]
    table_ref, m1_ref, m2_ref, hidden_ref, conv_ref, dense_ref, small_ref = refs[1 + received_count : 8 + received_count]
    conv_new, dense_new, small_new, conv_copy, dense_copy, small_copy = refs[8 + received_count : 14 + received_count]
    block, grads, rows, smalls = refs[14 + received_count :]
    me = position_of(plan.sizes)
    total = keep_ref[...]
    for ref in received:
        total = total + ref[...].astype(f32)
    odd = me & 1
    for index, pair in enumerate(PAIRS):
        at = index * plan.pair_rows
        rest = total[at + 2 * plan.full : at + plan.pair_rows]
        for side, k in enumerate(pair):
            full, half = plan.places(odd, k * plan.window)
            block[pl.ds(full, plan.full), :] = total[at + side * plan.full : at + (side + 1) * plan.full]
            block[pl.ds(half, 8), :] = pltpu.roll(rest, 4, 0) if side else rest
    extra = total[2 * plan.pair_rows :]
    smalls[0:8] = extra[0:8]
    dss = jnp.concatenate([extra[8 : 8 + NCLASS], extra[8 + NCLASS : 8 + 2 * NCLASS]], axis=1)
    tail = mlp_grads(table_ref[...], m1_ref, m2_ref, hidden_ref[...], dss, grads)
    for i, row in enumerate(tail):
        smalls[8 + i : 9 + i, :] = row

    for r in range(plan.conv_rows):
        at = slice(r * C, (r + 1) * C)
        gradient = block[pl.ds(4 * odd + r, 4, plan.window), :]
        new = adam(*[conv_ref[k, :, at] for k in range(4)], gradient, rate_conv, decay_weights)
        for k in range(4):
            conv_new[k, :, at] = new[k]
        conv_copy[:, at] = new[0].astype(bf16)

    start = me * plan.dense_rows
    for r in range(plan.dense_rows):
        at = slice(r * C, (r + 1) * C)
        gradient = grads[pl.ds(start + r, 1), :]
        rate = jnp.where(start + r < TABLE_ROWS, rate_table, rate_dense)
        new = adam(*[dense_ref[k : k + 1, at] for k in range(4)], gradient, rate, decay_weights)
        for k in range(4):
            dense_new[k : k + 1, at] = new[k]
        rows[r : r + 1, :] = new[0]
    dense_copy[...] = rows[...].astype(bf16)

    start = me * plan.small_len
    lane = lax.broadcasted_iota(jnp.int32, (8, C), 1)
    near = jnp.broadcast_to(smalls[pl.ds(start // C, 1), :], (8, C))
    far = jnp.broadcast_to(smalls[pl.ds(start // C + 1, 1), :], (8, C))
    off = C - start % C
    gradient = jnp.where(lane < off, pltpu.roll(near, off, 1), pltpu.roll(far, off, 1))
    gradient = gradient[0:1, 0 : plan.small_len]
    new = adam(*[small_ref[k : k + 1, :] for k in range(4)], gradient, rate_small, 0.0)
    for k in range(4):
        small_new[k : k + 1, :] = new[k]
    small_copy[...] = new[0].astype(bf16)


def run_update(plan, keep, received, mlp, states):
    struct = jax.ShapeDtypeStruct
    shapes = [struct(state.shape, f32) for state in states]
    shapes += [struct((4, plan.conv_len), bf16), struct((plan.dense_rows, C), bf16), struct((1, plan.small_len), bf16)]
    return pl.pallas_call(
        functools.partial(update_body, plan, len(received)),
        out_shape=shapes,
        in_specs=vmem_specs(1 + len(received) + 4 + 3),
        out_specs=vmem_specs(6),
        scratch_shapes=[
            pltpu.VMEM((4 * plan.window, C), f32),
            pltpu.VMEM((MLP_ROWS, C), f32),
            pltpu.VMEM((plan.dense_rows, C), f32),
            pltpu.VMEM((24, C), f32),
        ],
        compiler_params=limit(24),
        name="update",
    )(keep, *received, *mlp, *states)


def swap(values, axis, size, turn):
    return lax.ppermute(values, axis, [(i, i ^ turn) for i in range(size)])


def gather_ring(plan, own, prepare):
    (outer, outer_size), (inner, inner_size) = plan.sizes
    line = [swap(own, inner, inner_size, 2 * k) for k in range(1, plan.line)]
    line, (*prepared, own) = lax.optimization_barrier((line, prepare(own)))
    line = [own] + line
    half = plan.line // 2
    held = []
    for part, turn in ((jnp.stack(line[:half]), 1), (jnp.stack(line[half:]), 2)):
        held.append(jnp.concatenate([part, swap(part, outer, outer_size, turn)]))
    held = held + [swap(part, outer, outer_size, 2 - k) for k, part in enumerate(held)]
    return prepared, held + [swap(part, inner, inner_size, 1) for part in held]


def reduce_ring(plan, keep, send, beside):
    (outer, outer_size), (inner, inner_size) = plan.sizes
    received = [swap(send, inner, inner_size, 1)]
    keep, *sends = run_merge(plan, outer_size * plan.line, outer_size, keep, received)
    received = [swap(sends[k], outer, outer_size, k + 1) for k in range(outer_size - 1)]
    received, beside = lax.optimization_barrier((received, beside))
    keep, *sends = run_merge(plan, plan.line, plan.line, keep, received)
    return beside, keep, [swap(sends[k], inner, inner_size, 2 * (k + 1)) for k in reversed(range(plan.line - 1))]


def plain_update(plan, position, grads, extra, mlp, states):
    conv_state, mlp_state, small_state = states
    conv_red = lax.psum_scatter(grads.reshape(4, -1), AXES, scatter_dimension=1, tiled=True)
    extra = lax.psum(extra, AXES)
    dss = jnp.concatenate([extra[8 : 8 + NCLASS], extra[8 + NCLASS : 8 + 2 * NCLASS]], axis=1)
    dense_grad, tail = run_mlp(*mlp, dss)
    dense_red = lax.dynamic_slice_in_dim(dense_grad.reshape(-1), position * plan.dense_len, plan.dense_len)
    flat = jnp.concatenate([extra[:8], tail]).reshape(-1)
    small_red = lax.dynamic_slice_in_dim(flat, position * plan.small_len, plan.small_len)
    flat_index = position * plan.dense_len + jnp.arange(plan.dense_len, dtype=jnp.int32)
    dense_rate = jnp.where(flat_index < NCLASS * EMB, rate_table, rate_dense)
    new = [
        jnp.stack(adam(*state, red, rate, decay))
        for state, red, rate, decay in (
            (conv_state, conv_red, rate_conv, decay_weights),
            (mlp_state, dense_red, dense_rate, decay_weights),
            (small_state, small_red, rate_small, 0.0),
        )
    ]
    return new + [state[0].astype(bf16) for state in new]


def per_device(sizes, samples, cotangent, class_ids, *states):
    conv_state, mlp_state, small_state = states
    plan = Plan(sizes, conv_state.shape[2], mlp_state.shape[1], small_state.shape[1])
    x, cot = samples[0], cotangent[0]
    if plan.rings:
        prepared, inputs = gather_ring(plan, run_pack(plan, *states), lambda own: run_prepare(x, cot, own))
    else:
        conv, dense, small = [state[0].astype(bf16) for state in states]
        conv = lax.all_gather(conv, AXES, axis=1, tiled=True).reshape(4, KERNEL_ROWS, C)
        small = lax.all_gather(small, AXES, axis=0, tiled=True).reshape(-1, C)
        dense = lax.all_gather(dense, AXES, axis=0, tiled=True).reshape(MLP_ROWS, C)
        inputs = [conv[0], small, conv[1:], dense]
        prepared = run_prepare(x, cot, small)[:3]
    rw, kernels, smalls, slope, grad, factors, table, m1, m2, hidden, first, second = run_block(
        plan, class_ids, x, cot, prepared, inputs
    )
    out = run_down(rw, kernels, smalls)
    dx = run_finish(x, prepared[0], slope, grad, factors)
    mlp = (table, m1, m2, hidden)
    if plan.rings:
        (out, dx), keep, received = reduce_ring(plan, first, second, (out, dx))
        results = run_update(plan, keep, received, mlp, states)
    else:
        results = plain_update(plan, lax.axis_index(AXES), first, second, mlp, states)
    conv_new, mlp_new, small_new, conv_copy, mlp_copy, small_copy = results
    return out[None], dx[None], conv_new, mlp_new, small_new, conv_copy, mlp_copy.reshape(-1), small_copy.reshape(-1)


def solution(mesh):
    sizes = tuple((axis, mesh.shape[axis]) for axis in AXES)

    def body(*args):
        return per_device(sizes, *args)

    return jax.shard_map(
        body,
        mesh=mesh,
        in_specs=(
            P(AXES, None, None, None),
            P(AXES, None, None, None),
            P(AXES),
            P(None, None, AXES),
            P(None, AXES),
            P(None, AXES),
        ),
        out_specs=(
            P(AXES, None, None, None),
            P(AXES, None, None, None),
            P(None, None, AXES),
            P(None, AXES),
            P(None, AXES),
            P(None, AXES),
            P(AXES),
            P(AXES),
        ),
        check_vma=False,
    )
```

```python
import functools

import jax
import jax.numpy as jnp
from jax import lax
from jax.experimental import pallas as pl
from jax.experimental.pallas import tpu as pltpu
from jax.sharding import PartitionSpec as P

C = 128
EMB = 512
GROUPS = 8
H = 64
W = 64
NCLASS = 16
STEP = 10
TAPS = 9
CELLS = H * W
PER_GROUP = CELLS * (C // GROUPS)
TABLE_ROWS = NCLASS * EMB // C
M1_ROWS = EMB * EMB // C
M2_ROWS = EMB * 2
MLP_ROWS = TABLE_ROWS + M1_ROWS + M2_ROWS
KERNEL_ROWS = TAPS * C
AXES = ("dp", "fsdp")

beta_one = 0.9
beta_two = 0.999
adam_eps = 1e-08
ema_decay = 0.99
norm_eps = 1e-05
rate_conv = 0.08
rate_table = 0.6
rate_dense = 0.1
rate_small = 0.15
decay_weights = 0.01

f32 = jnp.float32
bf16 = jnp.bfloat16
NN = (((1,), (0,)), ((), ()))
NT = (((1,), (1,)), ((), ()))
TN = (((0,), (0,)), ((), ()))
EXTRA = -(-(8 + 2 * NCLASS) // 16) * 16
PAIRS = ((2, 3), (1, 0))
R = 4
Q = 2
STEPS = H // R
PART = CELLS // STEPS


def each(count, step, carry):
    for index in range(count):
        carry = step(index, carry)
    return carry


def mm(a, b, dims=NN):
    return lax.dot_general(a, b, dims, preferred_element_type=f32)


def three(v):
    high = v.astype(bf16)
    rest = v - high.astype(f32)
    mid = rest.astype(bf16)
    return high, mid, (rest - mid.astype(f32)).astype(bf16)


def exact(values, weights, dims=NN):
    rows = values.shape[0]
    got = mm(jnp.concatenate(three(values), axis=0), weights, dims)
    return got[:rows] + got[rows : 2 * rows] + got[2 * rows :]


def group_sum(rows):
    lane = lax.broadcasted_iota(jnp.int32, rows.shape, 1)
    for step in (1, 2, 4, 8):
        up = pltpu.roll(rows, C - step, 1)
        down = pltpu.roll(rows, step, 1)
        rows = rows + jnp.where((lane & step) == 0, up, down)
    return rows


def fold(values):
    return jnp.sum(values.reshape(-1, 8, values.shape[-1]), axis=0)


def total_of(partial):
    return jnp.broadcast_to(jnp.sum(partial, axis=0, keepdims=True), partial.shape)


def one(rows):
    return rows[0:1].reshape(1, 1, C)


def normal_cdf(v):
    return 0.5 * (1.0 + lax.erf(v * 0.7071067811865476))


def gelu_slope(v, prob):
    return prob + v * (jnp.exp(-0.5 * v * v) * 0.3989422804014327)


def put_windows(win_ref, row, values):
    rows = values.shape[0]
    place = lax.broadcasted_iota(jnp.int32, values.shape, 1)
    left = jnp.where(place == 0, 0.0, pltpu.roll(values, 1, 1))
    right = jnp.where(place == W - 1, 0.0, pltpu.roll(values, W - 1, 1))
    win_ref[pl.ds(row + 1, rows), :, 0:C] = left.astype(bf16)
    win_ref[pl.ds(row + 1, rows), :, C : 2 * C] = values.astype(bf16)
    win_ref[pl.ds(row + 1, rows), :, 2 * C : 3 * C] = right.astype(bf16)


def clear_edges(win_ref):
    edge = jnp.zeros((1,) + tuple(win_ref.shape[1:]), win_ref.dtype)
    win_ref[0:1] = edge
    win_ref[H + 1 : H + 2] = edge


def pair_forward(pair_ref, kernel_ref):
    zero = jnp.zeros((3 * C, C), bf16)
    pair_ref[0 : TAPS * C, 0:C] = kernel_ref[...]
    pair_ref[TAPS * C :, 0:C] = zero
    pair_ref[0 : 3 * C, C:] = zero
    pair_ref[3 * C :, C:] = kernel_ref[...]


def flip(block):
    return jnp.transpose(block.astype(f32)).astype(bf16)


def pair_backward(pair_ref, kernel_ref):
    zero = jnp.zeros((3 * C, C), bf16)
    pair_ref[TAPS * C :, 0:C] = zero
    pair_ref[0 : 3 * C, C:] = zero
    for tap in range(TAPS):
        block = flip(kernel_ref[(TAPS - 1 - tap) * C : (TAPS - tap) * C, :])
        pair_ref[tap * C : (tap + 1) * C, 0:C] = block
        pair_ref[(tap + 3) * C : (tap + 4) * C, C:] = block


def pair_conv(win_ref, pair_ref, first):
    view = win_ref.reshape(H // 2 + 1, 2, W, 3 * C)
    taken = [view[pl.ds(first + t // 2, Q), t % 2] for t in range(4)]
    stacked = jnp.concatenate(taken, axis=-1).reshape(Q * W, 12 * C)
    return mm(stacked, pair_ref[...]).reshape(Q, W, 2 * C)


def pairs_of(ref, first):
    view = ref.reshape(H // 2, 2, W, C)
    return [view.at[pl.ds(first, Q), parity] for parity in range(2)]


def kernel_grad(act_ref, win_ref, out_ref):
    left = act_ref[1 : H + 1, :, C : 2 * C].reshape(CELLS, C)
    right = jnp.concatenate([win_ref[t : t + H] for t in range(3)], axis=-1)
    got = mm(left, right.reshape(CELLS, TAPS * C), TN)
    for t in range(TAPS):
        out_ref[t * C : (t + 1) * C, :] = got[:, (TAPS - 1 - t) * C : (TAPS - t) * C]


def position_of(sizes):
    (outer, _), (inner, inner_size) = sizes
    return lax.axis_index(outer) * inner_size + lax.axis_index(inner)


def prepare_body(x_ref, cot_ref, stats_ref, cw, gdb_ref):
    zero8 = jnp.zeros((8, C), f32)

    def read_x(i):
        return x_ref[pl.ds(i * R, R)].astype(f32)

    total = each(H // R, lambda i, s: s + fold(read_x(i)), zero8)
    mean = group_sum(total_of(total)) * (1.0 / PER_GROUP)

    def square_x(i, s):
        d = read_x(i) - one(mean)
        return s + fold(d * d)

    var = group_sum(total_of(each(H // R, square_x, zero8))) * (1.0 / PER_GROUP)
    stats_ref[0:8] = mean
    stats_ref[8:16] = lax.rsqrt(var + norm_eps)
    cw[H // 2 : H // 2 + 1] = jnp.zeros((1, W // 2, 4 * C), bf16)

    def cot_windows(i, s):
        values = cot_ref[pl.ds(i * R, R)].astype(f32)
        place = lax.broadcasted_iota(jnp.int32, values.shape, 1)
        after = jnp.where(place == W // 2 - 1, 0.0, pltpu.roll(values, W // 2 - 1, 1))
        cw[pl.ds(i * R, R), :, 0 : 2 * C] = values.astype(bf16)
        cw[pl.ds(i * R, R), :, 2 * C :] = after.astype(bf16)
        return s + fold(values)

    gdb_ref[...] = total_of(each(H // 2 // R, cot_windows, jnp.zeros((8, 2 * C), f32)))


def copy_body(own_ref, near_ref):
    near_ref[...] = own_ref[...]


def run_copy(own):
    return pl.pallas_call(
        copy_body,
        out_shape=jax.ShapeDtypeStruct(own.shape, own.dtype),
        in_specs=vmem_specs(1),
        out_specs=pl.BlockSpec(memory_space=pltpu.VMEM),
        compiler_params=limit(4),
        cost_estimate=cost(0, 1 << 17),
        name="copy_own",
    )(own)


def run_prepare(x, cot):
    struct = jax.ShapeDtypeStruct
    return pl.pallas_call(
        prepare_body,
        out_shape=[struct((16, C), f32), struct((H // 2 + 1, W // 2, 4 * C), bf16), struct((8, 2 * C), f32)],
        in_specs=vmem_specs(2),
        out_specs=vmem_specs(3),
        compiler_params=limit(8),
        cost_estimate=cost(2, 3 << 20),
        name="prepare",
    )(x, cot)


def block_body(plan, *refs):
    refs = list(refs)
    count = 8 if plan.rings else 4
    cls_ref, x_ref, cot_ref, stats_ref, cw, gdb_ref = refs[:6]
    inputs = refs[6 : 6 + count]
    rw, kernels, smalls, slope1_ref, drf, factors_ref, table_ref, m1_ref, m2_ref, hidden_ref = refs[6 + count : 16 + count]
    made = 24 + count if plan.rings else 18 + count
    results = refs[16 + count : made]
    a1w, a2w, t1w, t2w, c1, g1p, g2p, rf, pairs, conv, dense = refs[made:]
    kernels_f = conv
    me = position_of(plan.sizes)
    k1_ref, k2_ref, kd0_ref, kd1_ref = [kernels.at[k] for k in range(4)]
    pair1, pair2, back1, back2 = [pairs.at[k] for k in range(4)]
    zero8 = jnp.zeros((8, C), f32)

    def take(k, part, place, owner):
        odd = owner & 1
        first = owner // 2 * plan.pair_rows
        full = plan.full
        mine = inputs[part][place, k * full : (k + 1) * full]
        mate = inputs[part + 4][place, k * full : (k + 1) * full]
        kernels_f[k, pl.ds(pl.multiple_of(first + (full + 8) * odd, 8), full), :] = mine.astype(f32)
        kernels_f[k, pl.ds(pl.multiple_of(first + (full + 8) * (1 - odd), 8), full), :] = mate.astype(f32)
        halves = [inputs[p][place, 4 * full : 4 * full + 16].astype(f32) for p in (part, part + 4)]
        halves = [v[8 * (k // 2) : 8 * (k // 2) + 8] for v in halves]
        if k % 2 == 1:
            halves = [pltpu.roll(v, 4, 0) for v in halves]
        kernels_f[k, pl.ds(pl.multiple_of(first + full, 8), 8), :] = jnp.where(own_half(odd), *halves)

    if plan.rings:
        shards = plan.sources(me)
        small = jnp.zeros((16, C), f32)
        row = lax.broadcasted_iota(jnp.int32, (16, C), 0)
        lane = lax.broadcasted_iota(jnp.int32, (16, C), 1)
        for part, place, owner in shards:
            take(0, part, place, owner)
            for p, device in ((part, owner), (part + 4, owner ^ 1)):
                at = row * C + lane - device * plan.small_len
                own = inputs[p][place, plan.small_at - 8 : plan.small_at + 8].astype(f32)[8:9]
                small = jnp.where((at >= 0) & (at < plan.small_len), jnp.broadcast_to(own, (16, C)), small)
        smalls[...] = small
        k1_ref[...] = kernels_f[0].astype(bf16)
    else:
        k1_ref[...] = inputs[0][...]
        smalls[0:14] = inputs[1][...].astype(f32)

    def take_rest(step, steps):
        if not plan.rings:
            return
        if step == 0:
            dense[...] = jnp.zeros(dense.shape, f32)
        for part, place, owner in shards[step::steps]:
            for k in (1, 2, 3):
                take(k, part, place, owner)
            for p, device in ((part, owner), (part + 4, owner ^ 1)):
                values = inputs[p][place, plan.dense_at : plan.small_at + 8].astype(f32)
                first = plan.tile_of(device * plan.dense_rows)
                dense[pl.ds(first, plan.dense_pad), :] += values[: plan.dense_pad]

    def small_row(index):
        return jnp.broadcast_to(smalls[index : index + 1, :], (8, C))

    def small_run(first, count):
        return jnp.concatenate([smalls[first + i : first + i + 1, :] for i in range(count)], axis=1)

    gain1, bias1, cb1, gain2, bias2, cb2 = [small_row(i) for i in range(6)]
    mean1, rs1 = stats_ref[0:8], stats_ref[8:16]
    slope1 = rs1 * (1.0 + gain1)

    pair_forward(pair1, k1_ref)
    clear_edges(a1w)

    def front1(i):
        v = (x_ref[pl.ds(i * R, R)].astype(f32) - one(mean1)) * one(slope1) + one(bias1)
        prob = normal_cdf(v)
        put_windows(a1w, i * R, v * prob)
        g1p[pl.ds(i * R, R)] = gelu_slope(v, prob)

    moments = []

    def conv1(i):
        got = pair_conv(a1w, pair1, i * Q)
        values = [got[..., parity * C : (parity + 1) * C] + one(cb1) for parity in range(2)]
        for place, value in zip(pairs_of(c1, i * Q), values):
            place[...] = value
        centre = total_of(fold(values[0]) + fold(values[1])) * (1.0 / PART)
        off = [value - one(centre) for value in values]
        moments.append((centre, fold(off[0] * off[0]) + fold(off[1] * off[1])))

    front1(0)
    for i in range(STEPS):
        if i + 1 < STEPS:
            front1(i + 1)
        conv1(i)
        take_rest(i, STEPS)
    centre = sum(part[0] for part in moments) * (1.0 / STEPS)
    spread = sum(total_of(part[1]) + PART * (part[0] - centre) * (part[0] - centre) for part in moments) * (1.0 / CELLS)

    if plan.rings:
        kernels[1:4] = conv[1:4].astype(bf16)
    else:
        kernels[1:4] = inputs[2][...]
        dense[0:MLP_ROWS] = inputs[3][...].astype(f32)

    def lanes(first, rows, parts):
        pieces = [dense[pl.ds(first + part, rows, parts), :] for part in range(parts)]
        return jnp.concatenate(pieces, axis=1).astype(bf16)

    table_ref[...] = lanes(0, NCLASS, EMB // C)
    m1_ref[...] = lanes(TABLE_ROWS, EMB, EMB // C)
    m2_ref[...] = lanes(TABLE_ROWS + M1_ROWS, EMB, 2)
    hidden = mm(table_ref[...], m1_ref[...]) + small_run(8, 4)
    hidden_ref[...] = hidden
    act = hidden * normal_cdf(hidden)
    ss = exact(act, m2_ref[...]) + small_run(12, 2)
    mine = lax.broadcasted_iota(jnp.int32, (NCLASS, 2 * C), 0) == cls_ref[0]
    chosen = jnp.sum(jnp.where(mine, ss, 0.0), axis=0, keepdims=True)
    scale = jnp.broadcast_to(1.0 + chosen[:, :C], (8, C))
    shift = jnp.broadcast_to(chosen[:, C:], (8, C))
    pair_forward(pair2, k2_ref)

    kd = jnp.concatenate([kd0_ref[...], kd1_ref[...]], axis=1)

    def tap(i, j):
        return flip(kd[(3 * i + j) * C : (3 * i + j + 1) * C, :])

    none = jnp.zeros((2 * C, C), bf16)
    even_rows = jnp.concatenate([
        jnp.concatenate([tap(1, 1), none], axis=0),
        jnp.concatenate([tap(1, 2), tap(1, 0)], axis=0),
    ], axis=1)
    odd_rows = jnp.concatenate([
        jnp.concatenate([tap(2, 1), none, tap(0, 1), none], axis=0),
        jnp.concatenate([tap(2, 2), tap(2, 0), tap(0, 2), tap(0, 0)], axis=0),
    ], axis=1)
    clear_edges(t2w)

    def back_down(i):
        rows = jnp.concatenate([cw[pl.ds(i * R, R)], cw[pl.ds(i * R + 1, R)]], axis=-1)
        rows = rows.reshape(R * W // 2, 8 * C)
        view = drf.reshape(H // 2, 2, W, C)
        for parity, got in enumerate((mm(rows[:, : 4 * C], even_rows), mm(rows, odd_rows))):
            got = got.reshape(R, W // 2, 2 * C)
            view[pl.ds(i * R, R), parity, pl.ds(0, W // 2, 2), :] = got[..., :C]
            view[pl.ds(i * R, R), parity, pl.ds(1, W // 2, 2), :] = got[..., C:]

    def t2_windows(i):
        values = drf[pl.ds(i * R, R)]
        put_windows(t2w, i * R, values)
        return fold(values)

    gcb2 = zero8
    for i in range(H // 2 // R):
        back_down(i)
        gcb2 = gcb2 + t2_windows(2 * i) + t2_windows(2 * i + 1)
    gcb2 = total_of(gcb2)

    centre_s = centre * scale + shift
    mean2 = group_sum(centre_s) * (GROUPS / C)
    off = centre_s - mean2
    var2 = group_sum(spread * scale * scale + off * off) * (GROUPS / C)
    rs2 = lax.rsqrt(var2 + norm_eps)

    def unit2(values):
        return (values * one(scale) + one(shift - mean2)) * one(rs2)

    clear_edges(a2w)

    def front2(i):
        v = unit2(c1[pl.ds(i * R, R)]) * one(1.0 + gain2) + one(bias2)
        prob = normal_cdf(v)
        put_windows(a2w, i * R, v * prob)
        g2p[pl.ds(i * R, R)] = gelu_slope(v, prob)

    rw[0:1] = jnp.zeros((1, W // 2, 3 * C), bf16)

    def conv2(i):
        got = pair_conv(a2w, pair2, i * Q)
        for parity, (place, source) in enumerate(zip(pairs_of(rf, i * Q), pairs_of(x_ref, i * Q))):
            r = source[...].astype(f32) + (got[..., parity * C : (parity + 1) * C] + one(cb2))
            place[...] = r.astype(bf16).astype(f32)
        even = rf[pl.ds(i * R, R), pl.ds(0, W // 2, 2), :]
        odd = rf[pl.ds(i * R, R), pl.ds(1, W // 2, 2), :]
        place = lax.broadcasted_iota(jnp.int32, odd.shape, 1)
        before = jnp.where(place == 0, 0.0, pltpu.roll(odd, 1, 1))
        rw[pl.ds(i * R + 1, R), :, 0:C] = before.astype(bf16)
        rw[pl.ds(i * R + 1, R), :, C : 2 * C] = even.astype(bf16)
        rw[pl.ds(i * R + 1, R), :, 2 * C :] = odd.astype(bf16)

    front2(0)
    for i in range(STEPS):
        if i + 1 < STEPS:
            front2(i + 1)
        conv2(i)

    gkd = mm(down_rows(rw, 0, H // 2), cot_ref[...].reshape(CELLS // 4, 2 * C), TN)
    conv[2] = gkd[:, :C]
    conv[3] = gkd[:, C:]

    def pull(i, s, win_ref, back_ref, slope_ref, out_slope_ref, units):
        got = pair_conv(win_ref, back_ref, i * Q)
        places = zip(pairs_of(slope_ref, i * Q), pairs_of(out_slope_ref, i * Q), units)
        for parity, (place, out_place, unit) in enumerate(places):
            dn = got[..., parity * C : (parity + 1) * C] * place[...]
            out_place[...] = dn
            s = s[0] + fold(dn), s[1] + fold(dn * unit)
        return s

    pair_backward(back2, k2_ref)
    sums = (zero8, zero8)
    for i in range(STEPS):
        sums = pull(i, sums, t2w, back2, g2p, g2p, [unit2(ref[...]) for ref in pairs_of(c1, i * Q)])
    gb2, gg2 = [total_of(part) for part in sums]
    mean_du2 = group_sum(gb2 * (1.0 + gain2)) * (1.0 / PER_GROUP)
    mean_duu2 = group_sum(gg2 * (1.0 + gain2)) * (1.0 / PER_GROUP)
    kernel_grad(a2w, t2w, conv.at[1])

    pair_backward(back1, k1_ref)
    clear_edges(t1w)

    def t1_windows(i, s):
        values = c1[pl.ds(i * R, R)]
        du = g2p[pl.ds(i * R, R)] * one(1.0 + gain2)
        ds = (du - one(mean_du2) - unit2(values) * one(mean_duu2)) * one(rs2)
        put_windows(t1w, i * R, ds * one(scale))
        return s[0] + fold(ds * values), s[1] + fold(ds)

    def unit1(ref):
        return (ref[...].astype(f32) - one(mean1)) * one(rs1)

    class_sums = t1_windows(0, (zero8, zero8))
    sums = (zero8, zero8)
    for i in range(STEPS):
        if i + 1 < STEPS:
            class_sums = t1_windows(i + 1, class_sums)
        sums = pull(i, sums, t1w, back1, g1p, slope1_ref, [unit1(ref) for ref in pairs_of(x_ref, i * Q)])
    gsc, gsh = [total_of(part) for part in class_sums]
    gb1, gg1 = [total_of(part) for part in sums]
    mean_du1 = group_sum(gb1 * (1.0 + gain1)) * (1.0 / PER_GROUP)
    mean_duu1 = group_sum(gg1 * (1.0 + gain1)) * (1.0 / PER_GROUP)
    for index, row in enumerate((1.0 + gain1, mean_du1, mean_duu1)):
        factors_ref[8 * index : 8 * index + 8] = row
    gdb = gdb_ref[...]
    rows = [gg1, gb1, gsh * scale, gg2, gb2, gcb2, gdb[:, :C], gdb[:, C:]]
    rows = [row[0:1] for row in rows]
    rows = rows + [jnp.where(mine[:, :C], row[0:1], 0.0) for row in (gsc, gsh)]
    extra = jnp.concatenate(rows + [jnp.zeros((EXTRA - len(rows) - 2 * NCLASS + 2, C), f32)], axis=0)
    if plan.rings:
        put_results(plan, me, 0, conv, results)
        kernel_grad(a1w, t1w, conv.at[0])
        put_results(plan, me, 1, conv, results)
        for ref in results:
            ref[plan.line * 2 * plan.pair_rows :] = extra.astype(ref.dtype)
    else:
        kernel_grad(a1w, t1w, conv.at[0])
        results[0][...] = conv[...]
        results[1][...] = extra


def down_rows(rw, first, rows):
    view = rw.reshape(H // 2 + 1, 2, W // 2, 3 * C)
    taken = [view[pl.ds(first + t // 2, rows), t % 2] for t in range(3)]
    return jnp.concatenate(taken, axis=-1).reshape(rows * W // 2, TAPS * C)


def down_body(rw, kernels, smalls, out_hbm, out_ref, sems):
    kd = jnp.concatenate([kernels[2], kernels[3]], axis=1)
    bias = jnp.concatenate([smalls[6:7, :], smalls[7:8, :]], axis=1)
    copies = []
    for part in range(4):
        rows = slice(part * H // 8, (part + 1) * H // 8)
        got = mm(down_rows(rw, part * H // 8, H // 8), kd) + bias
        out_ref[rows] = got.reshape(H // 8, W // 2, 2 * C).astype(bf16)
        copies.append(pltpu.make_async_copy(out_ref.at[rows], out_hbm.at[rows], sems.at[part]))
        copies[-1].start()
    for copy in copies:
        copy.wait()


def run_down(rw, kernels, smalls):
    shape = (H // 2, W // 2, 2 * C)
    return pl.pallas_call(
        down_body,
        out_shape=jax.ShapeDtypeStruct(shape, bf16),
        in_specs=vmem_specs(3),
        out_specs=pl.BlockSpec(memory_space=pltpu.HBM),
        scratch_shapes=[pltpu.VMEM(shape, bf16), pltpu.SemaphoreType.DMA((4,))],
        compiler_params=limit(8),
        cost_estimate=cost(604, 3 << 20),
        name="down",
    )(rw, kernels, smalls)


def finish_body(x_ref, stats_ref, slope_ref, grad_ref, factors_ref, dx_hbm, dx_ref, sems):
    mean, scale = stats_ref[0:8], stats_ref[8:16]
    gain, mean_du, mean_duu = [factors_ref[8 * k : 8 * k + 8] for k in range(3)]

    def finish(i, carry):
        du = slope_ref[pl.ds(i * R, R)] * one(gain)
        unit = (x_ref[pl.ds(i * R, R)].astype(f32) - one(mean)) * one(scale)
        dx = (du - one(mean_du) - unit * one(mean_duu)) * one(scale)
        dx_ref[pl.ds(i * R, R)] = (grad_ref[pl.ds(i * R, R)] + dx).astype(bf16)
        return carry

    copies = []
    for part in range(4):
        lax.fori_loop(part * H // R // 4, (part + 1) * H // R // 4, finish, 0)
        rows = pl.ds(part * H // 4, H // 4)
        copies.append(pltpu.make_async_copy(dx_ref.at[rows], dx_hbm.at[rows], sems.at[part]))
        copies[-1].start()
    for copy in copies:
        copy.wait()


def run_finish(x, stats, slope, grad, factors):
    return pl.pallas_call(
        finish_body,
        out_shape=jax.ShapeDtypeStruct((H, W, C), bf16),
        in_specs=vmem_specs(5),
        out_specs=pl.BlockSpec(memory_space=pltpu.HBM),
        scratch_shapes=[pltpu.VMEM((H, W, C), bf16), pltpu.SemaphoreType.DMA((4,))],
        compiler_params=limit(8),
        cost_estimate=cost(2, 6 << 20),
        name="finish",
    )(x, stats, slope, grad, factors)


def own_half(odd):
    return (lax.broadcasted_iota(jnp.int32, (8, C), 0) < 4) == (odd == 0)


def put_results(plan, me, index, conv, results):
    left, right = PAIRS[index]
    for core in (0, 1):
        odd = (me ^ core) & 1
        owners = plan.targets(me ^ core)
        for group, result in enumerate(results[4 * core : 4 * core + 4]):
            parts = []
            for owner in owners[group * plan.line : (group + 1) * plan.line]:
                full, half = plan.places(odd, plan.tile_of(owner * plan.conv_rows))
                parts += [conv[k, pl.ds(full, plan.full), :] for k in (left, right)]
                halves = [conv[k, pl.ds(half, 8), :] for k in (left, right)]
                parts.append(jnp.where(own_half(odd), halves[0], pltpu.roll(halves[1], 4, 0)))
            rows = 2 * plan.pair_rows
            for place in range(0, plan.line, 2):
                two = jnp.concatenate(parts[3 * place : 3 * place + 6], axis=0)
                at = (index * plan.line + place) * plan.pair_rows
                result[at : at + rows] = two.astype(result.dtype)


def vmem_specs(count):
    return [pl.BlockSpec(memory_space=pltpu.VMEM)] * count


def cost(mflops, moved):
    return pl.CostEstimate(flops=mflops << 20, bytes_accessed=moved, transcendentals=0)


def limit(size):
    return pltpu.CompilerParams(vmem_limit_bytes=size << 20)


class Plan:
    def __init__(self, sizes, conv_len, dense_len, small_len):
        (_, outer_size), (_, inner_size) = sizes
        count = outer_size * inner_size
        self.sizes, self.line = sizes, inner_size // 2
        self.conv_len, self.dense_len, self.small_len = conv_len, dense_len, small_len
        self.conv_rows, self.dense_rows = conv_len // C, dense_len // C
        powers = inner_size & (inner_size - 1) == 0 and inner_size >= 4 and outer_size == 4
        self.rings = powers and conv_len % C == 0 and dense_len % C == 0 and small_len <= C and self.conv_rows % 8 == 4
        self.dense_pad = max(-(-(self.dense_rows * k % 8 + self.dense_rows) // 8) * 8 for k in range(count))
        self.full = self.conv_rows - 4
        self.window = self.conv_rows + 4
        self.pair_rows = 2 * self.conv_rows
        self.dense_at = 4 * self.full + 16
        self.small_at = self.dense_at + self.dense_pad
        self.own_rows = -(-(self.small_at + 8) // 16) * 16
        self.inner = inner_size
        self.half = count // 2

    def sources(self, me):
        near = [0] + [2 * k for k in reversed(range(1, self.line))]
        low, high = near[: self.line // 2], near[self.line // 2 :]
        held = [low + [k ^ self.inner for k in low], high + [k ^ 2 * self.inner for k in high]]
        held += [[k ^ 2 * self.inner for k in held[0]], [k ^ self.inner for k in held[1]]]
        return [(part, place, me ^ turn) for part, turns in enumerate(held) for place, turn in enumerate(turns)]

    def targets(self, own):
        return [own ^ (plane * self.inner + 2 * k) for plane in range(4) for k in range(self.line)]

    def tile_of(self, row):
        return pl.multiple_of(row // 8 * 8, 8)

    def places(self, odd, first=0):
        return pl.multiple_of(first + 8 * odd, 8), pl.multiple_of(first + self.full * (1 - odd), 8)


def run_block(plan, class_ids, x, cot, prepared, inputs):
    struct = jax.ShapeDtypeStruct
    shapes = [
        struct((H + 2, W // 2, 3 * C), bf16),
        struct((4, KERNEL_ROWS, C), bf16),
        struct((16, C), f32),
        struct((H, W, C), f32),
        struct((H, W, C), f32),
        struct((24, C), f32),
        struct((NCLASS, EMB), bf16),
        struct((EMB, EMB), bf16),
        struct((EMB, 2 * C), bf16),
        struct((NCLASS, EMB), f32),
    ]
    if plan.rings:
        rows = plan.line * 2 * plan.pair_rows + EXTRA
        shapes += [struct((rows, C), f32)] * 4 + [struct((rows, C), bf16)] * 4
    else:
        shapes += [struct((4, KERNEL_ROWS, C), f32), struct((EXTRA, C), f32)]
    windows = pltpu.VMEM((H + 2, W, 3 * C), bf16)
    plane = pltpu.VMEM((H, W, C), f32)
    return pl.pallas_call(
        functools.partial(block_body, plan),
        out_shape=shapes,
        in_specs=[pl.BlockSpec(memory_space=pltpu.SMEM)] + vmem_specs(5 + len(inputs)),
        out_specs=vmem_specs(len(shapes)),
        scratch_shapes=[
            windows,
            windows,
            windows,
            windows,
            plane,
            plane,
            plane,
            plane,
            pltpu.VMEM((4, 12 * C, 2 * C), bf16),
            pltpu.VMEM((4, KERNEL_ROWS, C), f32),
            pltpu.VMEM((MLP_ROWS + 2 * plan.dense_pad, C), f32),
        ],
        compiler_params=limit(40),
        cost_estimate=cost(9000, 16 << 20),
        name="block",
    )(class_ids, x, cot, *prepared, *inputs)


def pack_body(plan, conv_hbm, dense_hbm, small_hbm, out_ref, conv_ref, dense_ref, small_ref, windows, rows, sems):
    pairs = ((conv_hbm.at[0], conv_ref), (dense_hbm, dense_ref), (small_hbm, small_ref))
    copies = [pltpu.make_async_copy(source, target, sems.at[k]) for k, (source, target) in enumerate(pairs)]
    for copy in copies:
        copy.start()
    me = position_of(plan.sizes)
    odd = me & 1
    windows[...] = jnp.zeros(windows.shape, f32)
    rows[...] = jnp.zeros(rows.shape, f32)
    copies[0].wait()
    for r in range(plan.conv_rows):
        for k in range(4):
            windows[pl.ds(k * plan.window + 4 * odd + r, 1), :] = conv_ref[k : k + 1, r * C : (r + 1) * C]
    halves = []
    for k in range(4):
        full, half = plan.places(odd, k * plan.window)
        rows[k * plan.full : (k + 1) * plan.full] = windows[pl.ds(full, plan.full), :]
        halves.append(windows[pl.ds(half, 8), :])
    for k in (0, 2):
        at = 4 * plan.full + 4 * k
        rows[at : at + 8] = jnp.where(own_half(odd), halves[k], pltpu.roll(halves[k + 1], 4, 0))
    copies[1].wait()
    first = plan.dense_at + me * plan.dense_rows % 8
    for r in range(plan.dense_rows):
        rows[pl.ds(first + r, 1), :] = dense_ref[0:1, r * C : (r + 1) * C]
    copies[2].wait()
    own = jnp.concatenate([small_ref[0:1, :], jnp.zeros((1, C - plan.small_len), f32)], axis=1)
    own = pltpu.roll(jnp.broadcast_to(own, (8, C)), me * plan.small_len % C, 1)
    rows[plan.small_at : plan.small_at + 1] = own[0:1]
    out_ref[...] = rows[...].astype(bf16)


def run_pack(plan, conv_state, mlp_state, small_state):
    return pl.pallas_call(
        functools.partial(pack_body, plan),
        out_shape=jax.ShapeDtypeStruct((plan.own_rows, C), bf16),
        in_specs=[pl.BlockSpec(memory_space=pltpu.HBM)] * 3,
        out_specs=pl.BlockSpec(memory_space=pltpu.VMEM),
        scratch_shapes=[
            pltpu.VMEM((4, plan.conv_len), f32),
            pltpu.VMEM((4, plan.dense_len), f32),
            pltpu.VMEM((4, plan.small_len), f32),
            pltpu.VMEM((4 * plan.window, C), f32),
            pltpu.VMEM((plan.own_rows, C), f32),
            pltpu.SemaphoreType.DMA((3,)),
        ],
        compiler_params=pltpu.CompilerParams(vmem_limit_bytes=(64 << 20) - (190 << 10)),
        name="pack",
    )(conv_state, mlp_state, small_state)


def merge_body(plan, blocks, groups, *refs):
    keep_ref, received = refs[0], refs[1 : len(refs) - groups]
    outs = refs[len(refs) - groups :]

    def sums(at, size):
        total = keep_ref[at : at + size]
        for ref in received:
            total = total + ref[at : at + size].astype(f32)
        return total

    size = blocks // groups * plan.pair_rows
    extra = sums(2 * blocks * plan.pair_rows, EXTRA)
    for group, out in enumerate(outs):
        parts = [sums(k * blocks * plan.pair_rows + group * size, size) for k in range(2)]
        out[...] = jnp.concatenate(parts + [extra], axis=0).astype(out.dtype)


def run_merge(plan, blocks, groups, keep, received):
    rows = blocks // groups * 2 * plan.pair_rows + EXTRA
    shapes = [jax.ShapeDtypeStruct((rows, C), f32 if group == 0 else bf16) for group in range(groups)]
    return pl.pallas_call(
        functools.partial(merge_body, plan, blocks, groups),
        out_shape=shapes,
        in_specs=vmem_specs(1 + len(received)),
        out_specs=vmem_specs(groups),
        compiler_params=limit(16),
        name="merge",
    )(keep, *received)


def mlp_grads(table, m1_ref, m2_ref, hidden, dss, out_ref):
    prob = normal_cdf(hidden)

    def put(first, values):
        parts = values.shape[1] // C
        for part in range(parts):
            out_ref[pl.ds(first + part, values.shape[0], parts), :] = values[:, part * C : (part + 1) * C]

    def outer(left, right):
        lefts = [a for k, a in enumerate(left) for b in right[: 3 - k]]
        rights = [b for k, a in enumerate(left) for b in right[: 3 - k]]
        return mm(jnp.concatenate(lefts, axis=0), jnp.concatenate(rights, axis=0), TN)

    dp = exact(dss, m2_ref[...], NT) * gelu_slope(hidden, prob)
    put(0, exact(dp, m1_ref[...], NT))
    put(TABLE_ROWS, outer([table], three(dp)))
    put(TABLE_ROWS + M1_ROWS, outer(three(hidden * prob), three(dss)))
    ge1 = jnp.sum(dp, axis=0, keepdims=True)
    ge2 = jnp.sum(dss, axis=0, keepdims=True)
    return [ge1[:, i * C : (i + 1) * C] for i in range(4)] + [ge2[:, i * C : (i + 1) * C] for i in range(2)]


def mlp_body(table_ref, m1_ref, m2_ref, hidden_ref, dss_ref, out_ref, tail_ref):
    tail = mlp_grads(table_ref[...], m1_ref, m2_ref, hidden_ref[...], dss_ref[...], out_ref)
    for i, row in enumerate(tail):
        tail_ref[i : i + 1, :] = row


def run_mlp(table, m1, m2, hidden, dss):
    return pl.pallas_call(
        mlp_body,
        out_shape=[jax.ShapeDtypeStruct((MLP_ROWS, C), f32), jax.ShapeDtypeStruct((6, C), f32)],
        in_specs=vmem_specs(5),
        out_specs=vmem_specs(2),
        compiler_params=limit(32),
        name="mlp_grad",
    )(table, m1, m2, hidden, dss)


def adam(weight, first, second, average, gradient, rate, decay):
    first = beta_one * first + (1.0 - beta_one) * gradient
    second = beta_two * second + (1.0 - beta_two) * gradient * gradient
    first_hat = first * (1.0 / (1.0 - beta_one**STEP))
    second_hat = second * (1.0 / (1.0 - beta_two**STEP))
    weight = weight - rate * (first_hat / (jnp.sqrt(second_hat) + adam_eps) + decay * weight)
    return weight, first, second, ema_decay * average + (1.0 - ema_decay) * weight


def update_body(plan, received_count, *refs):
    keep_ref, received = refs[0], refs[1 : 1 + received_count]
    table_ref, m1_ref, m2_ref, hidden_ref, conv_ref, dense_ref, small_ref = refs[1 + received_count : 8 + received_count]
    conv_new, dense_new, small_new, conv_copy, dense_copy, small_copy = refs[8 + received_count : 14 + received_count]
    block, grads, rows, smalls = refs[14 + received_count :]
    me = position_of(plan.sizes)
    total = keep_ref[...]
    for ref in received:
        total = total + ref[...].astype(f32)
    odd = me & 1
    for index, pair in enumerate(PAIRS):
        at = index * plan.pair_rows
        rest = total[at + 2 * plan.full : at + plan.pair_rows]
        for side, k in enumerate(pair):
            full, half = plan.places(odd, k * plan.window)
            block[pl.ds(full, plan.full), :] = total[at + side * plan.full : at + (side + 1) * plan.full]
            block[pl.ds(half, 8), :] = pltpu.roll(rest, 4, 0) if side else rest
    extra = total[2 * plan.pair_rows :]
    smalls[0:8] = extra[0:8]
    dss = jnp.concatenate([extra[8 : 8 + NCLASS], extra[8 + NCLASS : 8 + 2 * NCLASS]], axis=1)
    tail = mlp_grads(table_ref[...], m1_ref, m2_ref, hidden_ref[...], dss, grads)
    for i, row in enumerate(tail):
        smalls[8 + i : 9 + i, :] = row

    for r in range(plan.conv_rows):
        at = slice(r * C, (r + 1) * C)
        gradient = block[pl.ds(4 * odd + r, 4, plan.window), :]
        new = adam(*[conv_ref[k, :, at] for k in range(4)], gradient, rate_conv, decay_weights)
        for k in range(4):
            conv_new[k, :, at] = new[k]
        conv_copy[:, at] = new[0].astype(bf16)

    start = me * plan.dense_rows
    for r in range(plan.dense_rows):
        at = slice(r * C, (r + 1) * C)
        gradient = grads[pl.ds(start + r, 1), :]
        rate = jnp.where(start + r < TABLE_ROWS, rate_table, rate_dense)
        new = adam(*[dense_ref[k : k + 1, at] for k in range(4)], gradient, rate, decay_weights)
        for k in range(4):
            dense_new[k : k + 1, at] = new[k]
        rows[r : r + 1, :] = new[0]
    dense_copy[...] = rows[...].astype(bf16)

    start = me * plan.small_len
    lane = lax.broadcasted_iota(jnp.int32, (8, C), 1)
    near = jnp.broadcast_to(smalls[pl.ds(start // C, 1), :], (8, C))
    far = jnp.broadcast_to(smalls[pl.ds(start // C + 1, 1), :], (8, C))
    off = C - start % C
    gradient = jnp.where(lane < off, pltpu.roll(near, off, 1), pltpu.roll(far, off, 1))
    gradient = gradient[0:1, 0 : plan.small_len]
    new = adam(*[small_ref[k : k + 1, :] for k in range(4)], gradient, rate_small, 0.0)
    for k in range(4):
        small_new[k : k + 1, :] = new[k]
    small_copy[...] = new[0].astype(bf16)


def run_update(plan, keep, received, mlp, states):
    struct = jax.ShapeDtypeStruct
    shapes = [struct(state.shape, f32) for state in states]
    shapes += [struct((4, plan.conv_len), bf16), struct((plan.dense_rows, C), bf16), struct((1, plan.small_len), bf16)]
    return pl.pallas_call(
        functools.partial(update_body, plan, len(received)),
        out_shape=shapes,
        in_specs=vmem_specs(1 + len(received) + 4 + 3),
        out_specs=vmem_specs(6),
        scratch_shapes=[
            pltpu.VMEM((4 * plan.window, C), f32),
            pltpu.VMEM((MLP_ROWS, C), f32),
            pltpu.VMEM((plan.dense_rows, C), f32),
            pltpu.VMEM((24, C), f32),
        ],
        compiler_params=limit(24),
        name="update",
    )(keep, *received, *mlp, *states)


def swap(values, axis, size, turn):
    return lax.ppermute(values, axis, [(i, i ^ turn) for i in range(size)])


def gather_ring(plan, own, prepare):
    (outer, outer_size), (inner, inner_size) = plan.sizes
    half = plan.line // 2
    line = [swap(own, inner, inner_size, 2 * k) for k in reversed(range(1, plan.line))]
    low, own = lax.optimization_barrier((line[: half - 1], run_copy(own)))
    held = []
    for part, turn in (([own] + low, 1), (line[half - 1 :], 2)):
        part = jnp.stack(part)
        held.append(jnp.concatenate([part, swap(part, outer, outer_size, turn)]))
    late = [swap(part, outer, outer_size, 2 - k) for k, part in enumerate(held)]
    late, prepared = lax.optimization_barrier((late, prepare()))
    held = held + late
    return prepared, held + [swap(part, inner, inner_size, 1) for part in held]


def reduce_ring(plan, keeps, sends, beside):
    (outer, outer_size), (inner, inner_size) = plan.sizes
    mates = [swap(part, inner, inner_size, 1) for part in sends]
    received = []
    for turn in range(1, outer_size):
        part = keeps[turn] + mates[turn].astype(f32)
        received.append(swap(part.astype(bf16), outer, outer_size, turn))
    received, beside = lax.optimization_barrier((received, beside))
    keep, *parts = run_merge(plan, plan.line, plan.line, keeps[0], [mates[0], *received])
    return beside, keep, [swap(parts[k], inner, inner_size, 2 * (k + 1)) for k in reversed(range(plan.line - 1))]


def plain_update(plan, position, grads, extra, mlp, states):
    conv_state, mlp_state, small_state = states
    conv_red = lax.psum_scatter(grads.reshape(4, -1), AXES, scatter_dimension=1, tiled=True)
    extra = lax.psum(extra, AXES)
    dss = jnp.concatenate([extra[8 : 8 + NCLASS], extra[8 + NCLASS : 8 + 2 * NCLASS]], axis=1)
    dense_grad, tail = run_mlp(*mlp, dss)
    dense_red = lax.dynamic_slice_in_dim(dense_grad.reshape(-1), position * plan.dense_len, plan.dense_len)
    flat = jnp.concatenate([extra[:8], tail]).reshape(-1)
    small_red = lax.dynamic_slice_in_dim(flat, position * plan.small_len, plan.small_len)
    flat_index = position * plan.dense_len + jnp.arange(plan.dense_len, dtype=jnp.int32)
    dense_rate = jnp.where(flat_index < NCLASS * EMB, rate_table, rate_dense)
    new = [
        jnp.stack(adam(*state, red, rate, decay))
        for state, red, rate, decay in (
            (conv_state, conv_red, rate_conv, decay_weights),
            (mlp_state, dense_red, dense_rate, decay_weights),
            (small_state, small_red, rate_small, 0.0),
        )
    ]
    return new + [state[0].astype(bf16) for state in new]


def per_device(sizes, samples, cotangent, class_ids, *states):
    conv_state, mlp_state, small_state = states
    plan = Plan(sizes, conv_state.shape[2], mlp_state.shape[1], small_state.shape[1])
    x, cot = samples[0], cotangent[0]
    if plan.rings:
        prepared, inputs = gather_ring(plan, run_pack(plan, *states), lambda: run_prepare(x, cot))
    else:
        conv, dense, small = [state[0].astype(bf16) for state in states]
        conv = lax.all_gather(conv, AXES, axis=1, tiled=True).reshape(4, KERNEL_ROWS, C)
        small = lax.all_gather(small, AXES, axis=0, tiled=True).reshape(-1, C)
        dense = lax.all_gather(dense, AXES, axis=0, tiled=True).reshape(MLP_ROWS, C)
        inputs = [conv[0], small, conv[1:], dense]
        prepared = run_prepare(x, cot)
    rw, kernels, smalls, slope, grad, factors, table, m1, m2, hidden, *sums = run_block(
        plan, class_ids, x, cot, prepared, inputs
    )
    out = run_down(rw, kernels, smalls)
    dx = run_finish(x, prepared[0], slope, grad, factors)
    mlp = (table, m1, m2, hidden)
    if plan.rings:
        (out, dx), keep, received = reduce_ring(plan, sums[:4], sums[4:], (out, dx))
        results = run_update(plan, keep, received, mlp, states)
    else:
        results = plain_update(plan, lax.axis_index(AXES), *sums, mlp, states)
    conv_new, mlp_new, small_new, conv_copy, mlp_copy, small_copy = results
    return out[None], dx[None], conv_new, mlp_new, small_new, conv_copy, mlp_copy.reshape(-1), small_copy.reshape(-1)


def solution(mesh):
    sizes = tuple((axis, mesh.shape[axis]) for axis in AXES)

    def body(*args):
        return per_device(sizes, *args)

    return jax.shard_map(
        body,
        mesh=mesh,
        in_specs=(
            P(AXES, None, None, None),
            P(AXES, None, None, None),
            P(AXES),
            P(None, None, AXES),
            P(None, AXES),
            P(None, AXES),
        ),
        out_specs=(
            P(AXES, None, None, None),
            P(AXES, None, None, None),
            P(None, None, AXES),
            P(None, AXES),
            P(None, AXES),
            P(None, AXES),
            P(AXES),
            P(AXES),
        ),
        check_vma=False,
    )
```

```python
import functools

import jax
import jax.numpy as jnp
from jax import lax
from jax.experimental import pallas as pl
from jax.experimental.pallas import tpu as pltpu
from jax.sharding import PartitionSpec as P

C = 128
EMB = 512
GROUPS = 8
H = 64
W = 64
NCLASS = 16
STEP = 10
TAPS = 9
CELLS = H * W
PER_GROUP = CELLS * (C // GROUPS)
TABLE_ROWS = NCLASS * EMB // C
M1_ROWS = EMB * EMB // C
M2_ROWS = EMB * 2
MLP_ROWS = TABLE_ROWS + M1_ROWS + M2_ROWS
KERNEL_ROWS = TAPS * C
AXES = ("dp", "fsdp")

beta_one = 0.9
beta_two = 0.999
adam_eps = 1e-08
ema_decay = 0.99
norm_eps = 1e-05
rate_conv = 0.08
rate_table = 0.6
rate_dense = 0.1
rate_small = 0.15
decay_weights = 0.01

f32 = jnp.float32
bf16 = jnp.bfloat16
NN = (((1,), (0,)), ((), ()))
NT = (((1,), (1,)), ((), ()))
TN = (((0,), (0,)), ((), ()))
EXTRA = -(-(8 + 2 * NCLASS) // 16) * 16
PAIRS = ((2, 3), (1, 0))
R = 4
Q = 2
WIDE = 8
STEPS = H // R
PART = CELLS // STEPS


def each(count, step, carry):
    for index in range(count):
        carry = step(index, carry)
    return carry


def mm(a, b, dims=NN):
    return lax.dot_general(a, b, dims, preferred_element_type=f32)


def three(v):
    high = v.astype(bf16)
    rest = v - high.astype(f32)
    mid = rest.astype(bf16)
    return high, mid, (rest - mid.astype(f32)).astype(bf16)


def exact(values, weights, dims=NN):
    rows = values.shape[0]
    got = mm(jnp.concatenate(three(values), axis=0), weights, dims)
    return got[:rows] + got[rows : 2 * rows] + got[2 * rows :]


def group_sum(rows):
    lane = lax.broadcasted_iota(jnp.int32, rows.shape, 1)
    for step in (1, 2, 4, 8):
        up = pltpu.roll(rows, C - step, 1)
        down = pltpu.roll(rows, step, 1)
        rows = rows + jnp.where((lane & step) == 0, up, down)
    return rows


def fold(values):
    return jnp.sum(values.reshape(-1, 8, values.shape[-1]), axis=0)


def total_of(partial):
    return jnp.broadcast_to(jnp.sum(partial, axis=0, keepdims=True), partial.shape)


def one(rows):
    return rows[0:1].reshape(1, 1, C)


def normal_cdf(v):
    return 0.5 * (1.0 + lax.erf(v * 0.7071067811865476))


def gelu_slope(v, prob):
    return prob + v * (jnp.exp(-0.5 * v * v) * 0.3989422804014327)


def put_windows(win_ref, row, values):
    rows = values.shape[0]
    place = lax.broadcasted_iota(jnp.int32, values.shape, 1)
    left = jnp.where(place == 0, 0.0, pltpu.roll(values, 1, 1))
    right = jnp.where(place == W - 1, 0.0, pltpu.roll(values, W - 1, 1))
    win_ref[pl.ds(row + 1, rows), :, 0:C] = left.astype(bf16)
    win_ref[pl.ds(row + 1, rows), :, C : 2 * C] = values.astype(bf16)
    win_ref[pl.ds(row + 1, rows), :, 2 * C : 3 * C] = right.astype(bf16)


def clear_edges(win_ref):
    edge = jnp.zeros((1,) + tuple(win_ref.shape[1:]), win_ref.dtype)
    win_ref[0:1] = edge
    win_ref[H + 1 : H + 2] = edge


def pair_forward(pair_ref, kernel_ref):
    zero = jnp.zeros((3 * C, C), bf16)
    pair_ref[0 : TAPS * C, 0:C] = kernel_ref[...]
    pair_ref[TAPS * C :, 0:C] = zero
    pair_ref[0 : 3 * C, C:] = zero
    pair_ref[3 * C :, C:] = kernel_ref[...]


def flip(block):
    return jnp.transpose(block.astype(f32)).astype(bf16)


def pair_backward(pair_ref, kernel_ref):
    zero = jnp.zeros((3 * C, C), bf16)
    pair_ref[TAPS * C :, 0:C] = zero
    pair_ref[0 : 3 * C, C:] = zero
    for tap in range(TAPS):
        block = flip(kernel_ref[(TAPS - 1 - tap) * C : (TAPS - tap) * C, :])
        pair_ref[tap * C : (tap + 1) * C, 0:C] = block
        pair_ref[(tap + 3) * C : (tap + 4) * C, C:] = block


def pair_conv(win_ref, pair_ref, first, q=Q):
    view = win_ref.reshape(H // 2 + 1, 2, W, 3 * C)
    taken = [view[pl.ds(first + t // 2, q), t % 2] for t in range(4)]
    stacked = jnp.concatenate(taken, axis=-1).reshape(q * W, 12 * C)
    return mm(stacked, pair_ref[...]).reshape(q, W, 2 * C)


def pairs_of(ref, first, q=Q):
    view = ref.reshape(H // 2, 2, W, C)
    return [view.at[pl.ds(first, q), parity] for parity in range(2)]


def kernel_grad(act_ref, win_ref, out_ref):
    left = act_ref[1 : H + 1, :, C : 2 * C].reshape(CELLS, C)
    right = jnp.concatenate([win_ref[t : t + H] for t in range(3)], axis=-1)
    got = mm(left, right.reshape(CELLS, TAPS * C), TN)
    for t in range(TAPS):
        out_ref[t * C : (t + 1) * C, :] = got[:, (TAPS - 1 - t) * C : (TAPS - t) * C]


def position_of(sizes):
    (outer, _), (inner, inner_size) = sizes
    return lax.axis_index(outer) * inner_size + lax.axis_index(inner)


def prepare_body(cls_ref, x_ref, cot_ref, stats_ref, cw, gdb_ref, hot_ref):
    hot_ref[...] = (lax.broadcasted_iota(jnp.int32, hot_ref.shape, 0) == cls_ref[0]).astype(f32)
    zero8 = jnp.zeros((8, C), f32)

    def read_x(i):
        return x_ref[pl.ds(i * R, R)].astype(f32)

    total = each(H // R, lambda i, s: s + fold(read_x(i)), zero8)
    mean = group_sum(total_of(total)) * (1.0 / PER_GROUP)

    def square_x(i, s):
        d = read_x(i) - one(mean)
        return s + fold(d * d)

    var = group_sum(total_of(each(H // R, square_x, zero8))) * (1.0 / PER_GROUP)
    stats_ref[0:8] = mean
    stats_ref[8:16] = lax.rsqrt(var + norm_eps)
    cw[H // 2 : H // 2 + 1] = jnp.zeros((1, W // 2, 4 * C), bf16)

    def cot_windows(i, s):
        values = cot_ref[pl.ds(i * R, R)].astype(f32)
        place = lax.broadcasted_iota(jnp.int32, values.shape, 1)
        after = jnp.where(place == W // 2 - 1, 0.0, pltpu.roll(values, W // 2 - 1, 1))
        cw[pl.ds(i * R, R), :, 0 : 2 * C] = values.astype(bf16)
        cw[pl.ds(i * R, R), :, 2 * C :] = after.astype(bf16)
        return s + fold(values)

    gdb_ref[...] = total_of(each(H // 2 // R, cot_windows, jnp.zeros((8, 2 * C), f32)))


def copy_body(own_ref, near_ref):
    near_ref[...] = own_ref[...]


def run_copy(own):
    return pl.pallas_call(
        copy_body,
        out_shape=jax.ShapeDtypeStruct(own.shape, own.dtype),
        in_specs=vmem_specs(1),
        out_specs=pl.BlockSpec(memory_space=pltpu.VMEM),
        compiler_params=limit(4),
        cost_estimate=cost(0, 1 << 17),
        name="copy_own",
    )(own)


def run_prepare(class_ids, x, cot):
    struct = jax.ShapeDtypeStruct
    return pl.pallas_call(
        prepare_body,
        out_shape=[struct((16, C), f32), struct((H // 2 + 1, W // 2, 4 * C), bf16), struct((8, 2 * C), f32), struct((NCLASS, 2 * C), f32)],
        in_specs=[pl.BlockSpec(memory_space=pltpu.SMEM)] + vmem_specs(2),
        out_specs=vmem_specs(4),
        compiler_params=limit(8),
        cost_estimate=cost(2, 3 << 20),
        name="prepare",
    )(class_ids, x, cot)


def block_body(plan, *refs):
    refs = list(refs)
    count = 8 if plan.rings else 4
    x_ref, cot_ref, stats_ref, cw, gdb_ref, hot_ref = refs[:6]
    inputs = refs[6 : 6 + count]
    rw, kernels, smalls, slope1_ref, drf, factors_ref, table_ref, m1_ref, m2_ref, hidden_ref = refs[6 + count : 16 + count]
    made = 24 + count if plan.rings else 18 + count
    results = refs[16 + count : made]
    a1w, a2w, t1w, t2w, c1, g1p, g2p, rf, pairs, conv, dense = refs[made:]
    kernels_f = conv
    me = position_of(plan.sizes)
    k1_ref, k2_ref, kd0_ref, kd1_ref = [kernels.at[k] for k in range(4)]
    pair1, pair2, back1, back2 = [pairs.at[k] for k in range(4)]
    zero8 = jnp.zeros((8, C), f32)

    def take(k, part, place, owner):
        odd = owner & 1
        first = owner // 2 * plan.pair_rows
        full = plan.full
        mine = inputs[part][place, k * full : (k + 1) * full]
        mate = inputs[part + 4][place, k * full : (k + 1) * full]
        kernels_f[k, pl.ds(pl.multiple_of(first + (full + 8) * odd, 8), full), :] = mine.astype(f32)
        kernels_f[k, pl.ds(pl.multiple_of(first + (full + 8) * (1 - odd), 8), full), :] = mate.astype(f32)
        halves = [inputs[p][place, 4 * full : 4 * full + 16].astype(f32) for p in (part, part + 4)]
        halves = [v[8 * (k // 2) : 8 * (k // 2) + 8] for v in halves]
        if k % 2 == 1:
            halves = [pltpu.roll(v, 4, 0) for v in halves]
        kernels_f[k, pl.ds(pl.multiple_of(first + full, 8), 8), :] = jnp.where(own_half(odd), *halves)

    if plan.rings:
        shards = plan.sources(me)
        small = jnp.zeros((16, C), f32)
        row = lax.broadcasted_iota(jnp.int32, (16, C), 0)
        lane = lax.broadcasted_iota(jnp.int32, (16, C), 1)
        for part, place, owner in shards:
            take(0, part, place, owner)
            for p, device in ((part, owner), (part + 4, owner ^ 1)):
                at = row * C + lane - device * plan.small_len
                own = inputs[p][place, plan.small_at - 8 : plan.small_at + 8].astype(f32)[8:9]
                small = jnp.where((at >= 0) & (at < plan.small_len), jnp.broadcast_to(own, (16, C)), small)
        smalls[...] = small
        k1_ref[...] = kernels_f[0].astype(bf16)
    else:
        k1_ref[...] = inputs[0][...]
        smalls[0:14] = inputs[1][...].astype(f32)

    def take_rest(step, steps):
        if not plan.rings:
            return
        if step == 0:
            dense[...] = jnp.zeros(dense.shape, f32)
        for part, place, owner in shards[step::steps]:
            for k in (1, 2, 3):
                take(k, part, place, owner)
            for p, device in ((part, owner), (part + 4, owner ^ 1)):
                values = inputs[p][place, plan.dense_at : plan.small_at + 8].astype(f32)
                first = plan.tile_of(device * plan.dense_rows)
                dense[pl.ds(first, plan.dense_pad), :] += values[: plan.dense_pad]

    def small_row(index):
        return jnp.broadcast_to(smalls[index : index + 1, :], (8, C))

    def small_run(first, count):
        return jnp.concatenate([smalls[first + i : first + i + 1, :] for i in range(count)], axis=1)

    gain1, bias1, cb1, gain2, bias2, cb2 = [small_row(i) for i in range(6)]
    mean1, rs1 = stats_ref[0:8], stats_ref[8:16]
    slope1 = rs1 * (1.0 + gain1)

    pair_forward(pair1, k1_ref)
    clear_edges(a1w)

    def front1(i):
        v = (x_ref[pl.ds(i * R, R)].astype(f32) - one(mean1)) * one(slope1) + one(bias1)
        prob = normal_cdf(v)
        put_windows(a1w, i * R, v * prob)
        g1p[pl.ds(i * R, R)] = gelu_slope(v, prob)

    moments = []

    def conv1(i):
        got = pair_conv(a1w, pair1, i * Q)
        values = [got[..., parity * C : (parity + 1) * C] + one(cb1) for parity in range(2)]
        for place, value in zip(pairs_of(c1, i * Q), values):
            place[...] = value
        centre = total_of(fold(values[0]) + fold(values[1])) * (1.0 / PART)
        off = [value - one(centre) for value in values]
        moments.append((centre, fold(off[0] * off[0]) + fold(off[1] * off[1])))

    front1(0)
    for i in range(STEPS):
        if i + 1 < STEPS:
            front1(i + 1)
        conv1(i)
        take_rest(i, STEPS)
    centre = sum(part[0] for part in moments) * (1.0 / STEPS)
    spread = sum(total_of(part[1]) + PART * (part[0] - centre) * (part[0] - centre) for part in moments) * (1.0 / CELLS)

    if plan.rings:
        kernels[1:4] = conv[1:4].astype(bf16)
    else:
        kernels[1:4] = inputs[2][...]
        dense[0:MLP_ROWS] = inputs[3][...].astype(f32)

    def lanes(first, rows, parts):
        pieces = [dense[pl.ds(first + part, rows, parts), :] for part in range(parts)]
        return jnp.concatenate(pieces, axis=1).astype(bf16)

    table_ref[...] = lanes(0, NCLASS, EMB // C)
    m1_ref[...] = lanes(TABLE_ROWS, EMB, EMB // C)
    m2_ref[...] = lanes(TABLE_ROWS + M1_ROWS, EMB, 2)
    hidden = mm(table_ref[...], m1_ref[...]) + small_run(8, 4)
    hidden_ref[...] = hidden
    act = hidden * normal_cdf(hidden)
    ss = exact(act, m2_ref[...]) + small_run(12, 2)
    mine = hot_ref[...] > 0.5
    chosen = jnp.sum(jnp.where(mine, ss, 0.0), axis=0, keepdims=True)
    scale = jnp.broadcast_to(1.0 + chosen[:, :C], (8, C))
    shift = jnp.broadcast_to(chosen[:, C:], (8, C))
    pair_forward(pair2, k2_ref)

    kd = jnp.concatenate([kd0_ref[...], kd1_ref[...]], axis=1)

    def tap(i, j):
        return flip(kd[(3 * i + j) * C : (3 * i + j + 1) * C, :])

    none = jnp.zeros((2 * C, C), bf16)
    even_rows = jnp.concatenate([
        jnp.concatenate([tap(1, 1), none], axis=0),
        jnp.concatenate([tap(1, 2), tap(1, 0)], axis=0),
    ], axis=1)
    odd_rows = jnp.concatenate([
        jnp.concatenate([tap(2, 1), none, tap(0, 1), none], axis=0),
        jnp.concatenate([tap(2, 2), tap(2, 0), tap(0, 2), tap(0, 0)], axis=0),
    ], axis=1)
    clear_edges(t2w)

    def back_down(i):
        rows = jnp.concatenate([cw[pl.ds(i * R, R)], cw[pl.ds(i * R + 1, R)]], axis=-1)
        rows = rows.reshape(R * W // 2, 8 * C)
        view = drf.reshape(H // 2, 2, W, C)
        for parity, got in enumerate((mm(rows[:, : 4 * C], even_rows), mm(rows, odd_rows))):
            got = got.reshape(R, W // 2, 2 * C)
            view[pl.ds(i * R, R), parity, pl.ds(0, W // 2, 2), :] = got[..., :C]
            view[pl.ds(i * R, R), parity, pl.ds(1, W // 2, 2), :] = got[..., C:]

    def t2_windows(i):
        values = drf[pl.ds(i * R, R)]
        put_windows(t2w, i * R, values)
        return fold(values)

    gcb2 = zero8
    for i in range(H // 2 // R):
        back_down(i)
        gcb2 = gcb2 + t2_windows(2 * i) + t2_windows(2 * i + 1)
    gcb2 = total_of(gcb2)

    centre_s = centre * scale + shift
    mean2 = group_sum(centre_s) * (GROUPS / C)
    off = centre_s - mean2
    var2 = group_sum(spread * scale * scale + off * off) * (GROUPS / C)
    rs2 = lax.rsqrt(var2 + norm_eps)

    def unit2(values):
        return (values * one(scale) + one(shift - mean2)) * one(rs2)

    clear_edges(a2w)

    def front2(i):
        v = unit2(c1[pl.ds(i * R, R)]) * one(1.0 + gain2) + one(bias2)
        prob = normal_cdf(v)
        put_windows(a2w, i * R, v * prob)
        g2p[pl.ds(i * R, R)] = gelu_slope(v, prob)

    rw[0:1] = jnp.zeros((1, W // 2, 3 * C), bf16)

    def conv2(i):
        got = pair_conv(a2w, pair2, i * Q)
        for parity, (place, source) in enumerate(zip(pairs_of(rf, i * Q), pairs_of(x_ref, i * Q))):
            r = source[...].astype(f32) + (got[..., parity * C : (parity + 1) * C] + one(cb2))
            place[...] = r.astype(bf16).astype(f32)
        even = rf[pl.ds(i * R, R), pl.ds(0, W // 2, 2), :]
        odd = rf[pl.ds(i * R, R), pl.ds(1, W // 2, 2), :]
        place = lax.broadcasted_iota(jnp.int32, odd.shape, 1)
        before = jnp.where(place == 0, 0.0, pltpu.roll(odd, 1, 1))
        rw[pl.ds(i * R + 1, R), :, 0:C] = before.astype(bf16)
        rw[pl.ds(i * R + 1, R), :, C : 2 * C] = even.astype(bf16)
        rw[pl.ds(i * R + 1, R), :, 2 * C :] = odd.astype(bf16)

    front2(0)
    for i in range(STEPS):
        if i + 1 < STEPS:
            front2(i + 1)
        conv2(i)

    gkd = mm(down_rows(rw, 0, H // 2), cot_ref[...].reshape(CELLS // 4, 2 * C), TN)
    conv[2] = gkd[:, :C]
    conv[3] = gkd[:, C:]

    def pull(i, s, win_ref, back_ref, slope_ref, out_slope_ref, units, q=Q):
        got = pair_conv(win_ref, back_ref, i * q, q)
        places = zip(pairs_of(slope_ref, i * q, q), pairs_of(out_slope_ref, i * q, q), units)
        for parity, (place, out_place, unit) in enumerate(places):
            dn = got[..., parity * C : (parity + 1) * C] * place[...]
            out_place[...] = dn
            s = s[0] + fold(dn), s[1] + fold(dn * unit)
        return s

    pair_backward(back2, k2_ref)
    sums = (zero8, zero8)
    for i in range(H // 2 // WIDE):
        units = [unit2(ref[...]) for ref in pairs_of(c1, i * WIDE, WIDE)]
        sums = pull(i, sums, t2w, back2, g2p, g2p, units, WIDE)
    gb2, gg2 = [total_of(part) for part in sums]
    mean_du2 = group_sum(gb2 * (1.0 + gain2)) * (1.0 / PER_GROUP)
    mean_duu2 = group_sum(gg2 * (1.0 + gain2)) * (1.0 / PER_GROUP)
    kernel_grad(a2w, t2w, conv.at[1])

    pair_backward(back1, k1_ref)
    clear_edges(t1w)

    def t1_windows(i, s):
        values = c1[pl.ds(i * R, R)]
        du = g2p[pl.ds(i * R, R)] * one(1.0 + gain2)
        ds = (du - one(mean_du2) - unit2(values) * one(mean_duu2)) * one(rs2)
        put_windows(t1w, i * R, ds * one(scale))
        return s[0] + fold(ds * values), s[1] + fold(ds)

    def unit1(ref):
        return (ref[...].astype(f32) - one(mean1)) * one(rs1)

    class_sums = t1_windows(0, (zero8, zero8))
    sums = (zero8, zero8)
    for i in range(STEPS):
        if i + 1 < STEPS:
            class_sums = t1_windows(i + 1, class_sums)
        sums = pull(i, sums, t1w, back1, g1p, slope1_ref, [unit1(ref) for ref in pairs_of(x_ref, i * Q)])
    gsc, gsh = [total_of(part) for part in class_sums]
    gb1, gg1 = [total_of(part) for part in sums]
    mean_du1 = group_sum(gb1 * (1.0 + gain1)) * (1.0 / PER_GROUP)
    mean_duu1 = group_sum(gg1 * (1.0 + gain1)) * (1.0 / PER_GROUP)
    for index, row in enumerate((1.0 + gain1, mean_du1, mean_duu1)):
        factors_ref[8 * index : 8 * index + 8] = row
    gdb = gdb_ref[...]
    rows = [gg1, gb1, gsh * scale, gg2, gb2, gcb2, gdb[:, :C], gdb[:, C:]]
    rows = [row[0:1] for row in rows]
    rows = rows + [jnp.where(mine[:, :C], row[0:1], 0.0) for row in (gsc, gsh)]
    extra = jnp.concatenate(rows + [jnp.zeros((EXTRA - len(rows) - 2 * NCLASS + 2, C), f32)], axis=0)
    if plan.rings:
        put_results(plan, me, 0, conv, results)
        kernel_grad(a1w, t1w, conv.at[0])
        put_results(plan, me, 1, conv, results)
        for ref in results:
            ref[plan.line * 2 * plan.pair_rows :] = extra.astype(ref.dtype)
    else:
        kernel_grad(a1w, t1w, conv.at[0])
        results[0][...] = conv[...]
        results[1][...] = extra


def down_rows(rw, first, rows):
    view = rw.reshape(H // 2 + 1, 2, W // 2, 3 * C)
    taken = [view[pl.ds(first + t // 2, rows), t % 2] for t in range(3)]
    return jnp.concatenate(taken, axis=-1).reshape(rows * W // 2, TAPS * C)


def down_body(rw, kernels, smalls, out_hbm, out_ref, sems):
    kd = jnp.concatenate([kernels[2], kernels[3]], axis=1)
    bias = jnp.concatenate([smalls[6:7, :], smalls[7:8, :]], axis=1)
    copies = []
    for part in range(4):
        rows = slice(part * H // 8, (part + 1) * H // 8)
        got = mm(down_rows(rw, part * H // 8, H // 8), kd) + bias
        out_ref[rows] = got.reshape(H // 8, W // 2, 2 * C).astype(bf16)
        copies.append(pltpu.make_async_copy(out_ref.at[rows], out_hbm.at[rows], sems.at[part]))
        copies[-1].start()
    for copy in copies:
        copy.wait()


def run_down(rw, kernels, smalls):
    shape = (H // 2, W // 2, 2 * C)
    return pl.pallas_call(
        down_body,
        out_shape=jax.ShapeDtypeStruct(shape, bf16),
        in_specs=vmem_specs(3),
        out_specs=pl.BlockSpec(memory_space=pltpu.HBM),
        scratch_shapes=[pltpu.VMEM(shape, bf16), pltpu.SemaphoreType.DMA((4,))],
        compiler_params=limit(8),
        cost_estimate=cost(604, 3 << 20),
        name="down",
    )(rw, kernels, smalls)


def finish_body(x_ref, stats_ref, slope_ref, grad_ref, factors_ref, dx_hbm, dx_ref, sems):
    mean, scale = stats_ref[0:8], stats_ref[8:16]
    gain, mean_du, mean_duu = [factors_ref[8 * k : 8 * k + 8] for k in range(3)]

    def finish(i, carry):
        du = slope_ref[pl.ds(i * R, R)] * one(gain)
        unit = (x_ref[pl.ds(i * R, R)].astype(f32) - one(mean)) * one(scale)
        dx = (du - one(mean_du) - unit * one(mean_duu)) * one(scale)
        dx_ref[pl.ds(i * R, R)] = (grad_ref[pl.ds(i * R, R)] + dx).astype(bf16)
        return carry

    copies = []
    for part in range(4):
        lax.fori_loop(part * H // R // 4, (part + 1) * H // R // 4, finish, 0)
        rows = pl.ds(part * H // 4, H // 4)
        copies.append(pltpu.make_async_copy(dx_ref.at[rows], dx_hbm.at[rows], sems.at[part]))
        copies[-1].start()
    for copy in copies:
        copy.wait()


def run_finish(x, stats, slope, grad, factors):
    return pl.pallas_call(
        finish_body,
        out_shape=jax.ShapeDtypeStruct((H, W, C), bf16),
        in_specs=vmem_specs(5),
        out_specs=pl.BlockSpec(memory_space=pltpu.HBM),
        scratch_shapes=[pltpu.VMEM((H, W, C), bf16), pltpu.SemaphoreType.DMA((4,))],
        compiler_params=limit(8),
        cost_estimate=cost(2, 6 << 20),
        name="finish",
    )(x, stats, slope, grad, factors)


def own_half(odd):
    return (lax.broadcasted_iota(jnp.int32, (8, C), 0) < 4) == (odd == 0)


def put_results(plan, me, index, conv, results):
    left, right = PAIRS[index]
    for core in (0, 1):
        odd = (me ^ core) & 1
        owners = plan.targets(me ^ core)
        for group, result in enumerate(results[4 * core : 4 * core + 4]):
            parts = []
            for owner in owners[group * plan.line : (group + 1) * plan.line]:
                full, half = plan.places(odd, plan.tile_of(owner * plan.conv_rows))
                parts += [conv[k, pl.ds(full, plan.full), :] for k in (left, right)]
                halves = [conv[k, pl.ds(half, 8), :] for k in (left, right)]
                parts.append(jnp.where(own_half(odd), halves[0], pltpu.roll(halves[1], 4, 0)))
            rows = 2 * plan.pair_rows
            for place in range(0, plan.line, 2):
                two = jnp.concatenate(parts[3 * place : 3 * place + 6], axis=0)
                at = (index * plan.line + place) * plan.pair_rows
                result[at : at + rows] = two.astype(result.dtype)


def vmem_specs(count):
    return [pl.BlockSpec(memory_space=pltpu.VMEM)] * count


def cost(mflops, moved):
    return pl.CostEstimate(flops=mflops << 20, bytes_accessed=moved, transcendentals=0)


def limit(size):
    return pltpu.CompilerParams(vmem_limit_bytes=size << 20)


class Plan:
    def __init__(self, sizes, conv_len, dense_len, small_len):
        (_, outer_size), (_, inner_size) = sizes
        count = outer_size * inner_size
        self.sizes, self.line = sizes, inner_size // 2
        self.conv_len, self.dense_len, self.small_len = conv_len, dense_len, small_len
        self.conv_rows, self.dense_rows = conv_len // C, dense_len // C
        powers = inner_size & (inner_size - 1) == 0 and inner_size >= 4 and outer_size == 4
        self.rings = powers and conv_len % C == 0 and dense_len % C == 0 and small_len <= C and self.conv_rows % 8 == 4
        self.dense_pad = max(-(-(self.dense_rows * k % 8 + self.dense_rows) // 8) * 8 for k in range(count))
        self.full = self.conv_rows - 4
        self.window = self.conv_rows + 4
        self.pair_rows = 2 * self.conv_rows
        self.dense_at = 4 * self.full + 16
        self.small_at = self.dense_at + self.dense_pad
        self.own_rows = -(-(self.small_at + 8) // 16) * 16
        self.inner = inner_size
        self.half = count // 2

    def sources(self, me):
        near = [0] + [2 * k for k in reversed(range(1, self.line))]
        low, high = near[: self.line // 2], near[self.line // 2 :]
        held = [low + [k ^ self.inner for k in low], high + [k ^ 2 * self.inner for k in high]]
        held += [[k ^ 2 * self.inner for k in held[0]], [k ^ self.inner for k in held[1]]]
        return [(part, place, me ^ turn) for part, turns in enumerate(held) for place, turn in enumerate(turns)]

    def targets(self, own):
        return [own ^ (plane * self.inner + 2 * k) for plane in range(4) for k in range(self.line)]

    def tile_of(self, row):
        return pl.multiple_of(row // 8 * 8, 8)

    def places(self, odd, first=0):
        return pl.multiple_of(first + 8 * odd, 8), pl.multiple_of(first + self.full * (1 - odd), 8)


def run_block(plan, x, cot, prepared, inputs):
    struct = jax.ShapeDtypeStruct
    shapes = [
        struct((H + 2, W // 2, 3 * C), bf16),
        struct((4, KERNEL_ROWS, C), bf16),
        struct((16, C), f32),
        struct((H, W, C), f32),
        struct((H, W, C), f32),
        struct((24, C), f32),
        struct((NCLASS, EMB), bf16),
        struct((EMB, EMB), bf16),
        struct((EMB, 2 * C), bf16),
        struct((NCLASS, EMB), f32),
    ]
    if plan.rings:
        rows = plan.line * 2 * plan.pair_rows + EXTRA
        shapes += [struct((rows, C), f32)] * 4 + [struct((rows, C), bf16)] * 4
    else:
        shapes += [struct((4, KERNEL_ROWS, C), f32), struct((EXTRA, C), f32)]
    windows = pltpu.VMEM((H + 2, W, 3 * C), bf16)
    plane = pltpu.VMEM((H, W, C), f32)
    return pl.pallas_call(
        functools.partial(block_body, plan),
        out_shape=shapes,
        in_specs=vmem_specs(6 + len(inputs)),
        out_specs=vmem_specs(len(shapes)),
        scratch_shapes=[
            windows,
            windows,
            windows,
            windows,
            plane,
            plane,
            plane,
            plane,
            pltpu.VMEM((4, 12 * C, 2 * C), bf16),
            pltpu.VMEM((4, KERNEL_ROWS, C), f32),
            pltpu.VMEM((MLP_ROWS + 2 * plan.dense_pad, C), f32),
        ],
        compiler_params=limit(40),
        cost_estimate=cost(9000, 16 << 20),
        name="block",
    )(x, cot, *prepared, *inputs)


def pack_body(plan, conv_hbm, dense_hbm, small_hbm, out_ref, conv_ref, dense_ref, small_ref, windows, rows, sems):
    pairs = ((conv_hbm.at[0], conv_ref), (dense_hbm, dense_ref), (small_hbm, small_ref))
    copies = [pltpu.make_async_copy(source, target, sems.at[k]) for k, (source, target) in enumerate(pairs)]
    for copy in copies:
        copy.start()
    me = position_of(plan.sizes)
    odd = me & 1
    windows[...] = jnp.zeros(windows.shape, f32)
    rows[...] = jnp.zeros(rows.shape, f32)
    copies[0].wait()
    for r in range(plan.conv_rows):
        windows[pl.ds(4 * odd + r, 4, plan.window), :] = conv_ref[:, r * C : (r + 1) * C]
    halves = []
    for k in range(4):
        full, half = plan.places(odd, k * plan.window)
        rows[k * plan.full : (k + 1) * plan.full] = windows[pl.ds(full, plan.full), :]
        halves.append(windows[pl.ds(half, 8), :])
    for k in (0, 2):
        at = 4 * plan.full + 4 * k
        rows[at : at + 8] = jnp.where(own_half(odd), halves[k], pltpu.roll(halves[k + 1], 4, 0))
    copies[1].wait()
    first = plan.dense_at + me * plan.dense_rows % 8
    for r in range(plan.dense_rows):
        rows[pl.ds(first + r, 1), :] = dense_ref[0:1, r * C : (r + 1) * C]
    copies[2].wait()
    own = jnp.concatenate([small_ref[0:1, :], jnp.zeros((1, C - plan.small_len), f32)], axis=1)
    own = pltpu.roll(jnp.broadcast_to(own, (8, C)), me * plan.small_len % C, 1)
    rows[plan.small_at : plan.small_at + 1] = own[0:1]
    out_ref[...] = rows[...].astype(bf16)


def run_pack(plan, conv_state, mlp_state, small_state):
    return pl.pallas_call(
        functools.partial(pack_body, plan),
        out_shape=jax.ShapeDtypeStruct((plan.own_rows, C), bf16),
        in_specs=[pl.BlockSpec(memory_space=pltpu.HBM)] * 3,
        out_specs=pl.BlockSpec(memory_space=pltpu.VMEM),
        scratch_shapes=[
            pltpu.VMEM((4, plan.conv_len), f32),
            pltpu.VMEM((4, plan.dense_len), f32),
            pltpu.VMEM((4, plan.small_len), f32),
            pltpu.VMEM((4 * plan.window, C), f32),
            pltpu.VMEM((plan.own_rows, C), f32),
            pltpu.SemaphoreType.DMA((3,)),
        ],
        compiler_params=pltpu.CompilerParams(vmem_limit_bytes=(64 << 20) - (190 << 10)),
        name="pack",
    )(conv_state, mlp_state, small_state)


def merge_body(plan, blocks, groups, *refs):
    keep_ref, received = refs[0], refs[1 : len(refs) - groups]
    outs = refs[len(refs) - groups :]

    def sums(at, size):
        total = keep_ref[at : at + size]
        for ref in received:
            total = total + ref[at : at + size].astype(f32)
        return total

    size = blocks // groups * plan.pair_rows
    extra = sums(2 * blocks * plan.pair_rows, EXTRA)
    for group, out in enumerate(outs):
        parts = [sums(k * blocks * plan.pair_rows + group * size, size) for k in range(2)]
        out[...] = jnp.concatenate(parts + [extra], axis=0).astype(out.dtype)


def run_merge(plan, blocks, groups, keep, received):
    rows = blocks // groups * 2 * plan.pair_rows + EXTRA
    shapes = [jax.ShapeDtypeStruct((rows, C), f32 if group == 0 else bf16) for group in range(groups)]
    return pl.pallas_call(
        functools.partial(merge_body, plan, blocks, groups),
        out_shape=shapes,
        in_specs=vmem_specs(1 + len(received)),
        out_specs=vmem_specs(groups),
        compiler_params=limit(16),
        name="merge",
    )(keep, *received)


def mlp_grads(table, m1_ref, m2_ref, hidden, dss, out_ref):
    prob = normal_cdf(hidden)

    def put(first, values):
        parts = values.shape[1] // C
        for part in range(parts):
            out_ref[pl.ds(first + part, values.shape[0], parts), :] = values[:, part * C : (part + 1) * C]

    def outer(left, right):
        lefts = [a for k, a in enumerate(left) for b in right[: 3 - k]]
        rights = [b for k, a in enumerate(left) for b in right[: 3 - k]]
        return mm(jnp.concatenate(lefts, axis=0), jnp.concatenate(rights, axis=0), TN)

    dp = exact(dss, m2_ref[...], NT) * gelu_slope(hidden, prob)
    put(0, exact(dp, m1_ref[...], NT))
    put(TABLE_ROWS, outer([table], three(dp)))
    put(TABLE_ROWS + M1_ROWS, outer(three(hidden * prob), three(dss)))
    ge1 = jnp.sum(dp, axis=0, keepdims=True)
    ge2 = jnp.sum(dss, axis=0, keepdims=True)
    return [ge1[:, i * C : (i + 1) * C] for i in range(4)] + [ge2[:, i * C : (i + 1) * C] for i in range(2)]


def mlp_body(table_ref, m1_ref, m2_ref, hidden_ref, dss_ref, out_ref, tail_ref):
    tail = mlp_grads(table_ref[...], m1_ref, m2_ref, hidden_ref[...], dss_ref[...], out_ref)
    for i, row in enumerate(tail):
        tail_ref[i : i + 1, :] = row


def run_mlp(table, m1, m2, hidden, dss):
    return pl.pallas_call(
        mlp_body,
        out_shape=[jax.ShapeDtypeStruct((MLP_ROWS, C), f32), jax.ShapeDtypeStruct((6, C), f32)],
        in_specs=vmem_specs(5),
        out_specs=vmem_specs(2),
        compiler_params=limit(32),
        name="mlp_grad",
    )(table, m1, m2, hidden, dss)


def adam(weight, first, second, average, gradient, rate, decay):
    first = beta_one * first + (1.0 - beta_one) * gradient
    second = beta_two * second + (1.0 - beta_two) * gradient * gradient
    first_hat = first * (1.0 / (1.0 - beta_one**STEP))
    second_hat = second * (1.0 / (1.0 - beta_two**STEP))
    weight = weight - rate * (first_hat / (jnp.sqrt(second_hat) + adam_eps) + decay * weight)
    return weight, first, second, ema_decay * average + (1.0 - ema_decay) * weight


def update_body(plan, received_count, *refs):
    keep_ref, received = refs[0], refs[1 : 1 + received_count]
    table_ref, m1_ref, m2_ref, hidden_ref, conv_ref, dense_ref, small_ref = refs[1 + received_count : 8 + received_count]
    conv_new, dense_new, small_new, conv_copy, dense_copy, small_copy = refs[8 + received_count : 14 + received_count]
    block, grads, rows, smalls = refs[14 + received_count :]
    me = position_of(plan.sizes)
    total = keep_ref[...]
    for ref in received:
        total = total + ref[...].astype(f32)
    odd = me & 1
    for index, pair in enumerate(PAIRS):
        at = index * plan.pair_rows
        rest = total[at + 2 * plan.full : at + plan.pair_rows]
        for side, k in enumerate(pair):
            full, half = plan.places(odd, k * plan.window)
            block[pl.ds(full, plan.full), :] = total[at + side * plan.full : at + (side + 1) * plan.full]
            block[pl.ds(half, 8), :] = pltpu.roll(rest, 4, 0) if side else rest
    extra = total[2 * plan.pair_rows :]
    smalls[0:8] = extra[0:8]
    dss = jnp.concatenate([extra[8 : 8 + NCLASS], extra[8 + NCLASS : 8 + 2 * NCLASS]], axis=1)
    tail = mlp_grads(table_ref[...], m1_ref, m2_ref, hidden_ref[...], dss, grads)
    for i, row in enumerate(tail):
        smalls[8 + i : 9 + i, :] = row

    for r in range(plan.conv_rows):
        at = slice(r * C, (r + 1) * C)
        gradient = block[pl.ds(4 * odd + r, 4, plan.window), :]
        new = adam(*[conv_ref[k, :, at] for k in range(4)], gradient, rate_conv, decay_weights)
        for k in range(4):
            conv_new[k, :, at] = new[k]
        conv_copy[:, at] = new[0].astype(bf16)

    start = me * plan.dense_rows
    for r in range(plan.dense_rows):
        at = slice(r * C, (r + 1) * C)
        gradient = grads[pl.ds(start + r, 1), :]
        rate = jnp.where(start + r < TABLE_ROWS, rate_table, rate_dense)
        new = adam(*[dense_ref[k : k + 1, at] for k in range(4)], gradient, rate, decay_weights)
        for k in range(4):
            dense_new[k : k + 1, at] = new[k]
        rows[r : r + 1, :] = new[0]
    dense_copy[...] = rows[...].astype(bf16)

    start = me * plan.small_len
    lane = lax.broadcasted_iota(jnp.int32, (8, C), 1)
    near = jnp.broadcast_to(smalls[pl.ds(start // C, 1), :], (8, C))
    far = jnp.broadcast_to(smalls[pl.ds(start // C + 1, 1), :], (8, C))
    off = C - start % C
    gradient = jnp.where(lane < off, pltpu.roll(near, off, 1), pltpu.roll(far, off, 1))
    gradient = gradient[0:1, 0 : plan.small_len]
    new = adam(*[small_ref[k : k + 1, :] for k in range(4)], gradient, rate_small, 0.0)
    for k in range(4):
        small_new[k : k + 1, :] = new[k]
    small_copy[...] = new[0].astype(bf16)


def run_update(plan, keep, received, mlp, states):
    struct = jax.ShapeDtypeStruct
    shapes = [struct(state.shape, f32) for state in states]
    shapes += [struct((4, plan.conv_len), bf16), struct((plan.dense_rows, C), bf16), struct((1, plan.small_len), bf16)]
    return pl.pallas_call(
        functools.partial(update_body, plan, len(received)),
        out_shape=shapes,
        in_specs=vmem_specs(1 + len(received) + 4 + 3),
        out_specs=vmem_specs(6),
        scratch_shapes=[
            pltpu.VMEM((4 * plan.window, C), f32),
            pltpu.VMEM((MLP_ROWS, C), f32),
            pltpu.VMEM((plan.dense_rows, C), f32),
            pltpu.VMEM((24, C), f32),
        ],
        compiler_params=limit(24),
        name="update",
    )(keep, *received, *mlp, *states)


def swap(values, axis, size, turn):
    return lax.ppermute(values, axis, [(i, i ^ turn) for i in range(size)])


def gather_ring(plan, own, prepare):
    (outer, outer_size), (inner, inner_size) = plan.sizes
    half = plan.line // 2
    line = [swap(own, inner, inner_size, 2 * k) for k in reversed(range(1, plan.line))]
    low, own = lax.optimization_barrier((line[: half - 1], run_copy(own)))
    held = []
    for part, turn in (([own] + low, 1), (line[half - 1 :], 2)):
        part = jnp.stack(part)
        held.append(jnp.concatenate([part, swap(part, outer, outer_size, turn)]))
    late = [swap(part, outer, outer_size, 2 - k) for k, part in enumerate(held)]
    late, prepared = lax.optimization_barrier((late, prepare()))
    held = held + late
    return prepared, held + [swap(part, inner, inner_size, 1) for part in held]


def reduce_ring(plan, keeps, sends, beside):
    (outer, outer_size), (inner, inner_size) = plan.sizes
    mates = [swap(part, inner, inner_size, 1) for part in sends]
    received = []
    for turn in range(1, outer_size):
        part = keeps[turn] + mates[turn].astype(f32)
        received.append(swap(part.astype(bf16), outer, outer_size, turn))
    received, beside = lax.optimization_barrier((received, beside))
    keep, *parts = run_merge(plan, plan.line, plan.line, keeps[0], [mates[0], *received])
    return beside, keep, [swap(parts[k], inner, inner_size, 2 * (k + 1)) for k in reversed(range(plan.line - 1))]


def plain_update(plan, position, grads, extra, mlp, states):
    conv_state, mlp_state, small_state = states
    conv_red = lax.psum_scatter(grads.reshape(4, -1), AXES, scatter_dimension=1, tiled=True)
    extra = lax.psum(extra, AXES)
    dss = jnp.concatenate([extra[8 : 8 + NCLASS], extra[8 + NCLASS : 8 + 2 * NCLASS]], axis=1)
    dense_grad, tail = run_mlp(*mlp, dss)
    dense_red = lax.dynamic_slice_in_dim(dense_grad.reshape(-1), position * plan.dense_len, plan.dense_len)
    flat = jnp.concatenate([extra[:8], tail]).reshape(-1)
    small_red = lax.dynamic_slice_in_dim(flat, position * plan.small_len, plan.small_len)
    flat_index = position * plan.dense_len + jnp.arange(plan.dense_len, dtype=jnp.int32)
    dense_rate = jnp.where(flat_index < NCLASS * EMB, rate_table, rate_dense)
    new = [
        jnp.stack(adam(*state, red, rate, decay))
        for state, red, rate, decay in (
            (conv_state, conv_red, rate_conv, decay_weights),
            (mlp_state, dense_red, dense_rate, decay_weights),
            (small_state, small_red, rate_small, 0.0),
        )
    ]
    return new + [state[0].astype(bf16) for state in new]


def per_device(sizes, samples, cotangent, class_ids, *states):
    conv_state, mlp_state, small_state = states
    plan = Plan(sizes, conv_state.shape[2], mlp_state.shape[1], small_state.shape[1])
    x, cot = samples[0], cotangent[0]
    if plan.rings:
        prepared, inputs = gather_ring(plan, run_pack(plan, *states), lambda: run_prepare(class_ids, x, cot))
    else:
        conv, dense, small = [state[0].astype(bf16) for state in states]
        conv = lax.all_gather(conv, AXES, axis=1, tiled=True).reshape(4, KERNEL_ROWS, C)
        small = lax.all_gather(small, AXES, axis=0, tiled=True).reshape(-1, C)
        dense = lax.all_gather(dense, AXES, axis=0, tiled=True).reshape(MLP_ROWS, C)
        inputs = [conv[0], small, conv[1:], dense]
        prepared = run_prepare(class_ids, x, cot)
    rw, kernels, smalls, slope, grad, factors, table, m1, m2, hidden, *sums = run_block(
        plan, x, cot, prepared, inputs
    )
    out = run_down(rw, kernels, smalls)
    dx = run_finish(x, prepared[0], slope, grad, factors)
    mlp = (table, m1, m2, hidden)
    if plan.rings:
        (out, dx), keep, received = reduce_ring(plan, sums[:4], sums[4:], (out, dx))
        results = run_update(plan, keep, received, mlp, states)
    else:
        results = plain_update(plan, lax.axis_index(AXES), *sums, mlp, states)
    conv_new, mlp_new, small_new, conv_copy, mlp_copy, small_copy = results
    return out[None], dx[None], conv_new, mlp_new, small_new, conv_copy, mlp_copy.reshape(-1), small_copy.reshape(-1)


def solution(mesh):
    sizes = tuple((axis, mesh.shape[axis]) for axis in AXES)

    def body(*args):
        return per_device(sizes, *args)

    return jax.shard_map(
        body,
        mesh=mesh,
        in_specs=(
            P(AXES, None, None, None),
            P(AXES, None, None, None),
            P(AXES),
            P(None, None, AXES),
            P(None, AXES),
            P(None, AXES),
        ),
        out_specs=(
            P(AXES, None, None, None),
            P(AXES, None, None, None),
            P(None, None, AXES),
            P(None, AXES),
            P(None, AXES),
            P(None, AXES),
            P(AXES),
            P(AXES),
        ),
        check_vma=False,
    )
```

```python
import functools

import jax
import jax.numpy as jnp
from jax import lax
from jax.experimental import pallas as pl
from jax.experimental.pallas import tpu as pltpu
from jax.sharding import PartitionSpec as P

C = 128
EMB = 512
GROUPS = 8
H = 64
W = 64
NCLASS = 16
STEP = 10
TAPS = 9
CELLS = H * W
PER_GROUP = CELLS * (C // GROUPS)
TABLE_ROWS = NCLASS * EMB // C
M1_ROWS = EMB * EMB // C
M2_ROWS = EMB * 2
MLP_ROWS = TABLE_ROWS + M1_ROWS + M2_ROWS
KERNEL_ROWS = TAPS * C
AXES = ("dp", "fsdp")

beta_one = 0.9
beta_two = 0.999
adam_eps = 1e-08
ema_decay = 0.99
norm_eps = 1e-05
rate_conv = 0.08
rate_table = 0.6
rate_dense = 0.1
rate_small = 0.15
decay_weights = 0.01

f32 = jnp.float32
bf16 = jnp.bfloat16
NN = (((1,), (0,)), ((), ()))
NT = (((1,), (1,)), ((), ()))
TN = (((0,), (0,)), ((), ()))
EXTRA = -(-(8 + 2 * NCLASS) // 16) * 16
PAIRS = ((2, 3), (1, 0))
R = 4
Q = 2
WIDE = 8
STEPS = H // R
PART = CELLS // STEPS


def each(count, step, carry):
    for index in range(count):
        carry = step(index, carry)
    return carry


def mm(a, b, dims=NN):
    return lax.dot_general(a, b, dims, preferred_element_type=f32)


def three(v):
    high = v.astype(bf16)
    rest = v - high.astype(f32)
    mid = rest.astype(bf16)
    return high, mid, (rest - mid.astype(f32)).astype(bf16)


def exact(values, weights, dims=NN):
    rows = values.shape[0]
    got = mm(jnp.concatenate(three(values), axis=0), weights, dims)
    return got[:rows] + got[rows : 2 * rows] + got[2 * rows :]


def group_sum(rows):
    lane = lax.broadcasted_iota(jnp.int32, rows.shape, 1)
    for step in (1, 2, 4, 8):
        up = pltpu.roll(rows, C - step, 1)
        down = pltpu.roll(rows, step, 1)
        rows = rows + jnp.where((lane & step) == 0, up, down)
    return rows


def fold(values):
    return jnp.sum(values.reshape(-1, 8, values.shape[-1]), axis=0)


def total_of(partial):
    return jnp.broadcast_to(jnp.sum(partial, axis=0, keepdims=True), partial.shape)


def one(rows):
    return rows[0:1].reshape(1, 1, C)


def normal_cdf(v):
    return 0.5 * (1.0 + lax.erf(v * 0.7071067811865476))


def gelu_slope(v, prob):
    return prob + v * (jnp.exp(-0.5 * v * v) * 0.3989422804014327)


def put_windows(win_ref, row, values):
    rows = values.shape[0]
    place = lax.broadcasted_iota(jnp.int32, values.shape, 1)
    left = jnp.where(place == 0, 0.0, pltpu.roll(values, 1, 1))
    right = jnp.where(place == W - 1, 0.0, pltpu.roll(values, W - 1, 1))
    win_ref[pl.ds(row + 1, rows), :, 0:C] = left.astype(bf16)
    win_ref[pl.ds(row + 1, rows), :, C : 2 * C] = values.astype(bf16)
    win_ref[pl.ds(row + 1, rows), :, 2 * C : 3 * C] = right.astype(bf16)


def clear_edges(win_ref):
    edge = jnp.zeros((1,) + tuple(win_ref.shape[1:]), win_ref.dtype)
    win_ref[0:1] = edge
    win_ref[H + 1 : H + 2] = edge


def pair_forward(pair_ref, kernel_ref):
    zero = jnp.zeros((3 * C, C), bf16)
    pair_ref[0 : TAPS * C, 0:C] = kernel_ref[...]
    pair_ref[TAPS * C :, 0:C] = zero
    pair_ref[0 : 3 * C, C:] = zero
    pair_ref[3 * C :, C:] = kernel_ref[...]


def flip(block):
    return jnp.transpose(block.astype(f32)).astype(bf16)


def pair_backward(pair_ref, kernel_ref):
    zero = jnp.zeros((3 * C, C), bf16)
    pair_ref[TAPS * C :, 0:C] = zero
    pair_ref[0 : 3 * C, C:] = zero
    for tap in range(TAPS):
        block = flip(kernel_ref[(TAPS - 1 - tap) * C : (TAPS - tap) * C, :])
        pair_ref[tap * C : (tap + 1) * C, 0:C] = block
        pair_ref[(tap + 3) * C : (tap + 4) * C, C:] = block


def pair_conv(win_ref, pair_ref, first, q=Q):
    view = win_ref.reshape(H // 2 + 1, 2, W, 3 * C)
    taken = [view[pl.ds(first + t // 2, q), t % 2] for t in range(4)]
    stacked = jnp.concatenate(taken, axis=-1).reshape(q * W, 12 * C)
    return mm(stacked, pair_ref[...]).reshape(q, W, 2 * C)


def pairs_of(ref, first, q=Q):
    view = ref.reshape(H // 2, 2, W, C)
    return [view.at[pl.ds(first, q), parity] for parity in range(2)]


def kernel_grad(act_ref, win_ref, out_ref):
    left = act_ref[1 : H + 1, :, C : 2 * C].reshape(CELLS, C)
    right = jnp.concatenate([win_ref[t : t + H] for t in range(3)], axis=-1)
    got = mm(left, right.reshape(CELLS, TAPS * C), TN)
    for t in range(TAPS):
        out_ref[t * C : (t + 1) * C, :] = got[:, (TAPS - 1 - t) * C : (TAPS - t) * C]


def position_of(sizes):
    (outer, _), (inner, inner_size) = sizes
    return lax.axis_index(outer) * inner_size + lax.axis_index(inner)


def prepare_body(cls_ref, x_ref, cot_ref, stats_ref, cw, gdb_ref, hot_ref):
    hot_ref[...] = (lax.broadcasted_iota(jnp.int32, hot_ref.shape, 0) == cls_ref[0]).astype(f32)
    zero8 = jnp.zeros((8, C), f32)

    def read_x(i):
        return x_ref[pl.ds(i * R, R)].astype(f32)

    total = each(H // R, lambda i, s: s + fold(read_x(i)), zero8)
    mean = group_sum(total_of(total)) * (1.0 / PER_GROUP)

    def square_x(i, s):
        d = read_x(i) - one(mean)
        return s + fold(d * d)

    var = group_sum(total_of(each(H // R, square_x, zero8))) * (1.0 / PER_GROUP)
    stats_ref[0:8] = mean
    stats_ref[8:16] = lax.rsqrt(var + norm_eps)
    cw[H // 2 : H // 2 + 1] = jnp.zeros((1, W // 2, 4 * C), bf16)

    def cot_windows(i, s):
        values = cot_ref[pl.ds(i * R, R)].astype(f32)
        place = lax.broadcasted_iota(jnp.int32, values.shape, 1)
        after = jnp.where(place == W // 2 - 1, 0.0, pltpu.roll(values, W // 2 - 1, 1))
        cw[pl.ds(i * R, R), :, 0 : 2 * C] = values.astype(bf16)
        cw[pl.ds(i * R, R), :, 2 * C :] = after.astype(bf16)
        return s + fold(values)

    gdb_ref[...] = total_of(each(H // 2 // R, cot_windows, jnp.zeros((8, 2 * C), f32)))


def copy_body(own_ref, near_ref):
    near_ref[...] = own_ref[...]


def run_copy(own):
    return pl.pallas_call(
        copy_body,
        out_shape=jax.ShapeDtypeStruct(own.shape, own.dtype),
        in_specs=vmem_specs(1),
        out_specs=pl.BlockSpec(memory_space=pltpu.VMEM),
        compiler_params=limit(4),
        cost_estimate=cost(0, 1 << 17),
        name="copy_own",
    )(own)


def run_prepare(class_ids, x, cot):
    struct = jax.ShapeDtypeStruct
    return pl.pallas_call(
        prepare_body,
        out_shape=[struct((16, C), f32), struct((H // 2 + 1, W // 2, 4 * C), bf16), struct((8, 2 * C), f32), struct((NCLASS, 2 * C), f32)],
        in_specs=[pl.BlockSpec(memory_space=pltpu.SMEM)] + vmem_specs(2),
        out_specs=vmem_specs(4),
        compiler_params=limit(8),
        cost_estimate=cost(2, 3 << 20),
        name="prepare",
    )(class_ids, x, cot)


def block_body(plan, *refs):
    refs = list(refs)
    count = 8 if plan.rings else 4
    x_ref, cot_ref, stats_ref, cw, gdb_ref, hot_ref = refs[:6]
    inputs = refs[6 : 6 + count]
    rw, kernels, smalls, slope1_ref, drf, factors_ref, table_ref, m1_ref, m2_ref, hidden_ref = refs[6 + count : 16 + count]
    made = 24 + count if plan.rings else 18 + count
    results = refs[16 + count : made]
    a1w, a2w, t1w, t2w, c1, g1p, g2p, rf, pairs, conv, dense = refs[made:]
    kernels_f = conv
    me = position_of(plan.sizes)
    k1_ref, k2_ref, kd0_ref, kd1_ref = [kernels.at[k] for k in range(4)]
    pair1, pair2, back1, back2 = [pairs.at[k] for k in range(4)]
    zero8 = jnp.zeros((8, C), f32)

    def take(k, part, place, owner):
        odd = owner & 1
        first = owner // 2 * plan.pair_rows
        full = plan.full
        mine = inputs[part][place, k * full : (k + 1) * full]
        mate = inputs[part + 4][place, k * full : (k + 1) * full]
        kernels_f[k, pl.ds(pl.multiple_of(first + (full + 8) * odd, 8), full), :] = mine.astype(f32)
        kernels_f[k, pl.ds(pl.multiple_of(first + (full + 8) * (1 - odd), 8), full), :] = mate.astype(f32)
        halves = [inputs[p][place, 4 * full : 4 * full + 16].astype(f32) for p in (part, part + 4)]
        halves = [v[8 * (k // 2) : 8 * (k // 2) + 8] for v in halves]
        if k % 2 == 1:
            halves = [pltpu.roll(v, 4, 0) for v in halves]
        kernels_f[k, pl.ds(pl.multiple_of(first + full, 8), 8), :] = jnp.where(own_half(odd), *halves)

    if plan.rings:
        shards = plan.sources(me)
        small = jnp.zeros((16, C), f32)
        row = lax.broadcasted_iota(jnp.int32, (16, C), 0)
        lane = lax.broadcasted_iota(jnp.int32, (16, C), 1)
        for part, place, owner in shards:
            take(0, part, place, owner)
            for p, device in ((part, owner), (part + 4, owner ^ 1)):
                at = row * C + lane - device * plan.small_len
                own = inputs[p][place, plan.small_at - 8 : plan.small_at + 8].astype(f32)[8:9]
                small = jnp.where((at >= 0) & (at < plan.small_len), jnp.broadcast_to(own, (16, C)), small)
        smalls[...] = small
        k1_ref[...] = kernels_f[0].astype(bf16)
    else:
        k1_ref[...] = inputs[0][...]
        smalls[0:14] = inputs[1][...].astype(f32)

    def take_rest(step, steps):
        if not plan.rings:
            return
        if step == 0:
            dense[...] = jnp.zeros(dense.shape, f32)
        for part, place, owner in shards[step::steps]:
            for k in (1, 2, 3):
                take(k, part, place, owner)
            for p, device in ((part, owner), (part + 4, owner ^ 1)):
                values = inputs[p][place, plan.dense_at : plan.small_at + 8].astype(f32)
                first = plan.tile_of(device * plan.dense_rows)
                dense[pl.ds(first, plan.dense_pad), :] += values[: plan.dense_pad]

    def small_row(index):
        return jnp.broadcast_to(smalls[index : index + 1, :], (8, C))

    def small_run(first, count):
        return jnp.concatenate([smalls[first + i : first + i + 1, :] for i in range(count)], axis=1)

    gain1, bias1, cb1, gain2, bias2, cb2 = [small_row(i) for i in range(6)]
    mean1, rs1 = stats_ref[0:8], stats_ref[8:16]
    slope1 = rs1 * (1.0 + gain1)

    pair_forward(pair1, k1_ref)
    clear_edges(a1w)

    def front1(i):
        v = (x_ref[pl.ds(i * R, R)].astype(f32) - one(mean1)) * one(slope1) + one(bias1)
        prob = normal_cdf(v)
        put_windows(a1w, i * R, v * prob)
        g1p[pl.ds(i * R, R)] = gelu_slope(v, prob)

    moments = []

    def conv1(i):
        got = pair_conv(a1w, pair1, i * Q)
        values = [got[..., parity * C : (parity + 1) * C] + one(cb1) for parity in range(2)]
        for place, value in zip(pairs_of(c1, i * Q), values):
            place[...] = value
        centre = total_of(fold(values[0]) + fold(values[1])) * (1.0 / PART)
        off = [value - one(centre) for value in values]
        moments.append((centre, fold(off[0] * off[0]) + fold(off[1] * off[1])))

    front1(0)
    for i in range(STEPS):
        if i + 1 < STEPS:
            front1(i + 1)
        conv1(i)
        take_rest(i, STEPS)
    centre = sum(part[0] for part in moments) * (1.0 / STEPS)
    spread = sum(total_of(part[1]) + PART * (part[0] - centre) * (part[0] - centre) for part in moments) * (1.0 / CELLS)

    if plan.rings:
        kernels[1:4] = conv[1:4].astype(bf16)
    else:
        kernels[1:4] = inputs[2][...]
        dense[0:MLP_ROWS] = inputs[3][...].astype(f32)

    def lanes(first, rows, parts):
        pieces = [dense[pl.ds(first + part, rows, parts), :] for part in range(parts)]
        return jnp.concatenate(pieces, axis=1).astype(bf16)

    table_ref[...] = lanes(0, NCLASS, EMB // C)
    m1_ref[...] = lanes(TABLE_ROWS, EMB, EMB // C)
    m2_ref[...] = lanes(TABLE_ROWS + M1_ROWS, EMB, 2)
    hidden = mm(table_ref[...], m1_ref[...]) + small_run(8, 4)
    hidden_ref[...] = hidden
    act = hidden * normal_cdf(hidden)
    ss = exact(act, m2_ref[...]) + small_run(12, 2)
    mine = hot_ref[...] > 0.5
    chosen = jnp.sum(jnp.where(mine, ss, 0.0), axis=0, keepdims=True)
    scale = jnp.broadcast_to(1.0 + chosen[:, :C], (8, C))
    shift = jnp.broadcast_to(chosen[:, C:], (8, C))
    pair_forward(pair2, k2_ref)

    kd = jnp.concatenate([kd0_ref[...], kd1_ref[...]], axis=1)

    def tap(i, j):
        return flip(kd[(3 * i + j) * C : (3 * i + j + 1) * C, :])

    none = jnp.zeros((2 * C, C), bf16)
    even_rows = jnp.concatenate([
        jnp.concatenate([tap(1, 1), none], axis=0),
        jnp.concatenate([tap(1, 2), tap(1, 0)], axis=0),
    ], axis=1)
    odd_rows = jnp.concatenate([
        jnp.concatenate([tap(2, 1), none, tap(0, 1), none], axis=0),
        jnp.concatenate([tap(2, 2), tap(2, 0), tap(0, 2), tap(0, 0)], axis=0),
    ], axis=1)
    clear_edges(t2w)

    def back_down(i):
        rows = jnp.concatenate([cw[pl.ds(i * R, R)], cw[pl.ds(i * R + 1, R)]], axis=-1)
        rows = rows.reshape(R * W // 2, 8 * C)
        view = drf.reshape(H // 2, 2, W, C)
        for parity, got in enumerate((mm(rows[:, : 4 * C], even_rows), mm(rows, odd_rows))):
            got = got.reshape(R, W // 2, 2 * C)
            view[pl.ds(i * R, R), parity, pl.ds(0, W // 2, 2), :] = got[..., :C]
            view[pl.ds(i * R, R), parity, pl.ds(1, W // 2, 2), :] = got[..., C:]

    def t2_windows(i):
        values = drf[pl.ds(i * R, R)]
        put_windows(t2w, i * R, values)
        return fold(values)

    gcb2 = zero8
    for i in range(H // 2 // R):
        back_down(i)
        gcb2 = gcb2 + t2_windows(2 * i) + t2_windows(2 * i + 1)
    gcb2 = total_of(gcb2)

    centre_s = centre * scale + shift
    mean2 = group_sum(centre_s) * (GROUPS / C)
    off = centre_s - mean2
    var2 = group_sum(spread * scale * scale + off * off) * (GROUPS / C)
    rs2 = lax.rsqrt(var2 + norm_eps)

    def unit2(values):
        return (values * one(scale) + one(shift - mean2)) * one(rs2)

    clear_edges(a2w)

    def front2(i):
        v = unit2(c1[pl.ds(i * R, R)]) * one(1.0 + gain2) + one(bias2)
        prob = normal_cdf(v)
        put_windows(a2w, i * R, v * prob)
        g2p[pl.ds(i * R, R)] = gelu_slope(v, prob)

    rw[0:1] = jnp.zeros((1, W // 2, 3 * C), bf16)

    def conv2(i):
        got = pair_conv(a2w, pair2, i * Q)
        for parity, (place, source) in enumerate(zip(pairs_of(rf, i * Q), pairs_of(x_ref, i * Q))):
            r = source[...].astype(f32) + (got[..., parity * C : (parity + 1) * C] + one(cb2))
            place[...] = r.astype(bf16).astype(f32)
        even = rf[pl.ds(i * R, R), pl.ds(0, W // 2, 2), :]
        odd = rf[pl.ds(i * R, R), pl.ds(1, W // 2, 2), :]
        place = lax.broadcasted_iota(jnp.int32, odd.shape, 1)
        before = jnp.where(place == 0, 0.0, pltpu.roll(odd, 1, 1))
        rw[pl.ds(i * R + 1, R), :, 0:C] = before.astype(bf16)
        rw[pl.ds(i * R + 1, R), :, C : 2 * C] = even.astype(bf16)
        rw[pl.ds(i * R + 1, R), :, 2 * C :] = odd.astype(bf16)

    front2(0)
    for i in range(STEPS):
        if i + 1 < STEPS:
            front2(i + 1)
        conv2(i)

    gkd = mm(down_rows(rw, 0, H // 2), cot_ref[...].reshape(CELLS // 4, 2 * C), TN)
    conv[2] = gkd[:, :C]
    conv[3] = gkd[:, C:]

    def pull(i, s, win_ref, back_ref, slope_ref, out_slope_ref, units, q=Q):
        got = pair_conv(win_ref, back_ref, i * q, q)
        places = zip(pairs_of(slope_ref, i * q, q), pairs_of(out_slope_ref, i * q, q), units)
        for parity, (place, out_place, unit) in enumerate(places):
            dn = got[..., parity * C : (parity + 1) * C] * place[...]
            out_place[...] = dn
            s = s[0] + fold(dn), s[1] + fold(dn * unit)
        return s

    pair_backward(back2, k2_ref)
    sums = (zero8, zero8)
    for i in range(H // 2 // WIDE):
        units = [unit2(ref[...]) for ref in pairs_of(c1, i * WIDE, WIDE)]
        sums = pull(i, sums, t2w, back2, g2p, g2p, units, WIDE)
    gb2, gg2 = [total_of(part) for part in sums]
    mean_du2 = group_sum(gb2 * (1.0 + gain2)) * (1.0 / PER_GROUP)
    mean_duu2 = group_sum(gg2 * (1.0 + gain2)) * (1.0 / PER_GROUP)
    kernel_grad(a2w, t2w, conv.at[1])

    pair_backward(back1, k1_ref)
    clear_edges(t1w)

    def t1_windows(i, s):
        values = c1[pl.ds(i * R, R)]
        du = g2p[pl.ds(i * R, R)] * one(1.0 + gain2)
        ds = (du - one(mean_du2) - unit2(values) * one(mean_duu2)) * one(rs2)
        put_windows(t1w, i * R, ds * one(scale))
        return s[0] + fold(ds * values), s[1] + fold(ds)

    def unit1(ref):
        return (ref[...].astype(f32) - one(mean1)) * one(rs1)

    class_sums = t1_windows(0, (zero8, zero8))
    sums = (zero8, zero8)
    for i in range(STEPS):
        if i + 1 < STEPS:
            class_sums = t1_windows(i + 1, class_sums)
        sums = pull(i, sums, t1w, back1, g1p, slope1_ref, [unit1(ref) for ref in pairs_of(x_ref, i * Q)])
    gsc, gsh = [total_of(part) for part in class_sums]
    gb1, gg1 = [total_of(part) for part in sums]
    mean_du1 = group_sum(gb1 * (1.0 + gain1)) * (1.0 / PER_GROUP)
    mean_duu1 = group_sum(gg1 * (1.0 + gain1)) * (1.0 / PER_GROUP)
    for index, row in enumerate((1.0 + gain1, mean_du1, mean_duu1)):
        factors_ref[8 * index : 8 * index + 8] = row
    gdb = gdb_ref[...]
    rows = [gg1, gb1, gsh * scale, gg2, gb2, gcb2, gdb[:, :C], gdb[:, C:]]
    rows = [row[0:1] for row in rows]
    rows = rows + [jnp.where(mine[:, :C], row[0:1], 0.0) for row in (gsc, gsh)]
    extra = jnp.concatenate(rows + [jnp.zeros((EXTRA - len(rows) - 2 * NCLASS + 2, C), f32)], axis=0)
    if plan.rings:
        put_results(plan, me, 0, conv, results)
        kernel_grad(a1w, t1w, conv.at[0])
        put_results(plan, me, 1, conv, results)
        for ref in results:
            ref[plan.line * 2 * plan.pair_rows :] = extra.astype(ref.dtype)
    else:
        kernel_grad(a1w, t1w, conv.at[0])
        results[0][...] = conv[...]
        results[1][...] = extra


def down_rows(rw, first, rows):
    view = rw.reshape(H // 2 + 1, 2, W // 2, 3 * C)
    taken = [view[pl.ds(first + t // 2, rows), t % 2] for t in range(3)]
    return jnp.concatenate(taken, axis=-1).reshape(rows * W // 2, TAPS * C)


def down_body(rw, kernels, smalls, out_hbm, out_ref, sems):
    kd = jnp.concatenate([kernels[2], kernels[3]], axis=1)
    bias = jnp.concatenate([smalls[6:7, :], smalls[7:8, :]], axis=1)
    copies = []
    for part in range(4):
        rows = slice(part * H // 8, (part + 1) * H // 8)
        got = mm(down_rows(rw, part * H // 8, H // 8), kd) + bias
        out_ref[rows] = got.reshape(H // 8, W // 2, 2 * C).astype(bf16)
        copies.append(pltpu.make_async_copy(out_ref.at[rows], out_hbm.at[rows], sems.at[part]))
        copies[-1].start()
    for copy in copies:
        copy.wait()


def run_down(rw, kernels, smalls):
    shape = (H // 2, W // 2, 2 * C)
    return pl.pallas_call(
        down_body,
        out_shape=jax.ShapeDtypeStruct(shape, bf16),
        in_specs=vmem_specs(3),
        out_specs=pl.BlockSpec(memory_space=pltpu.HBM),
        scratch_shapes=[pltpu.VMEM(shape, bf16), pltpu.SemaphoreType.DMA((4,))],
        compiler_params=limit(8),
        cost_estimate=cost(604, 3 << 20),
        name="down",
    )(rw, kernels, smalls)


def finish_body(x_ref, stats_ref, slope_ref, grad_ref, factors_ref, dx_hbm, dx_ref, sems):
    mean, scale = stats_ref[0:8], stats_ref[8:16]
    gain, mean_du, mean_duu = [factors_ref[8 * k : 8 * k + 8] for k in range(3)]

    def finish(i, carry):
        du = slope_ref[pl.ds(i * R, R)] * one(gain)
        unit = (x_ref[pl.ds(i * R, R)].astype(f32) - one(mean)) * one(scale)
        dx = (du - one(mean_du) - unit * one(mean_duu)) * one(scale)
        dx_ref[pl.ds(i * R, R)] = (grad_ref[pl.ds(i * R, R)] + dx).astype(bf16)
        return carry

    copies = []
    for part in range(4):
        lax.fori_loop(part * H // R // 4, (part + 1) * H // R // 4, finish, 0)
        rows = pl.ds(part * H // 4, H // 4)
        copies.append(pltpu.make_async_copy(dx_ref.at[rows], dx_hbm.at[rows], sems.at[part]))
        copies[-1].start()
    for copy in copies:
        copy.wait()


def run_finish(x, stats, slope, grad, factors):
    return pl.pallas_call(
        finish_body,
        out_shape=jax.ShapeDtypeStruct((H, W, C), bf16),
        in_specs=vmem_specs(5),
        out_specs=pl.BlockSpec(memory_space=pltpu.HBM),
        scratch_shapes=[pltpu.VMEM((H, W, C), bf16), pltpu.SemaphoreType.DMA((4,))],
        compiler_params=limit(8),
        cost_estimate=cost(2, 6 << 20),
        name="finish",
    )(x, stats, slope, grad, factors)


def own_half(odd):
    return (lax.broadcasted_iota(jnp.int32, (8, C), 0) < 4) == (odd == 0)


def put_results(plan, me, index, conv, results):
    left, right = PAIRS[index]
    for core in (0, 1):
        odd = (me ^ core) & 1
        owners = plan.targets(me ^ core)
        for group, result in enumerate(results[4 * core : 4 * core + 4]):
            parts = []
            for owner in owners[group * plan.line : (group + 1) * plan.line]:
                full, half = plan.places(odd, plan.tile_of(owner * plan.conv_rows))
                parts += [conv[k, pl.ds(full, plan.full), :] for k in (left, right)]
                halves = [conv[k, pl.ds(half, 8), :] for k in (left, right)]
                parts.append(jnp.where(own_half(odd), halves[0], pltpu.roll(halves[1], 4, 0)))
            rows = 2 * plan.pair_rows
            for place in range(0, plan.line, 2):
                two = jnp.concatenate(parts[3 * place : 3 * place + 6], axis=0)
                at = (index * plan.line + place) * plan.pair_rows
                result[at : at + rows] = two.astype(result.dtype)


def vmem_specs(count):
    return [pl.BlockSpec(memory_space=pltpu.VMEM)] * count


def cost(mflops, moved):
    return pl.CostEstimate(flops=mflops << 20, bytes_accessed=moved, transcendentals=0)


def limit(size):
    return pltpu.CompilerParams(vmem_limit_bytes=size << 20)


class Plan:
    def __init__(self, sizes, conv_len, dense_len, small_len):
        (_, outer_size), (_, inner_size) = sizes
        count = outer_size * inner_size
        self.sizes, self.line = sizes, inner_size // 2
        self.conv_len, self.dense_len, self.small_len = conv_len, dense_len, small_len
        self.conv_rows, self.dense_rows = conv_len // C, dense_len // C
        powers = inner_size & (inner_size - 1) == 0 and inner_size >= 4 and outer_size == 4
        self.rings = powers and conv_len % C == 0 and dense_len % C == 0 and small_len <= C and self.conv_rows % 8 == 4
        self.dense_pad = max(-(-(self.dense_rows * k % 8 + self.dense_rows) // 8) * 8 for k in range(count))
        self.full = self.conv_rows - 4
        self.window = self.conv_rows + 4
        self.pair_rows = 2 * self.conv_rows
        self.dense_at = 4 * self.full + 16
        self.small_at = self.dense_at + self.dense_pad
        self.own_rows = -(-(self.small_at + 8) // 16) * 16
        self.inner = inner_size
        self.half = count // 2

    def sources(self, me):
        near = [0] + [2 * k for k in reversed(range(1, self.line))]
        low, high = near[: self.line // 2], near[self.line // 2 :]
        held = [low + [k ^ self.inner for k in low], high + [k ^ 2 * self.inner for k in high]]
        held += [[k ^ 2 * self.inner for k in held[0]], [k ^ self.inner for k in held[1]]]
        return [(part, place, me ^ turn) for part, turns in enumerate(held) for place, turn in enumerate(turns)]

    def targets(self, own):
        return [own ^ (plane * self.inner + 2 * k) for plane in range(4) for k in range(self.line)]

    def tile_of(self, row):
        return pl.multiple_of(row // 8 * 8, 8)

    def places(self, odd, first=0):
        return pl.multiple_of(first + 8 * odd, 8), pl.multiple_of(first + self.full * (1 - odd), 8)


def run_block(plan, x, cot, prepared, inputs):
    struct = jax.ShapeDtypeStruct
    shapes = [
        struct((H + 2, W // 2, 3 * C), bf16),
        struct((4, KERNEL_ROWS, C), bf16),
        struct((16, C), f32),
        struct((H, W, C), f32),
        struct((H, W, C), f32),
        struct((24, C), f32),
        struct((NCLASS, EMB), bf16),
        struct((EMB, EMB), bf16),
        struct((EMB, 2 * C), bf16),
        struct((NCLASS, EMB), f32),
    ]
    if plan.rings:
        rows = plan.line * 2 * plan.pair_rows + EXTRA
        shapes += [struct((rows, C), f32)] * 4 + [struct((rows, C), bf16)] * 4
    else:
        shapes += [struct((4, KERNEL_ROWS, C), f32), struct((EXTRA, C), f32)]
    windows = pltpu.VMEM((H + 2, W, 3 * C), bf16)
    plane = pltpu.VMEM((H, W, C), f32)
    return pl.pallas_call(
        functools.partial(block_body, plan),
        out_shape=shapes,
        in_specs=vmem_specs(6 + len(inputs)),
        out_specs=vmem_specs(len(shapes)),
        scratch_shapes=[
            windows,
            windows,
            windows,
            windows,
            plane,
            plane,
            plane,
            plane,
            pltpu.VMEM((4, 12 * C, 2 * C), bf16),
            pltpu.VMEM((4, KERNEL_ROWS, C), f32),
            pltpu.VMEM((MLP_ROWS + 2 * plan.dense_pad, C), f32),
        ],
        compiler_params=limit(40),
        cost_estimate=cost(9000, 16 << 20),
        name="block",
    )(x, cot, *prepared, *inputs)


def pack_body(plan, conv_hbm, dense_hbm, small_hbm, out_ref, conv_ref, dense_ref, small_ref, windows, rows, sems):
    pairs = ((conv_hbm.at[0], conv_ref), (dense_hbm, dense_ref), (small_hbm, small_ref))
    copies = [pltpu.make_async_copy(source, target, sems.at[k]) for k, (source, target) in enumerate(pairs)]
    for copy in copies:
        copy.start()
    me = position_of(plan.sizes)
    odd = me & 1
    windows[...] = jnp.zeros(windows.shape, f32)
    rows[...] = jnp.zeros(rows.shape, f32)
    copies[0].wait()
    for r in range(plan.conv_rows):
        windows[pl.ds(4 * odd + r, 4, plan.window), :] = conv_ref[:, r * C : (r + 1) * C]
    halves = []
    for k in range(4):
        full, half = plan.places(odd, k * plan.window)
        rows[k * plan.full : (k + 1) * plan.full] = windows[pl.ds(full, plan.full), :]
        halves.append(windows[pl.ds(half, 8), :])
    for k in (0, 2):
        at = 4 * plan.full + 4 * k
        rows[at : at + 8] = jnp.where(own_half(odd), halves[k], pltpu.roll(halves[k + 1], 4, 0))
    copies[1].wait()
    first = plan.dense_at + me * plan.dense_rows % 8
    for r in range(plan.dense_rows):
        rows[pl.ds(first + r, 1), :] = dense_ref[0:1, r * C : (r + 1) * C]
    copies[2].wait()
    own = jnp.concatenate([small_ref[0:1, :], jnp.zeros((1, C - plan.small_len), f32)], axis=1)
    own = pltpu.roll(jnp.broadcast_to(own, (8, C)), me * plan.small_len % C, 1)
    rows[plan.small_at : plan.small_at + 1] = own[0:1]
    out_ref[...] = rows[...].astype(bf16)


def run_pack(plan, conv_state, mlp_state, small_state):
    return pl.pallas_call(
        functools.partial(pack_body, plan),
        out_shape=jax.ShapeDtypeStruct((plan.own_rows, C), bf16),
        in_specs=[pl.BlockSpec(memory_space=pltpu.HBM)] * 3,
        out_specs=pl.BlockSpec(memory_space=pltpu.VMEM),
        scratch_shapes=[
            pltpu.VMEM((4, plan.conv_len), f32),
            pltpu.VMEM((4, plan.dense_len), f32),
            pltpu.VMEM((4, plan.small_len), f32),
            pltpu.VMEM((5 * plan.window, C), f32),
            pltpu.VMEM((plan.own_rows, C), f32),
            pltpu.SemaphoreType.DMA((3,)),
        ],
        compiler_params=pltpu.CompilerParams(vmem_limit_bytes=(64 << 20) - (190 << 10)),
        name="pack",
    )(conv_state, mlp_state, small_state)


def merge_body(plan, blocks, groups, *refs):
    keep_ref, received = refs[0], refs[1 : len(refs) - groups]
    outs = refs[len(refs) - groups :]

    def sums(at, size):
        total = keep_ref[at : at + size]
        for ref in received:
            total = total + ref[at : at + size].astype(f32)
        return total

    size = blocks // groups * plan.pair_rows
    extra = sums(2 * blocks * plan.pair_rows, EXTRA)
    for group, out in enumerate(outs):
        parts = [sums(k * blocks * plan.pair_rows + group * size, size) for k in range(2)]
        out[...] = jnp.concatenate(parts + [extra], axis=0).astype(out.dtype)


def run_merge(plan, blocks, groups, keep, received):
    rows = blocks // groups * 2 * plan.pair_rows + EXTRA
    shapes = [jax.ShapeDtypeStruct((rows, C), f32 if group == 0 else bf16) for group in range(groups)]
    return pl.pallas_call(
        functools.partial(merge_body, plan, blocks, groups),
        out_shape=shapes,
        in_specs=vmem_specs(1 + len(received)),
        out_specs=vmem_specs(groups),
        compiler_params=limit(16),
        name="merge",
    )(keep, *received)


def mlp_grads(table, m1_ref, m2_ref, hidden, dss, out_ref):
    prob = normal_cdf(hidden)

    def put(first, values):
        parts = values.shape[1] // C
        for part in range(parts):
            out_ref[pl.ds(first + part, values.shape[0], parts), :] = values[:, part * C : (part + 1) * C]

    def outer(left, right):
        lefts = [a for k, a in enumerate(left) for b in right[: 3 - k]]
        rights = [b for k, a in enumerate(left) for b in right[: 3 - k]]
        return mm(jnp.concatenate(lefts, axis=0), jnp.concatenate(rights, axis=0), TN)

    dp = exact(dss, m2_ref[...], NT) * gelu_slope(hidden, prob)
    put(0, exact(dp, m1_ref[...], NT))
    put(TABLE_ROWS, outer([table], three(dp)))
    put(TABLE_ROWS + M1_ROWS, outer(three(hidden * prob), three(dss)))
    ge1 = jnp.sum(dp, axis=0, keepdims=True)
    ge2 = jnp.sum(dss, axis=0, keepdims=True)
    return [ge1[:, i * C : (i + 1) * C] for i in range(4)] + [ge2[:, i * C : (i + 1) * C] for i in range(2)]


def mlp_body(table_ref, m1_ref, m2_ref, hidden_ref, dss_ref, out_ref, tail_ref):
    tail = mlp_grads(table_ref[...], m1_ref, m2_ref, hidden_ref[...], dss_ref[...], out_ref)
    for i, row in enumerate(tail):
        tail_ref[i : i + 1, :] = row


def run_mlp(table, m1, m2, hidden, dss):
    return pl.pallas_call(
        mlp_body,
        out_shape=[jax.ShapeDtypeStruct((MLP_ROWS, C), f32), jax.ShapeDtypeStruct((6, C), f32)],
        in_specs=vmem_specs(5),
        out_specs=vmem_specs(2),
        compiler_params=limit(32),
        name="mlp_grad",
    )(table, m1, m2, hidden, dss)


def adam(weight, first, second, average, gradient, rate, decay):
    first = beta_one * first + (1.0 - beta_one) * gradient
    second = beta_two * second + (1.0 - beta_two) * gradient * gradient
    first_hat = first * (1.0 / (1.0 - beta_one**STEP))
    second_hat = second * (1.0 / (1.0 - beta_two**STEP))
    weight = weight - rate * (first_hat / (jnp.sqrt(second_hat) + adam_eps) + decay * weight)
    return weight, first, second, ema_decay * average + (1.0 - ema_decay) * weight


def update_body(plan, received_count, *refs):
    keep_ref, received = refs[0], refs[1 : 1 + received_count]
    table_ref, m1_ref, m2_ref, hidden_ref, conv_ref, dense_ref, small_ref = refs[1 + received_count : 8 + received_count]
    conv_new, dense_new, small_new, conv_copy, dense_copy, small_copy = refs[8 + received_count : 14 + received_count]
    block, grads, rows, smalls = refs[14 + received_count :]
    me = position_of(plan.sizes)
    total = keep_ref[...]
    for ref in received:
        total = total + ref[...].astype(f32)
    odd = me & 1
    for index, pair in enumerate(PAIRS):
        at = index * plan.pair_rows
        rest = total[at + 2 * plan.full : at + plan.pair_rows]
        for side, k in enumerate(pair):
            full, half = plan.places(odd, k * plan.window)
            block[pl.ds(full, plan.full), :] = total[at + side * plan.full : at + (side + 1) * plan.full]
            block[pl.ds(half, 8), :] = pltpu.roll(rest, 4, 0) if side else rest
    extra = total[2 * plan.pair_rows :]
    smalls[0:8] = extra[0:8]
    dss = jnp.concatenate([extra[8 : 8 + NCLASS], extra[8 + NCLASS : 8 + 2 * NCLASS]], axis=1)
    tail = mlp_grads(table_ref[...], m1_ref, m2_ref, hidden_ref[...], dss, grads)
    for i, row in enumerate(tail):
        smalls[8 + i : 9 + i, :] = row

    for r in range(plan.conv_rows):
        at = slice(r * C, (r + 1) * C)
        gradient = block[pl.ds(4 * odd + r, 4, plan.window), :]
        new = adam(*[conv_ref[k, :, at] for k in range(4)], gradient, rate_conv, decay_weights)
        for k in range(4):
            conv_new[k, :, at] = new[k]
        conv_copy[:, at] = new[0].astype(bf16)

    start = me * plan.dense_rows
    for r in range(plan.dense_rows):
        at = slice(r * C, (r + 1) * C)
        gradient = grads[pl.ds(start + r, 1), :]
        rate = jnp.where(start + r < TABLE_ROWS, rate_table, rate_dense)
        new = adam(*[dense_ref[k : k + 1, at] for k in range(4)], gradient, rate, decay_weights)
        for k in range(4):
            dense_new[k : k + 1, at] = new[k]
        rows[r : r + 1, :] = new[0]
    dense_copy[...] = rows[...].astype(bf16)

    start = me * plan.small_len
    lane = lax.broadcasted_iota(jnp.int32, (8, C), 1)
    near = jnp.broadcast_to(smalls[pl.ds(start // C, 1), :], (8, C))
    far = jnp.broadcast_to(smalls[pl.ds(start // C + 1, 1), :], (8, C))
    off = C - start % C
    gradient = jnp.where(lane < off, pltpu.roll(near, off, 1), pltpu.roll(far, off, 1))
    gradient = gradient[0:1, 0 : plan.small_len]
    new = adam(*[small_ref[k : k + 1, :] for k in range(4)], gradient, rate_small, 0.0)
    for k in range(4):
        small_new[k : k + 1, :] = new[k]
    small_copy[...] = new[0].astype(bf16)


def run_update(plan, keep, received, mlp, states):
    struct = jax.ShapeDtypeStruct
    shapes = [struct(state.shape, f32) for state in states]
    shapes += [struct((4, plan.conv_len), bf16), struct((plan.dense_rows, C), bf16), struct((1, plan.small_len), bf16)]
    return pl.pallas_call(
        functools.partial(update_body, plan, len(received)),
        out_shape=shapes,
        in_specs=vmem_specs(1 + len(received) + 4 + 3),
        out_specs=vmem_specs(6),
        scratch_shapes=[
            pltpu.VMEM((5 * plan.window, C), f32),
            pltpu.VMEM((MLP_ROWS + 8, C), f32),
            pltpu.VMEM((plan.dense_rows, C), f32),
            pltpu.VMEM((24, C), f32),
        ],
        compiler_params=limit(24),
        name="update",
    )(keep, *received, *mlp, *states)


def swap(values, axis, size, turn):
    return lax.ppermute(values, axis, [(i, i ^ turn) for i in range(size)])


def gather_ring(plan, own, prepare):
    (outer, outer_size), (inner, inner_size) = plan.sizes
    half = plan.line // 2
    line = [swap(own, inner, inner_size, 2 * k) for k in reversed(range(1, plan.line))]
    low, own = lax.optimization_barrier((line[: half - 1], run_copy(own)))
    held = []
    for part, turn in (([own] + low, 1), (line[half - 1 :], 2)):
        part = jnp.stack(part)
        held.append(jnp.concatenate([part, swap(part, outer, outer_size, turn)]))
    late = [swap(part, outer, outer_size, 2 - k) for k, part in enumerate(held)]
    late, prepared = lax.optimization_barrier((late, prepare()))
    held = held + late
    return prepared, held + [swap(part, inner, inner_size, 1) for part in held]


def reduce_ring(plan, keeps, sends, beside):
    (outer, outer_size), (inner, inner_size) = plan.sizes
    mates = [swap(part, inner, inner_size, 1) for part in sends]
    received = []
    for turn in range(1, outer_size):
        part = keeps[turn] + mates[turn].astype(f32)
        received.append(swap(part.astype(bf16), outer, outer_size, turn))
    received, beside = lax.optimization_barrier((received, beside))
    keep, *parts = run_merge(plan, plan.line, plan.line, keeps[0], [mates[0], *received])
    return beside, keep, [swap(parts[k], inner, inner_size, 2 * (k + 1)) for k in reversed(range(plan.line - 1))]


def plain_update(plan, position, grads, extra, mlp, states):
    conv_state, mlp_state, small_state = states
    conv_red = lax.psum_scatter(grads.reshape(4, -1), AXES, scatter_dimension=1, tiled=True)
    extra = lax.psum(extra, AXES)
    dss = jnp.concatenate([extra[8 : 8 + NCLASS], extra[8 + NCLASS : 8 + 2 * NCLASS]], axis=1)
    dense_grad, tail = run_mlp(*mlp, dss)
    dense_red = lax.dynamic_slice_in_dim(dense_grad.reshape(-1), position * plan.dense_len, plan.dense_len)
    flat = jnp.concatenate([extra[:8], tail]).reshape(-1)
    small_red = lax.dynamic_slice_in_dim(flat, position * plan.small_len, plan.small_len)
    flat_index = position * plan.dense_len + jnp.arange(plan.dense_len, dtype=jnp.int32)
    dense_rate = jnp.where(flat_index < NCLASS * EMB, rate_table, rate_dense)
    new = [
        jnp.stack(adam(*state, red, rate, decay))
        for state, red, rate, decay in (
            (conv_state, conv_red, rate_conv, decay_weights),
            (mlp_state, dense_red, dense_rate, decay_weights),
            (small_state, small_red, rate_small, 0.0),
        )
    ]
    return new + [state[0].astype(bf16) for state in new]


def per_device(sizes, samples, cotangent, class_ids, *states):
    conv_state, mlp_state, small_state = states
    plan = Plan(sizes, conv_state.shape[2], mlp_state.shape[1], small_state.shape[1])
    x, cot = samples[0], cotangent[0]
    if plan.rings:
        prepared, inputs = gather_ring(plan, run_pack(plan, *states), lambda: run_prepare(class_ids, x, cot))
    else:
        conv, dense, small = [state[0].astype(bf16) for state in states]
        conv = lax.all_gather(conv, AXES, axis=1, tiled=True).reshape(4, KERNEL_ROWS, C)
        small = lax.all_gather(small, AXES, axis=0, tiled=True).reshape(-1, C)
        dense = lax.all_gather(dense, AXES, axis=0, tiled=True).reshape(MLP_ROWS, C)
        inputs = [conv[0], small, conv[1:], dense]
        prepared = run_prepare(class_ids, x, cot)
    rw, kernels, smalls, slope, grad, factors, table, m1, m2, hidden, *sums = run_block(
        plan, x, cot, prepared, inputs
    )
    out = run_down(rw, kernels, smalls)
    dx = run_finish(x, prepared[0], slope, grad, factors)
    mlp = (table, m1, m2, hidden)
    if plan.rings:
        (out, dx), keep, received = reduce_ring(plan, sums[:4], sums[4:], (out, dx))
        results = run_update(plan, keep, received, mlp, states)
    else:
        results = plain_update(plan, lax.axis_index(AXES), *sums, mlp, states)
    conv_new, mlp_new, small_new, conv_copy, mlp_copy, small_copy = results
    return out[None], dx[None], conv_new, mlp_new, small_new, conv_copy, mlp_copy.reshape(-1), small_copy.reshape(-1)


def solution(mesh):
    sizes = tuple((axis, mesh.shape[axis]) for axis in AXES)

    def body(*args):
        return per_device(sizes, *args)

    return jax.shard_map(
        body,
        mesh=mesh,
        in_specs=(
            P(AXES, None, None, None),
            P(AXES, None, None, None),
            P(AXES),
            P(None, None, AXES),
            P(None, AXES),
            P(None, AXES),
        ),
        out_specs=(
            P(AXES, None, None, None),
            P(AXES, None, None, None),
            P(None, None, AXES),
            P(None, AXES),
            P(None, AXES),
            P(None, AXES),
            P(AXES),
            P(AXES),
        ),
        check_vma=False,
    )
```
